32 devices in a mesh: grp: 2 (over x), gx: 8 (over z, y), gy: 2 (over core).
Axes of the slice: x: 2, y: 2, z: 4, core: 2. Of those that a mesh axis runs over, the one named last changes fastest.
Arguments:
- hidden_rows: bfloat16 [384, 8192], P(('grp', 'gy'), 'gx'), parts along dimension 0, may hold values from -40 to 40
- norm_gain: bfloat16 [8192], P('gx'), may hold values from 0.25 to 1.75
- w_query: bfloat16 [8192, 8192], P('gx', 'gy'), may hold values from -0.0625 to 0.0625
- key_weight: bfloat16 [8192, 1024], P('gx', 'gy'), may hold values from -0.0625 to 0.0625
- value_weight: bfloat16 [8192, 1024], P('gx', 'gy'), may hold values from -0.0625 to 0.0625
- query_bias: bfloat16 [8192], P('gy'), may hold values from -3 to 3
- key_bias_vector: bfloat16 [1024], P('gy'), may hold values from -3 to 3
- value_bias_vector: bfloat16 [1024], P('gy'), may hold values from -3 to 3
- rotated_key_cache: bfloat16 [384, 128, 1024], P(('grp', 'gx'), None, 'gy'), parts along dimension 0, may hold values from -2500 to 2500
- stored_value_cache: bfloat16 [384, 128, 1024], P(('grp', 'gx'), None, 'gy'), parts along dimension 0, may hold values from -6 to 6
- slot_valid_lengths: int32 [384], P('grp'), parts along dimension 0, may hold values from 2 to 128, as said below
- slot_of_row: int32 [384], P('grp'), parts along dimension 0, may hold values from 0 to 191, each once
- w_out: bfloat16 [8192, 8192], P('gy', 'gx'), may hold values from -0.0625 to 0.0625
Outputs:
- mixed: bfloat16 [384, 8192], P(('grp', 'gy'), 'gx'), parts along dimension 0
The draws below stay inside these ranges and needn't reach their ends.
There are 2 independent parts, one for each index of `grp`. The reference program is written for one: setup_inputs(seed, part) draws one part's arguments, and reference() takes and returns one part's arrays. A program takes and returns all parts, laid end to end along the dimension named above; an argument that names none is the same for every part. Nothing has to cross between parts.
Inputs may be any that keep to these rules, and one draw needn't show every extreme that they name: `slot_valid_lengths`: every slot holds at least 2 valid positions; some slot holds all 128.
All inputs are finite; a program needn't handle non-finite values.
Results may differ from the reference program's by a relative error of at most 0.006.
Values may be sent and summed in bfloat16 or wider, within the bound.
No kernel may reach another device: no remote copies, remote signals or barrier semaphores. Data moves between devices by JAX's collectives and lax.ppermute only.
A program may use at most 128 MiB of HBM per device.

```python
import math
import jax
import jax.numpy as jnp
from jax import lax

MODEL_WIDTH = 8192
QUERY_HEADS = 64
KEY_VALUE_HEADS = 8
HEAD_SIZE = 128
RPD = 24
CACHE_CAPACITY = 128
GROUP_ROWS = 192


def draw_hidden_rows(key, part):
    key = jax.random.fold_in(key, 11)
    random_key_base, key_row, key_col = jax.random.split(key, 3)
    column = jnp.arange(MODEL_WIDTH).astype(jnp.float32) / MODEL_WIDTH
    rough_scale = jnp.exp(jax.random.uniform(key_col, (MODEL_WIDTH,), minval=math.log(0.6), maxval=math.log(1.6)))
    col_scale = 2.0 ** column * rough_scale
    random_base = jnp.clip(jax.random.normal(random_key_base, (GROUP_ROWS, MODEL_WIDTH)), -6.0, 6.0)
    row_scale = jnp.exp(jax.random.uniform(key_row, (GROUP_ROWS, 1), minval=math.log(0.5), maxval=math.log(2.0)))
    return (random_base * row_scale * col_scale[None, :]).astype(jnp.bfloat16)


def draw_rotated_key_cache(key, part):
    key = jax.random.fold_in(key, 37)
    random_key_base = jax.random.fold_in(key, 0)
    random_base = jnp.clip(jax.random.normal(random_key_base, (GROUP_ROWS, CACHE_CAPACITY, KEY_VALUE_HEADS, HEAD_SIZE)), -6.0, 6.0)
    return random_base.reshape(GROUP_ROWS, CACHE_CAPACITY, KEY_VALUE_HEADS * HEAD_SIZE).astype(jnp.bfloat16)


def draw_slot_valid_lengths(key, part):
    key = jax.random.fold_in(key, 29)
    key_cap, key_len, key_top = jax.random.split(key, 3)
    owners = GROUP_ROWS // RPD
    owner_caps = jax.random.randint(key_cap, (owners,), max(2, CACHE_CAPACITY // 4), CACHE_CAPACITY + 1, dtype=jnp.int32)
    slot_caps = jnp.repeat(owner_caps, RPD)
    lengths = jax.random.randint(key_len, (GROUP_ROWS,), 2, slot_caps + 1, dtype=jnp.int32)
    chosen = jax.random.randint(key_top, (), 0, GROUP_ROWS, dtype=jnp.int32)
    return lengths.at[chosen].set(CACHE_CAPACITY)


def block_levels(key, dims, pieces, least, largest):
    gain, own = 1.0, jax.random.fold_in(key, 6)
    for position, blocks in pieces:
        draws = jnp.exp(jax.random.uniform(jax.random.fold_in(own, position), (blocks,), jnp.float32, least / len(pieces), largest / len(pieces)))
        gain = gain * jnp.repeat(draws, dims[position] // blocks).reshape([-1 if axis == position else 1 for axis in range(len(dims))])
    return gain


def gaussian(key, shape, scale, reach, cuts=(), held_as=jnp.bfloat16):
    gain = block_levels(key, shape, cuts, -0.22, 0.18) if cuts else 1.0
    array = jax.random.normal(key, shape, jnp.float32) * scale * gain
    return jnp.minimum(jnp.maximum(array, -reach), reach).astype(held_as)


def setup_inputs(seed: int = 0, part: int = 0) -> dict:
    key_list = jax.random.split(jax.random.key(seed), 14)
    own_keys = jax.random.split(jax.random.fold_in(key_list[13], part), 14)
    return {
        "hidden_rows": draw_hidden_rows(jax.random.fold_in(jax.random.fold_in(key_list[13], part), 71), part),
        "norm_gain": jnp.clip(1.0 + 0.15 * jax.random.normal(key_list[1], (MODEL_WIDTH,), jnp.float32), 0.25, 1.75).astype(jnp.bfloat16),
        "w_query": gaussian(key_list[2], (MODEL_WIDTH, QUERY_HEADS * HEAD_SIZE), MODEL_WIDTH ** -0.5, 0.0625, ((0, 8), (1, 2))),
        "key_weight": gaussian(key_list[3], (MODEL_WIDTH, KEY_VALUE_HEADS * HEAD_SIZE), MODEL_WIDTH ** -0.5, 0.0625, ((0, 8), (1, 2))),
        "value_weight": gaussian(key_list[4], (MODEL_WIDTH, KEY_VALUE_HEADS * HEAD_SIZE), MODEL_WIDTH ** -0.5, 0.0625, ((0, 8), (1, 2))),
        "query_bias": gaussian(key_list[5], (QUERY_HEADS * HEAD_SIZE,), 0.5, 3.0, ((0, 2),)),
        "key_bias_vector": gaussian(key_list[6], (KEY_VALUE_HEADS * HEAD_SIZE,), 0.5, 3.0, ((0, 2),)),
        "value_bias_vector": gaussian(key_list[7], (KEY_VALUE_HEADS * HEAD_SIZE,), 0.5, 3.0, ((0, 2),)),
        "rotated_key_cache": draw_rotated_key_cache(jax.random.fold_in(jax.random.fold_in(key_list[13], part), 71), part),
        "stored_value_cache": gaussian(own_keys[9], (GROUP_ROWS, CACHE_CAPACITY, KEY_VALUE_HEADS * HEAD_SIZE), 1.0, 6.0, ((0, 8), (2, 2))),
        "slot_valid_lengths": draw_slot_valid_lengths(jax.random.fold_in(jax.random.fold_in(key_list[13], part), 71), part),
        "slot_of_row": jax.random.permutation(own_keys[11], GROUP_ROWS).astype(jnp.int32),
        "w_out": gaussian(key_list[12], (QUERY_HEADS * HEAD_SIZE, MODEL_WIDTH), (QUERY_HEADS * HEAD_SIZE) ** -0.5, 0.0625, ((0, 2), (1, 8))),
    }


EPSILON = 1e-06
ROPE_BASE = 1000000.0

def apply_rotary(values, positions, heads):
    total_row_count = values.shape[0]
    head_width = values.shape[1] // heads
    half_width = head_width // 2
    shaped = values.reshape(total_row_count, heads, head_width)
    frequency = ROPE_BASE ** (-(jnp.arange(half_width).astype(jnp.float32) * 2.0 / head_width))
    angles = positions.astype(jnp.float32)[:, None, None] * frequency[None, None, :]
    cosine = jnp.cos(angles)
    sine_part = jnp.sin(angles)
    first_half = shaped[:, :, :half_width]
    second_half = shaped[:, :, half_width:]
    turned = jnp.concatenate([first_half * cosine - second_half * sine_part, second_half * cosine + first_half * sine_part], axis=2)
    return turned.reshape(total_row_count, heads * head_width)

def attend(query_vectors, current_key, current_value, rotated_key_cache, stored_value_cache, lengths):
    total_row_count = query_vectors.shape[0]
    query_group_count = QUERY_HEADS // KEY_VALUE_HEADS
    grouped_queries = query_vectors.reshape(total_row_count, KEY_VALUE_HEADS, query_group_count, HEAD_SIZE).astype(jnp.float32)
    cached_key_rows = rotated_key_cache.reshape(total_row_count, CACHE_CAPACITY, KEY_VALUE_HEADS, HEAD_SIZE).astype(jnp.float32)
    cached_value_rows = stored_value_cache.reshape(total_row_count, CACHE_CAPACITY, KEY_VALUE_HEADS, HEAD_SIZE).astype(jnp.float32)
    appended_key = current_key.reshape(total_row_count, KEY_VALUE_HEADS, HEAD_SIZE).astype(jnp.float32)
    appended_value = current_value.reshape(total_row_count, KEY_VALUE_HEADS, HEAD_SIZE).astype(jnp.float32)
    score_scale = 1.0 / math.sqrt(HEAD_SIZE)
    cache_scores = jnp.einsum('rgqd,rpgd->rgqp', grouped_queries, cached_key_rows) * score_scale
    own_score = jnp.einsum('rgqd,rgd->rgq', grouped_queries, appended_key) * score_scale
    valid_mask = (jnp.arange(CACHE_CAPACITY)[None, :] < lengths[:, None])[:, None, None, :]
    cache_scores = jnp.where(valid_mask, cache_scores, -1e+30)
    row_max = jnp.maximum(lax.optimization_barrier(jnp.max(cache_scores, axis=3)), own_score)
    cache_exp = jnp.where(valid_mask, jnp.exp(cache_scores - row_max[..., None]), 0.0)
    own_exp = jnp.exp(own_score - row_max)
    denominator = lax.optimization_barrier(jnp.sum(cache_exp, axis=3)) + own_exp
    cache_weight = (cache_exp / denominator[..., None]).astype(jnp.bfloat16).astype(jnp.float32)
    own_weight = (own_exp / denominator).astype(jnp.bfloat16).astype(jnp.float32)
    combined = jnp.einsum('rgqp,rpgd->rgqd', cache_weight, cached_value_rows) + own_weight[..., None] * appended_value[:, :, None, :]
    return combined.reshape(total_row_count, QUERY_HEADS * HEAD_SIZE).astype(jnp.bfloat16)

def reference(hidden_rows, norm_gain, w_query, key_weight, value_weight, query_bias, key_bias_vector, value_bias_vector, rotated_key_cache, stored_value_cache, slot_valid_lengths, slot_of_row, w_out):
    widened = hidden_rows.astype(jnp.float32)
    square_sum = lax.optimization_barrier(jnp.sum(widened * widened, axis=1, keepdims=True))
    normed = (widened * lax.rsqrt(square_sum / MODEL_WIDTH + EPSILON) * norm_gain.astype(jnp.float32)).astype(jnp.bfloat16)
    row_of_slot = jnp.zeros((GROUP_ROWS,), jnp.int32).at[slot_of_row].set(jnp.arange(GROUP_ROWS, dtype=jnp.int32))
    slotted = normed[row_of_slot]
    query_vectors = jnp.dot(slotted, w_query, preferred_element_type=jnp.float32) + query_bias.astype(jnp.float32)
    current_key = jnp.dot(slotted, key_weight, preferred_element_type=jnp.float32) + key_bias_vector.astype(jnp.float32)
    current_value = jnp.dot(slotted, value_weight, preferred_element_type=jnp.float32) + value_bias_vector.astype(jnp.float32)
    query_vectors = apply_rotary(query_vectors, slot_valid_lengths, QUERY_HEADS).astype(jnp.bfloat16)
    current_key = apply_rotary(current_key, slot_valid_lengths, KEY_VALUE_HEADS).astype(jnp.bfloat16)
    current_value = current_value.astype(jnp.bfloat16)
    attended = attend(query_vectors, current_key, current_value, rotated_key_cache, stored_value_cache, slot_valid_lengths)
    projected = jnp.dot(attended, w_out, preferred_element_type=jnp.float32)[slot_of_row]
    return (widened + projected).astype(jnp.bfloat16)
```

```python
import functools
import math

import jax
import jax.numpy as jnp
from jax import lax
from jax.experimental import pallas as pl
from jax.experimental.pallas import tpu as pltpu
from jax.sharding import PartitionSpec as P

MODEL_WIDTH = 8192
QUERY_HEADS = 64
KEY_VALUE_HEADS = 8
HEAD_SIZE = 128
QUERIES_PER_KV = QUERY_HEADS // KEY_VALUE_HEADS
TILES = QUERIES_PER_KV + 2
SQUARE_ROWS = 32

EPSILON = 1e-06
ROPE_BASE = 1000000.0
CHUNKS = 2
SLOTS_PER_STEP = 8
F32 = jnp.float32
BF16 = jnp.bfloat16


def peer(z, q, nz):
    return z ^ q


def peer_pairs(q, nz):
    pairs = []
    for z in range(nz):
        for y in range(2):
            pairs.append((z * 2 + y, peer(z, q, nz) * 2 + y))
    return pairs


def neighbour_pairs(nz):
    return [(z * 2 + y, z * 2 + 1 - y) for z in range(nz) for y in range(2)]


def slot_one_hot(place_ref, slot_of_row, nz, per):
    rows = slot_of_row.shape[1]
    place_z, place_y = place_ref[0], place_ref[1]
    base = lax.broadcasted_iota(jnp.int32, (per, rows), 0)
    blocks = []
    for h in range(2):
        for q in range(nz):
            owner = peer(place_z, q, nz) * 2 + (place_y ^ h)
            blocks.append(jnp.where(base + owner * per == slot_of_row, 1.0, 0.0).astype(F32))
    return jnp.concatenate(blocks, axis=0).astype(BF16)


def project_kernel(
    place_ref, own_ref, other_ref, gain_ref, sor_ref, wq_ref, wk_ref, wv_ref,
    keep_ref, send_ref, slotted_ref, acc, *, nz, per, first, heads,
):
    step = pl.program_id(0)
    half = nz * per

    if first:

        @pl.when(step == 0)
        def _():
            one_hot = slot_one_hot(place_ref, sor_ref[...], nz, per)
            rows = jnp.concatenate([own_ref[...], other_ref[...]], axis=0)
            hidden = jnp.dot(one_hot, rows, preferred_element_type=F32)
            slotted_ref[...] = (hidden * gain_ref[...].astype(F32)).astype(BF16)
            squares = jnp.sum(hidden * hidden, axis=1, keepdims=True)
            high = squares.astype(BF16).astype(F32)
            low = squares - high
            lane = lax.broadcasted_iota(jnp.int32, (per, HEAD_SIZE), 1)
            lane_high = place_ref[1] * 2
            for h, ref in enumerate((keep_ref, send_ref)):
                for q in range(nz):
                    at = h * half + q * per
                    packed = jnp.where(
                        lane == lane_high,
                        high[at : at + per],
                        jnp.where(lane == lane_high + 1, low[at : at + per], 0.0),
                    )
                    packed = jnp.concatenate(
                        [packed, jnp.zeros((SQUARE_ROWS - per, HEAD_SIZE), F32)], axis=0
                    )
                    ref[q, heads * TILES * per :, :] = packed.astype(BF16)

        source = slotted_ref
    else:
        source = own_ref

    columns = QUERIES_PER_KV * HEAD_SIZE
    acc[:, :columns] = jnp.dot(source[...], wq_ref[...], preferred_element_type=F32)
    acc[:, columns : columns + HEAD_SIZE] = jnp.dot(
        source[...], wk_ref[...], preferred_element_type=F32
    )
    acc[:, columns + HEAD_SIZE :] = jnp.dot(source[...], wv_ref[...], preferred_element_type=F32)
    start = pl.multiple_of(step * TILES * per, 16)
    for h, ref in enumerate((keep_ref, send_ref)):
        for q in range(nz):
            at = h * half + q * per
            block = jnp.concatenate(
                [
                    acc[at : at + per, c * HEAD_SIZE : (c + 1) * HEAD_SIZE]
                    for c in range(TILES)
                ],
                axis=0,
            )
            ref[q, pl.ds(start, TILES * per), :] = block.astype(BF16)


def project(place, own, other, gain, sor, wq, wk, wv, *, chunk, heads, nz, per):
    first = chunk == 0
    rows = 2 * nz * per
    depth = wq.shape[0]
    block_rows = heads * TILES * per + (SQUARE_ROWS if first else 0)
    out_block = jax.ShapeDtypeStruct((nz, block_rows, HEAD_SIZE), BF16)
    whole3 = pl.BlockSpec((nz, block_rows, HEAD_SIZE), lambda i, p: (0, 0, 0))
    column = lambda i, p: (0, chunk * heads + i)

    def whole2(array):
        return pl.BlockSpec(array.shape, lambda i, p: (0, 0))

    kernel = functools.partial(
        project_kernel, nz=nz, per=per, first=first, heads=heads
    )
    outs = pl.pallas_call(
        kernel,
        grid_spec=pltpu.PrefetchScalarGridSpec(
            num_scalar_prefetch=1,
            grid=(heads,),
            in_specs=[
                whole2(own),
                whole2(other),
                whole2(gain),
                whole2(sor),
                pl.BlockSpec((depth, QUERIES_PER_KV * HEAD_SIZE), column),
                pl.BlockSpec((depth, HEAD_SIZE), column),
                pl.BlockSpec((depth, HEAD_SIZE), column),
            ],
            out_specs=[whole3, whole3, pl.BlockSpec((rows, depth), lambda i, p: (0, 0))],
            scratch_shapes=[pltpu.VMEM((rows, TILES * HEAD_SIZE), F32)],
        ),
        out_shape=[out_block, out_block, jax.ShapeDtypeStruct((rows, depth), BF16)],
        compiler_params=pltpu.CompilerParams(vmem_limit_bytes=32 * 1024 * 1024),
        cost_estimate=pl.CostEstimate(
            flops=2 * rows * depth * heads * TILES * HEAD_SIZE,
            bytes_accessed=2 * depth * heads * TILES * HEAD_SIZE,
            transcendentals=0,
        ),
        name="project" + str(chunk),
    )(place, own, other, gain, sor, wq, wk, wv)
    return outs


def attend_kernel(
    *refs, parts, first, heads, per, group,
):
    lengths_ref = refs[0]
    part_refs = refs[1 : 1 + parts]
    if first:
        bias_ref, cos_ref, sin_ref, k_ref, v_ref, out_ref, scale_ref, fresh, result = refs[1 + parts :]
    else:
        (
            scale_in_ref, bias_ref, cos_ref, sin_ref, k_ref, v_ref, out_ref, fresh, result,
        ) = refs[1 + parts :]
    step = pl.program_id(0)
    body = heads * TILES * per
    head_rows = TILES * per

    @pl.when(step == 0)
    def _():
        if first:
            squares = part_refs[0][body : body + per, :].astype(F32) if per % 16 == 0 else (
                part_refs[0][body : body + SQUARE_ROWS, :].astype(F32)[:per]
            )
            for ref in part_refs[1:]:
                squares = squares + ref[body : body + SQUARE_ROWS, :].astype(F32)[:per]
            total = jnp.sum(squares, axis=1, keepdims=True)
            scale = jnp.broadcast_to(
                lax.rsqrt(total / MODEL_WIDTH + EPSILON), (per, HEAD_SIZE)
            )
            scale_ref[...] = scale
        else:
            scale = scale_in_ref[...]
        cos, sin = cos_ref[...], sin_ref[...]
        for g in range(heads):
            rows = pl.ds(g * head_rows, head_rows)
            summed = part_refs[0][rows, :].astype(F32)
            for ref in part_refs[1:]:
                summed = summed + ref[rows, :].astype(F32)
            for c in range(TILES):
                tile = summed[c * per : (c + 1) * per] * scale + bias_ref[
                    g * TILES + c : g * TILES + c + 1, :
                ].astype(F32)
                if c < TILES - 1:
                    tile = tile * cos + pltpu.roll(tile, HEAD_SIZE // 2, 1) * sin
                fresh[pl.ds(g * head_rows + c * per, per), :] = tile.astype(BF16).astype(F32)

    score_scale = 1.0 / math.sqrt(HEAD_SIZE)
    positions = k_ref.shape[1]
    qrows = heads * QUERIES_PER_KV
    scores, owns, masks = [], [], []
    position = lax.broadcasted_iota(jnp.int32, (qrows, positions), 1)
    zero = jnp.zeros((QUERIES_PER_KV, HEAD_SIZE), F32)
    for i in range(group):
        s = step * group + i
        query, own = [], []
        for g in range(heads):
            q = fresh[pl.ds(g * head_rows + s, QUERIES_PER_KV, stride=per), :]
            new_key = fresh[pl.ds(g * head_rows + QUERIES_PER_KV * per + s, 1), :]
            own.append(jnp.sum(q * new_key, axis=1, keepdims=True))
            query.append(jnp.concatenate([q if j == g else zero for j in range(heads)], axis=1))
        query = jnp.concatenate(query, axis=0).astype(BF16)
        score = lax.dot_general(
            query, k_ref[i], (((1,), (1,)), ((), ())), preferred_element_type=F32
        )
        valid = position < lengths_ref[s]
        masks.append(valid)
        scores.append(jnp.where(valid, score * score_scale, -1e30))
        owns.append(jnp.concatenate(own, axis=0) * score_scale)
    scores = jnp.concatenate(scores, axis=0)
    owns = jnp.concatenate(owns, axis=0)
    top = jnp.maximum(jnp.max(scores, axis=1, keepdims=True), owns)
    cache_exp = jnp.exp(scores - top)
    own_exp = jnp.exp(owns - top)
    cache_exp = jnp.concatenate(
        [
            jnp.where(masks[i], cache_exp[i * qrows : (i + 1) * qrows], 0.0)
            for i in range(group)
        ],
        axis=0,
    )
    denominator = jnp.sum(cache_exp, axis=1, keepdims=True) + own_exp
    weight = cache_exp / denominator
    own_weight = (own_exp / denominator).astype(BF16).astype(F32)
    for i in range(group):
        s = step * group + i
        mixed = jnp.dot(
            weight[i * qrows : (i + 1) * qrows].astype(BF16), v_ref[i], preferred_element_type=F32
        )
        for g in range(heads):
            lo, hi = g * QUERIES_PER_KV, (g + 1) * QUERIES_PER_KV
            new_value = fresh[pl.ds(g * head_rows + (QUERIES_PER_KV + 1) * per + s, 1), :]
            result[pl.ds(g * QUERIES_PER_KV * per + s, QUERIES_PER_KV, stride=per), :] = (
                mixed[lo:hi, g * HEAD_SIZE : (g + 1) * HEAD_SIZE]
                + own_weight[i * qrows + lo : i * qrows + hi] * new_value
            )

    @pl.when(step == pl.num_programs(0) - 1)
    def _():
        out_ref[...] = result[...].astype(BF16)


def attend(lengths, parts, scale, bias, cos, sin, keys, values, *, chunk, heads):
    first = chunk == 0
    per, positions = keys.shape[0], keys.shape[1]
    group = SLOTS_PER_STEP if per % SLOTS_PER_STEP == 0 else 1

    def whole2(array):
        return pl.BlockSpec(array.shape, lambda i, p: (0, 0))

    cache_spec = pl.BlockSpec(
        (group, positions, heads * HEAD_SIZE), lambda i, p: (i, 0, chunk)
    )
    ins = list(parts) + ([] if first else [scale]) + [bias, cos, sin]
    out_rows = heads * QUERIES_PER_KV * per
    out_shape = [jax.ShapeDtypeStruct((out_rows, HEAD_SIZE), BF16)]
    out_specs = [pl.BlockSpec((out_rows, HEAD_SIZE), lambda i, p: (0, 0))]
    if first:
        out_shape.append(jax.ShapeDtypeStruct((per, HEAD_SIZE), F32))
        out_specs.append(pl.BlockSpec((per, HEAD_SIZE), lambda i, p: (0, 0)))
    return pl.pallas_call(
        functools.partial(
            attend_kernel, parts=len(parts), first=first, heads=heads, per=per, group=group
        ),
        grid_spec=pltpu.PrefetchScalarGridSpec(
            num_scalar_prefetch=1,
            grid=(per // group,),
            in_specs=[whole2(a) for a in ins] + [cache_spec, cache_spec],
            out_specs=out_specs,
            scratch_shapes=[
                pltpu.VMEM((heads * TILES * per, HEAD_SIZE), F32),
                pltpu.VMEM((out_rows, HEAD_SIZE), F32),
            ],
        ),
        out_shape=out_shape,
        compiler_params=pltpu.CompilerParams(vmem_limit_bytes=32 * 1024 * 1024),
        cost_estimate=pl.CostEstimate(
            flops=4 * per * heads * QUERIES_PER_KV * positions * HEAD_SIZE,
            bytes_accessed=4 * per * positions * heads * HEAD_SIZE,
            transcendentals=per * heads * QUERIES_PER_KV * positions,
        ),
        name="attend" + str(chunk),
    )(lengths, *ins, keys, values)


def output_kernel(*refs, blocks, nz, per, first, last, steps):
    place_ref = refs[0]
    block_refs = refs[1 : 1 + blocks]
    rest = refs[1 + blocks :]
    sor_ref, w_ref = rest[0], rest[1]
    rest = rest[2:]
    if not first:
        acc_in_ref, rest = rest[0], rest[1:]
    if last:
        mine_ref, send_ref, permuted, total = rest
    else:
        acc_out_ref, permuted, total = rest
    step = pl.program_id(0)
    tiles = block_refs[0].shape[0] // per

    @pl.when(step == 0)
    def _():
        one_hot = slot_one_hot(place_ref, sor_ref[...], nz, per)
        wide = [ref[...].astype(F32) for ref in block_refs]
        for c in range(tiles):
            stacked = jnp.concatenate(
                [block[c * per : (c + 1) * per] for block in wide], axis=0
            ).astype(BF16)
            permuted[c // (tiles // steps), :, (c % (tiles // steps)) * HEAD_SIZE : (c % (tiles // steps) + 1) * HEAD_SIZE] = lax.dot_general(
                one_hot, stacked, (((0,), (0,)), ((), ())), preferred_element_type=F32
            ).astype(BF16)
        if first:
            total[...] = jnp.zeros_like(total)
        else:
            total[...] = acc_in_ref[...]

    total[...] += jnp.dot(permuted[step], w_ref[...], preferred_element_type=F32)

    @pl.when(step == steps - 1)
    def _():
        if last:
            half = total.shape[0] // 2
            mine_ref[...] = total[:half]
            send_ref[...] = total[half:].astype(BF16)
        else:
            acc_out_ref[...] = total[...]


def output(place, blocks, sor, w_out, acc, *, chunk, heads, chunks, nz, per):
    first, last = chunk == 0, chunk == chunks - 1
    rows = 2 * nz * per
    width = w_out.shape[1]
    depth = heads * QUERIES_PER_KV * HEAD_SIZE
    steps = 4
    step_depth = depth // steps

    def whole2(array):
        return pl.BlockSpec(array.shape, lambda i, p: (0, 0))

    half = jax.ShapeDtypeStruct((rows // 2, width), F32)
    half_sent = jax.ShapeDtypeStruct((rows // 2, width), BF16)
    full = jax.ShapeDtypeStruct((rows, width), F32)
    out_shape = [half, half_sent] if last else [full]
    ins = list(blocks) + [sor]
    in_specs = [whole2(a) for a in ins] + [
        pl.BlockSpec((step_depth, width), lambda i, p: (chunk * steps + i, 0))
    ]
    args = ins + [w_out]
    if not first:
        args.append(acc)
        in_specs.append(whole2(acc))
    return pl.pallas_call(
        functools.partial(
            output_kernel, blocks=len(blocks), nz=nz, per=per, first=first, last=last, steps=steps
        ),
        grid_spec=pltpu.PrefetchScalarGridSpec(
            num_scalar_prefetch=1,
            grid=(steps,),
            in_specs=in_specs,
            out_specs=[whole2(o) for o in out_shape],
            scratch_shapes=[
                pltpu.VMEM((steps, rows, step_depth), BF16),
                pltpu.VMEM((rows, width), F32),
            ],
        ),
        out_shape=out_shape,
        compiler_params=pltpu.CompilerParams(vmem_limit_bytes=40 * 1024 * 1024),
        cost_estimate=pl.CostEstimate(
            flops=2 * rows * depth * width, bytes_accessed=2 * depth * width, transcendentals=0
        ),
        name="output" + str(chunk),
    )(place, *args)


def on_device(
    hidden_rows,
    norm_gain,
    w_query,
    key_weight,
    value_weight,
    query_bias,
    key_bias_vector,
    value_bias_vector,
    rotated_key_cache,
    stored_value_cache,
    slot_valid_lengths,
    slot_of_row,
    w_out,
    *,
    size,
):
    nz = size // 2
    assert size % 2 == 0 and nz & (nz - 1) == 0
    per = rotated_key_cache.shape[0]
    kv_heads = key_weight.shape[1] // HEAD_SIZE
    heads = kv_heads // CHUNKS
    gx = lax.axis_index("gx")
    gy = lax.axis_index("gy")
    place = jnp.stack([gx // 2, gx % 2]).astype(jnp.int32)
    half = hidden_rows.shape[0]

    other = lax.ppermute(hidden_rows, "gy", [(0, 1), (1, 0)])
    sor = jnp.where(gy == 0, slot_of_row, jnp.roll(slot_of_row, half))[None, :]
    gain = norm_gain[None, :]

    lengths = lax.dynamic_slice_in_dim(slot_valid_lengths, gx * per, per, 0)
    half_width = HEAD_SIZE // 2
    frequency = ROPE_BASE ** (-(jnp.arange(half_width).astype(F32) * 2.0 / HEAD_SIZE))
    angles = lengths.astype(F32)[:, None] * frequency[None, :]
    cosine, sine = jnp.cos(angles), jnp.sin(angles)
    cos = jnp.concatenate([cosine, cosine], axis=1)
    sin = jnp.concatenate([-sine, sine], axis=1)
    bias = jnp.concatenate(
        [
            query_bias.reshape(kv_heads, QUERIES_PER_KV, HEAD_SIZE),
            key_bias_vector.reshape(kv_heads, 1, HEAD_SIZE),
            value_bias_vector.reshape(kv_heads, 1, HEAD_SIZE),
        ],
        axis=1,
    ).astype(F32).reshape(CHUNKS, heads * TILES, HEAD_SIZE)

    swapped, kept = [], []
    source, partner = hidden_rows, other
    for c in range(CHUNKS):
        keep, send, slotted = project(
            place, source, partner, gain, sor, w_query, key_weight, value_weight,
            chunk=c, heads=heads, nz=nz, per=per,
        )
        source = partner = slotted if c == 0 else source
        kept.append(keep)
        swapped.append(lax.ppermute(send, "gx", neighbour_pairs(nz)))
    parts = []
    for c in range(CHUNKS):
        blocks = []
        for q in range(nz):
            total = (kept[c][q].astype(F32) + swapped[c][q].astype(F32)).astype(BF16)
            blocks.append(total if q == 0 else lax.ppermute(total, "gx", peer_pairs(q, nz)))
        parts.append(blocks)

    scale = None
    gathered = []
    for c in range(CHUNKS):
        outs = attend(
            lengths, parts[c], scale, bias[c], cos, sin, rotated_key_cache, stored_value_cache,
            chunk=c, heads=heads,
        )
        if c == 0:
            attended, scale = outs
        else:
            (attended,) = outs
        blocks = [attended] + [
            lax.ppermute(attended, "gx", peer_pairs(q, nz)) for q in range(1, nz)
        ]
        blocks += [lax.ppermute(b, "gx", neighbour_pairs(nz)) for b in blocks]
        gathered.append(blocks)

    acc = None
    for c in range(CHUNKS):
        outs = output(
            place, gathered[c], sor, w_out, acc,
            chunk=c, heads=heads, chunks=CHUNKS, nz=nz, per=per,
        )
        if c < CHUNKS - 1:
            (acc,) = outs
    mine, send = outs
    received = lax.ppermute(send, "gy", [(0, 1), (1, 0)])
    return (hidden_rows.astype(F32) + mine + received.astype(F32)).astype(BF16)


def solution(mesh):
    in_specs = (
        P(("grp", "gy"), "gx"),
        P("gx"),
        P("gx", "gy"),
        P("gx", "gy"),
        P("gx", "gy"),
        P("gy"),
        P("gy"),
        P("gy"),
        P(("grp", "gx"), None, "gy"),
        P(("grp", "gx"), None, "gy"),
        P("grp"),
        P("grp"),
        P("gy", "gx"),
    )
    out_specs = P(("grp", "gy"), "gx")
    return jax.shard_map(
        functools.partial(on_device, size=mesh.shape["gx"]),
        mesh=mesh,
        in_specs=in_specs,
        out_specs=out_specs,
        check_vma=False,
    )
```

```python
import functools
import math

import jax
import jax.numpy as jnp
from jax import lax
from jax.experimental import pallas as pl
from jax.experimental.pallas import tpu as pltpu
from jax.sharding import PartitionSpec as P

MODEL_WIDTH = 8192
QUERY_HEADS = 64
KEY_VALUE_HEADS = 8
HEAD_SIZE = 128
QUERIES_PER_KV = QUERY_HEADS // KEY_VALUE_HEADS
TILES = QUERIES_PER_KV + 2
SQUARE_ROWS = 32

EPSILON = 1e-06
ROPE_BASE = 1000000.0
CHUNKS = 2
SLOTS_PER_STEP = 8
VMEM_LIMIT = 56 * 1024 * 1024
F32 = jnp.float32
BF16 = jnp.bfloat16


def peer(z, q, nz):
    return z ^ q


def peer_pairs(q, nz):
    pairs = []
    for z in range(nz):
        for y in range(2):
            pairs.append((z * 2 + y, peer(z, q, nz) * 2 + y))
    return pairs


def neighbour_pairs(nz):
    return [(z * 2 + y, z * 2 + 1 - y) for z in range(nz) for y in range(2)]


def slot_one_hot(place_ref, slot_of_row, nz, per):
    rows = slot_of_row.shape[1]
    place_z, place_y = place_ref[0], place_ref[1]
    base = lax.broadcasted_iota(jnp.int32, (per, rows), 0)
    blocks = []
    for h in range(2):
        for q in range(nz):
            owner = peer(place_z, q, nz) * 2 + (place_y ^ h)
            blocks.append(jnp.where(base + owner * per == slot_of_row, 1.0, 0.0).astype(F32))
    return jnp.concatenate(blocks, axis=0).astype(BF16)


def project_kernel(*refs, nz, per, first, heads):
    place_ref = refs[0]
    if first:
        (
            own_ref, other_ref, gain_ref, sor_ref, wq_ref, wk_ref, wv_ref,
            keep_ref, send_ref, slotted_ref, acc,
        ) = refs[1:]
    else:
        own_ref, wq_ref, wk_ref, wv_ref, keep_ref, send_ref, acc = refs[1:]
    step = pl.program_id(0)
    half = nz * per

    if first:

        @pl.when(step == 0)
        def _():
            one_hot = slot_one_hot(place_ref, sor_ref[...], nz, per)
            own, other = own_ref[...], other_ref[...]
            lower = place_ref[2] == 0
            rows = jnp.concatenate(
                [jnp.where(lower, own, other), jnp.where(lower, other, own)], axis=0
            )
            hidden = jnp.dot(one_hot, rows, preferred_element_type=F32)
            gain = gain_ref[...].astype(F32)
            gain = jnp.concatenate([gain[j : j + 1] for j in range(gain.shape[0])], axis=1)
            slotted_ref[...] = (hidden * gain).astype(BF16)
            squares = jnp.sum(hidden * hidden, axis=1, keepdims=True)
            high = squares.astype(BF16).astype(F32)
            low = squares - high
            lane = lax.broadcasted_iota(jnp.int32, (per, HEAD_SIZE), 1)
            lane_high = place_ref[1] * 2
            for h, ref in enumerate((keep_ref, send_ref)):
                for q in range(nz):
                    at = h * half + q * per
                    packed = jnp.where(
                        lane == lane_high,
                        high[at : at + per],
                        jnp.where(lane == lane_high + 1, low[at : at + per], 0.0),
                    )
                    packed = jnp.concatenate(
                        [packed, jnp.zeros((SQUARE_ROWS - per, HEAD_SIZE), F32)], axis=0
                    )
                    ref[q, heads * TILES * per :, :] = packed.astype(BF16)

        source = slotted_ref
    else:
        source = own_ref

    columns = QUERIES_PER_KV * HEAD_SIZE
    acc[:, :columns] = jnp.dot(source[...], wq_ref[...], preferred_element_type=F32)
    acc[:, columns : columns + HEAD_SIZE] = jnp.dot(
        source[...], wk_ref[...], preferred_element_type=F32
    )
    acc[:, columns + HEAD_SIZE :] = jnp.dot(source[...], wv_ref[...], preferred_element_type=F32)
    start = pl.multiple_of(step * TILES * per, 16)
    for h, ref in enumerate((keep_ref, send_ref)):
        for q in range(nz):
            at = h * half + q * per
            block = jnp.concatenate(
                [
                    acc[at : at + per, c * HEAD_SIZE : (c + 1) * HEAD_SIZE]
                    for c in range(TILES)
                ],
                axis=0,
            )
            ref[q, pl.ds(start, TILES * per), :] = block.astype(BF16)


def project(place, inputs, wq, wk, wv, *, chunk, heads, nz, per):
    first = chunk == 0
    rows = 2 * nz * per
    depth = wq.shape[0]
    block_rows = heads * TILES * per + (SQUARE_ROWS if first else 0)
    out_block = jax.ShapeDtypeStruct((nz, block_rows, HEAD_SIZE), BF16)
    whole3 = pl.BlockSpec((nz, block_rows, HEAD_SIZE), lambda i, p: (0, 0, 0))
    column = lambda i, p: (0, chunk * heads + i)

    def whole2(array):
        return pl.BlockSpec(array.shape, lambda i, p: (0, 0))

    slotted = jax.ShapeDtypeStruct((rows, depth), BF16)
    return pl.pallas_call(
        functools.partial(project_kernel, nz=nz, per=per, first=first, heads=heads),
        grid_spec=pltpu.PrefetchScalarGridSpec(
            num_scalar_prefetch=1,
            grid=(heads,),
            in_specs=[whole2(a) for a in inputs]
            + [
                pl.BlockSpec((depth, QUERIES_PER_KV * HEAD_SIZE), column),
                pl.BlockSpec((depth, HEAD_SIZE), column),
                pl.BlockSpec((depth, HEAD_SIZE), column),
            ],
            out_specs=[whole3, whole3] + ([whole2(slotted)] if first else []),
            scratch_shapes=[pltpu.VMEM((rows, TILES * HEAD_SIZE), F32)],
        ),
        out_shape=[out_block, out_block] + ([slotted] if first else []),
        compiler_params=pltpu.CompilerParams(vmem_limit_bytes=VMEM_LIMIT),
        cost_estimate=pl.CostEstimate(
            flops=20 * rows * depth * heads * TILES * HEAD_SIZE,
            bytes_accessed=20 * depth * heads * TILES * HEAD_SIZE,
            transcendentals=0,
        ),
        name="project" + str(chunk),
    )(place, *inputs, wq, wk, wv)


def attend_kernel(*refs, parts, first, heads, per, group, chunk):
    place_ref, lengths_ref = refs[:2]
    part_refs = refs[2 : 2 + parts]
    rest = refs[2 + parts :]
    if first:
        qb_ref, kb_ref, vb_ref, cos_ref, sin_ref, k_ref, v_ref, out_ref, scale_ref = rest[:9]
    else:
        scale_in_ref, qb_ref, kb_ref, vb_ref, cos_ref, sin_ref, k_ref, v_ref, out_ref = rest[:9]
    fresh, result = rest[9:]
    step = pl.program_id(0)
    body = heads * TILES * per
    head_rows = TILES * per

    @pl.when(step == 0)
    def _():
        if first:
            squares = part_refs[0][body:, :].astype(F32)
            for ref in part_refs[1:]:
                squares = squares + ref[body:, :].astype(F32)
            total = jnp.sum(squares[:per], axis=1, keepdims=True)
            scale = jnp.broadcast_to(
                lax.rsqrt(total / MODEL_WIDTH + EPSILON), (per, HEAD_SIZE)
            )
            scale_ref[...] = scale
        else:
            scale = scale_in_ref[...]
        cos, sin = cos_ref[...], sin_ref[...]
        query_bias = qb_ref[...].astype(F32)
        key_bias = kb_ref[...].astype(F32)
        value_bias = vb_ref[...].astype(F32)
        for g in range(heads):
            rows = pl.ds(g * head_rows, head_rows)
            summed = part_refs[0][rows, :].astype(F32)
            for ref in part_refs[1:]:
                summed = summed + ref[rows, :].astype(F32)
            head = chunk * heads + g
            for c in range(TILES):
                if c < QUERIES_PER_KV:
                    at = head * QUERIES_PER_KV + c
                    bias = query_bias[at : at + 1]
                else:
                    bias = (key_bias if c == QUERIES_PER_KV else value_bias)[head : head + 1]
                tile = summed[c * per : (c + 1) * per] * scale + bias
                if c < TILES - 1:
                    tile = tile * cos + pltpu.roll(tile, HEAD_SIZE // 2, 1) * sin
                fresh[pl.ds(g * head_rows + c * per, per), :] = tile.astype(BF16).astype(F32)

    positions = k_ref.shape[1]
    qrows = heads * QUERIES_PER_KV
    lanes = group * qrows
    extra = 16
    slots = [step * group + i for i in range(group)]
    queries = jnp.concatenate(
        [
            fresh[pl.ds(g * head_rows + s, QUERIES_PER_KV, stride=per), :]
            for s in slots
            for g in range(heads)
        ],
        axis=0,
    )
    turned = queries.T
    lane_block = lax.broadcasted_iota(jnp.int32, (HEAD_SIZE, lanes), 1) // QUERIES_PER_KV
    top_row = lax.broadcasted_iota(jnp.int32, (extra, HEAD_SIZE), 0) == 0
    scores = None
    for i, s in enumerate(slots):
        query, new_key = [], []
        for g in range(heads):
            query.append(jnp.where(lane_block == i * heads + g, turned, 0.0).astype(BF16))
            key = fresh[pl.ds(g * head_rows + QUERIES_PER_KV * per + s, 1), :]
            new_key.append(jnp.where(top_row, key, 0.0).astype(BF16))
        keys = jnp.concatenate([k_ref[i], jnp.concatenate(new_key, axis=1)], axis=0)
        term = jnp.dot(keys, jnp.concatenate(query, axis=0), preferred_element_type=F32)
        scores = term if scores is None else scores + term

    lane_slot = lax.broadcasted_iota(jnp.int32, (1, lanes), 1) // qrows
    lengths = jnp.zeros((1, lanes), jnp.int32)
    base = (place_ref[0] * 2 + place_ref[1]) * per
    for i, s in enumerate(slots):
        lengths = jnp.where(lane_slot == i, lengths_ref[base + s], lengths)
    row = lax.broadcasted_iota(jnp.int32, (positions + extra, lanes), 0)
    valid = (row < lengths) | (row == positions)
    scores = jnp.where(valid, scores * (1.0 / math.sqrt(HEAD_SIZE)), -1e30)
    top = jnp.max(scores, axis=0, keepdims=True)
    exps = jnp.where(valid, jnp.exp(scores - top), 0.0)
    weights = exps * (1.0 / jnp.sum(exps, axis=0, keepdims=True))
    cache_weights = weights[:positions].T.astype(BF16)
    own_weights = weights[positions : positions + 8].T[:, 0:1].astype(BF16).astype(F32)
    for i, s in enumerate(slots):
        mixed = jnp.dot(
            cache_weights[i * qrows : (i + 1) * qrows], v_ref[i], preferred_element_type=F32
        )
        for g in range(heads):
            lo, hi = g * QUERIES_PER_KV, (g + 1) * QUERIES_PER_KV
            new_value = fresh[pl.ds(g * head_rows + (QUERIES_PER_KV + 1) * per + s, 1), :]
            result[pl.ds(g * QUERIES_PER_KV * per + s, QUERIES_PER_KV, stride=per), :] = (
                mixed[lo:hi, g * HEAD_SIZE : (g + 1) * HEAD_SIZE]
                + own_weights[i * qrows + lo : i * qrows + hi] * new_value
            )

    @pl.when(step == pl.num_programs(0) - 1)
    def _():
        out_ref[...] = result[...].astype(BF16)


def attend(place, lengths, parts, scale, biases, cos, sin, keys, values, *, chunk, heads):
    first = chunk == 0
    per, positions = keys.shape[0], keys.shape[1]
    group = SLOTS_PER_STEP

    def whole2(array):
        return pl.BlockSpec(array.shape, lambda i, p, n: (0, 0))

    cache_spec = pl.BlockSpec(
        (group, positions, heads * HEAD_SIZE), lambda i, p, n: (i, 0, chunk)
    )
    ins = list(parts) + ([] if first else [scale]) + list(biases) + [cos, sin]
    out_rows = heads * QUERIES_PER_KV * per
    out_shape = [jax.ShapeDtypeStruct((out_rows, HEAD_SIZE), BF16)]
    if first:
        out_shape.append(jax.ShapeDtypeStruct((per, HEAD_SIZE), F32))
    return pl.pallas_call(
        functools.partial(
            attend_kernel,
            parts=len(parts),
            first=first,
            heads=heads,
            per=per,
            group=group,
            chunk=chunk,
        ),
        grid_spec=pltpu.PrefetchScalarGridSpec(
            num_scalar_prefetch=2,
            grid=(per // group,),
            in_specs=[whole2(a) for a in ins] + [cache_spec, cache_spec],
            out_specs=[whole2(o) for o in out_shape],
            scratch_shapes=[
                pltpu.VMEM((heads * TILES * per, HEAD_SIZE), F32),
                pltpu.VMEM((out_rows, HEAD_SIZE), F32),
            ],
        ),
        out_shape=out_shape,
        compiler_params=pltpu.CompilerParams(vmem_limit_bytes=VMEM_LIMIT),
        cost_estimate=pl.CostEstimate(
            flops=4 * per * heads * QUERIES_PER_KV * positions * HEAD_SIZE,
            bytes_accessed=4 * per * positions * heads * HEAD_SIZE,
            transcendentals=per * heads * QUERIES_PER_KV * positions,
        ),
        name="attend" + str(chunk),
    )(place, lengths, *ins, keys, values)


def output_kernel(*refs, blocks, nz, per, first, last):
    place_ref = refs[0]
    block_refs = refs[1 : 1 + blocks]
    rest = refs[1 + blocks :]
    sor_ref, w_ref = rest[:2]
    rest = rest[2:]
    if not first:
        acc_in_ref, rest = rest[0], rest[1:]
    if last:
        mine_ref, send_ref, stacked, permuted, total = rest
    else:
        acc_out_ref, stacked, permuted = rest
    tiles = block_refs[0].shape[0] // per

    @pl.when(pl.program_id(0) == 0)
    def _():
        one_hot = slot_one_hot(place_ref, sor_ref[...], nz, per)
        wide = [ref[...].astype(F32) for ref in block_refs]
        for c in range(tiles):
            stacked[:, c * HEAD_SIZE : (c + 1) * HEAD_SIZE] = jnp.concatenate(
                [block[c * per : (c + 1) * per] for block in wide], axis=0
            ).astype(BF16)
        permuted[...] = lax.dot_general(
            one_hot, stacked[...], (((0,), (0,)), ((), ())), preferred_element_type=F32
        ).astype(BF16)

    product = jnp.dot(permuted[...], w_ref[...], preferred_element_type=F32)
    if not first:
        product = product + acc_in_ref[...]
    if last:
        half = product.shape[0] // 2
        total[...] = product
        mine_ref[...] = total[pl.ds(pl.multiple_of(place_ref[2] * half, half), half), :]
        send_ref[...] = total[
            pl.ds(pl.multiple_of((1 - place_ref[2]) * half, half), half), :
        ].astype(BF16)
    else:
        acc_out_ref[...] = product


def output(place, blocks, sor, w_out, acc, *, chunk, heads, chunks, nz, per):
    first, last = chunk == 0, chunk == chunks - 1
    rows = 2 * nz * per
    width = w_out.shape[1]
    depth = heads * QUERIES_PER_KV * HEAD_SIZE
    columns = min(width, 256)

    def whole2(array):
        return pl.BlockSpec(array.shape, lambda i, p: (0, 0))

    def striped(count):
        return pl.BlockSpec((count, columns), lambda i, p: (0, i))

    if last:
        out_shape = [
            jax.ShapeDtypeStruct((rows // 2, width), F32),
            jax.ShapeDtypeStruct((rows // 2, width), BF16),
        ]
    else:
        out_shape = [jax.ShapeDtypeStruct((rows, width), F32)]
    ins = list(blocks) + [sor]
    in_specs = [whole2(a) for a in ins] + [
        pl.BlockSpec((depth, columns), lambda i, p: (chunk, i))
    ]
    args = ins + [w_out]
    if not first:
        args.append(acc)
        in_specs.append(striped(rows))
    return pl.pallas_call(
        functools.partial(
            output_kernel, blocks=len(blocks), nz=nz, per=per, first=first, last=last
        ),
        grid_spec=pltpu.PrefetchScalarGridSpec(
            num_scalar_prefetch=1,
            grid=(width // columns,),
            in_specs=in_specs,
            out_specs=[striped(o.shape[0]) for o in out_shape],
            scratch_shapes=[pltpu.VMEM((rows, depth), BF16), pltpu.VMEM((rows, depth), BF16)]
            + ([pltpu.VMEM((rows, columns), F32)] if last else []),
        ),
        out_shape=out_shape,
        compiler_params=pltpu.CompilerParams(vmem_limit_bytes=VMEM_LIMIT),
        cost_estimate=pl.CostEstimate(
            flops=2 * rows * depth * width, bytes_accessed=2 * depth * width, transcendentals=0
        ),
        name="output" + str(chunk),
    )(place, *args)


def on_device(
    hidden_rows,
    norm_gain,
    w_query,
    key_weight,
    value_weight,
    query_bias,
    key_bias_vector,
    value_bias_vector,
    rotated_key_cache,
    stored_value_cache,
    slot_valid_lengths,
    slot_of_row,
    w_out,
    *,
    size,
):
    nz = size // 2
    assert size % 2 == 0 and nz & (nz - 1) == 0
    per = rotated_key_cache.shape[0]
    kv_heads = key_weight.shape[1] // HEAD_SIZE
    heads = kv_heads // CHUNKS
    gx = lax.axis_index("gx")
    gy = lax.axis_index("gy")
    place = jnp.stack([gx // 2, gx % 2, gy]).astype(jnp.int32)

    other = lax.ppermute(hidden_rows, "gy", [(0, 1), (1, 0)])
    sor = slot_of_row[None, :]
    gain = norm_gain.reshape(-1, HEAD_SIZE)

    lengths = lax.dynamic_slice_in_dim(slot_valid_lengths, gx * per, per, 0)
    lane = jnp.arange(HEAD_SIZE)
    half_width = HEAD_SIZE // 2
    frequency = ROPE_BASE ** (-((lane % half_width).astype(F32) * 2.0 / HEAD_SIZE))
    angles = lengths.astype(F32)[:, None] * frequency[None, :]
    cos = jnp.cos(angles)
    sin = jnp.sin(angles) * jnp.where(lane < half_width, -1.0, 1.0)[None, :]
    biases = [b.reshape(-1, HEAD_SIZE) for b in (query_bias, key_bias_vector, value_bias_vector)]

    swapped, kept = [], []
    inputs = [hidden_rows, other, gain, sor]
    for c in range(CHUNKS):
        outs = project(
            place, inputs, w_query, key_weight, value_weight,
            chunk=c, heads=heads, nz=nz, per=per,
        )
        keep, send = outs[:2]
        if c == 0:
            inputs = [outs[2]]
        kept.append(keep)
        swapped.append(lax.ppermute(send, "gx", neighbour_pairs(nz)))
    parts = []
    for c in range(CHUNKS):
        blocks = []
        for q in range(nz):
            total = (kept[c][q].astype(F32) + swapped[c][q].astype(F32)).astype(BF16)
            blocks.append(total if q == 0 else lax.ppermute(total, "gx", peer_pairs(q, nz)))
        parts.append(blocks)

    scale = None
    gathered = []
    for c in range(CHUNKS):
        outs = attend(
            place, slot_valid_lengths, parts[c], scale, biases, cos, sin,
            rotated_key_cache, stored_value_cache, chunk=c, heads=heads,
        )
        if c == 0:
            attended, scale = outs
        else:
            (attended,) = outs
        blocks = [attended] + [
            lax.ppermute(attended, "gx", peer_pairs(q, nz)) for q in range(1, nz)
        ]
        blocks += [lax.ppermute(b, "gx", neighbour_pairs(nz)) for b in blocks]
        gathered.append(blocks)

    acc = None
    for c in range(CHUNKS):
        outs = output(
            place, gathered[c], sor, w_out, acc,
            chunk=c, heads=heads, chunks=CHUNKS, nz=nz, per=per,
        )
        if c < CHUNKS - 1:
            (acc,) = outs
    mine, send = outs
    received = lax.ppermute(send, "gy", [(0, 1), (1, 0)])
    return (hidden_rows.astype(F32) + mine + received.astype(F32)).astype(BF16)


def solution(mesh):
    in_specs = (
        P(("grp", "gy"), "gx"),
        P("gx"),
        P("gx", "gy"),
        P("gx", "gy"),
        P("gx", "gy"),
        P("gy"),
        P("gy"),
        P("gy"),
        P(("grp", "gx"), None, "gy"),
        P(("grp", "gx"), None, "gy"),
        P("grp"),
        P("grp"),
        P("gy", "gx"),
    )
    out_specs = P(("grp", "gy"), "gx")
    return jax.shard_map(
        functools.partial(on_device, size=mesh.shape["gx"]),
        mesh=mesh,
        in_specs=in_specs,
        out_specs=out_specs,
        check_vma=False,
    )
```

```python
import functools
import math

import jax
import jax.numpy as jnp
from jax import lax
from jax.experimental import pallas as pl
from jax.experimental.pallas import tpu as pltpu
from jax.sharding import PartitionSpec as P

MODEL_WIDTH = 8192
QUERY_HEADS = 64
KEY_VALUE_HEADS = 8
HEAD_SIZE = 128
QUERIES_PER_KV = QUERY_HEADS // KEY_VALUE_HEADS
TILES = QUERIES_PER_KV + 2
SQUARE_ROWS = 32

EPSILON = 1e-06
ROPE_BASE = 1000000.0
CHUNKS = 2
SLOTS_PER_STEP = 8
VMEM_LIMIT = 32 * 1024 * 1024
F32 = jnp.float32
BF16 = jnp.bfloat16


def neighbour_pairs(nz):
    return [(z * 2 + y, z * 2 + 1 - y) for z in range(nz) for y in range(2)]


def column_groups(nz):
    return [[z * 2 + y for z in range(nz)] for y in range(2)]


def slot_one_hot(place_ref, slot_of_row, nz, per):
    rows = slot_of_row.shape[1]
    base = lax.broadcasted_iota(jnp.int32, (per, rows), 0)
    blocks = []
    for h in range(2):
        for z in range(nz):
            owner = z * 2 + (place_ref[1] ^ h)
            blocks.append(jnp.where(base + owner * per == slot_of_row, 1.0, 0.0).astype(F32))
    return jnp.concatenate(blocks, axis=0).astype(BF16)


def load_kernel(*refs, windows):
    count = len(windows)
    sources, targets, sems = refs[:count], refs[-1 - count : -1], refs[-1]
    copies = [
        pltpu.make_async_copy(source.at[window], target, sems.at[i])
        for i, (source, target, window) in enumerate(zip(sources, targets, windows))
    ]
    for copy in copies:
        copy.start()
    for copy in copies:
        copy.wait()


def load(name, arrays, windows, after=()):
    shapes = [
        tuple(w.size if isinstance(w, pl.Slice) else n for w, n in zip(window, a.shape))
        for a, window in zip(arrays, windows)
    ]
    size = sum(2 * math.prod(shape) for shape in shapes)
    return pl.pallas_call(
        functools.partial(load_kernel, windows=windows),
        in_specs=[pl.BlockSpec(memory_space=pltpu.HBM)] * len(arrays)
        + [pl.BlockSpec(memory_space=pl.ANY)] * len(after),
        out_specs=[pl.BlockSpec(memory_space=pltpu.VMEM)] * len(arrays),
        out_shape=[pltpu.VMEM(shape, a.dtype) for a, shape in zip(arrays, shapes)],
        scratch_shapes=[pltpu.SemaphoreType.DMA((len(arrays),))],
        compiler_params=pltpu.CompilerParams(vmem_limit_bytes=VMEM_LIMIT),
        cost_estimate=pl.CostEstimate(flops=0, bytes_accessed=size, transcendentals=0),
        name=name,
    )(*[pltpu.with_memory_space_constraint(a, pltpu.HBM) for a in arrays], *after)


def on_chip(count):
    return [pl.BlockSpec(memory_space=pltpu.VMEM)] * count


SCALARS = pl.BlockSpec(memory_space=pltpu.SMEM)


def project_kernel(*refs, nz, per, first, heads):
    place_ref = refs[0]
    half = nz * per
    if first:
        own_ref, other_ref, gain_ref, sor_ref, wq_ref, wk_ref, wv_ref = refs[1:8]
        keep_ref, send_ref, slotted_ref, acc = refs[8:]
        one_hot = slot_one_hot(place_ref, sor_ref[...], nz, per)
        own, other = own_ref[...], other_ref[...]
        lower = place_ref[2] == 0
        rows = jnp.concatenate(
            [jnp.where(lower, own, other), jnp.where(lower, other, own)], axis=0
        )
        hidden = jnp.dot(one_hot, rows, preferred_element_type=F32)
        gain = gain_ref[...].astype(F32)
        gain = jnp.concatenate([gain[j : j + 1] for j in range(gain.shape[0])], axis=1)
        slotted_ref[...] = (hidden * gain).astype(BF16)
        squares = jnp.sum(hidden * hidden, axis=1, keepdims=True)
        high = squares.astype(BF16).astype(F32)
        low = squares - high
        lane = lax.broadcasted_iota(jnp.int32, (per, HEAD_SIZE), 1)
        lane_high = place_ref[1] * 2
        for h, ref in enumerate((keep_ref, send_ref)):
            for z in range(nz):
                at = h * half + z * per
                packed = jnp.where(
                    lane == lane_high,
                    high[at : at + per],
                    jnp.where(lane == lane_high + 1, low[at : at + per], 0.0),
                )
                packed = jnp.concatenate(
                    [packed, jnp.zeros((SQUARE_ROWS - per, HEAD_SIZE), F32)], axis=0
                )
                ref[z, heads * TILES * per :, :] = packed.astype(BF16)
    else:
        slotted_ref, wq_ref, wk_ref, wv_ref = refs[1:5]
        keep_ref, send_ref, acc = refs[5:]

    columns = QUERIES_PER_KV * HEAD_SIZE
    slotted = slotted_ref[...]
    for g in range(heads):
        acc[:, :columns] = jnp.dot(
            slotted, wq_ref[:, g * columns : (g + 1) * columns], preferred_element_type=F32
        )
        narrow = slice(g * HEAD_SIZE, (g + 1) * HEAD_SIZE)
        acc[:, columns:] = jnp.dot(
            slotted,
            jnp.concatenate([wk_ref[:, narrow], wv_ref[:, narrow]], axis=1),
            preferred_element_type=F32,
        )
        for h, ref in enumerate((keep_ref, send_ref)):
            for z in range(nz):
                at = h * half + z * per
                block = jnp.concatenate(
                    [
                        acc[at : at + per, c * HEAD_SIZE : (c + 1) * HEAD_SIZE]
                        for c in range(TILES)
                    ],
                    axis=0,
                )
                ref[z, g * TILES * per : (g + 1) * TILES * per, :] = block.astype(BF16)


def project(place, inputs, weights, *, chunk, heads, nz, per):
    first = chunk == 0
    rows = 2 * nz * per
    depth = weights[0].shape[0]
    block_rows = heads * TILES * per + (SQUARE_ROWS if first else 0)
    out_block = jax.ShapeDtypeStruct((nz, block_rows, HEAD_SIZE), BF16)
    slotted = jax.ShapeDtypeStruct((rows, depth), BF16)
    out_shape = [out_block, out_block] + ([slotted] if first else [])
    return pl.pallas_call(
        functools.partial(project_kernel, nz=nz, per=per, first=first, heads=heads),
        in_specs=[SCALARS] + on_chip(len(inputs) + 3),
        out_specs=on_chip(len(out_shape)),
        out_shape=out_shape,
        scratch_shapes=[pltpu.VMEM((rows, TILES * HEAD_SIZE), F32)],
        compiler_params=pltpu.CompilerParams(vmem_limit_bytes=VMEM_LIMIT),
        cost_estimate=pl.CostEstimate(
            flops=20 * rows * depth * heads * TILES * HEAD_SIZE,
            bytes_accessed=20 * depth * heads * TILES * HEAD_SIZE,
            transcendentals=0,
        ),
        name="project" + str(chunk),
    )(place, *inputs, *weights)


def attend_kernel(*refs, first, heads, per, group, chunk):
    place_ref, lengths_ref, part_ref = refs[:3]
    rest = refs[3:]
    if first:
        qb_ref, kb_ref, vb_ref, cos_ref, sin_ref, k_ref, v_ref, out_ref, scale_ref = rest[:9]
    else:
        scale_in_ref, qb_ref, kb_ref, vb_ref, cos_ref, sin_ref, k_ref, v_ref, out_ref = rest[:9]
    fresh, result = rest[9:]
    body = heads * TILES * per
    head_rows = TILES * per
    parts = part_ref.shape[0]

    if first:
        squares = part_ref[0, body:, :].astype(F32)
        for z in range(1, parts):
            squares = squares + part_ref[z, body:, :].astype(F32)
        total = jnp.sum(squares[:per], axis=1, keepdims=True)
        scale = jnp.broadcast_to(lax.rsqrt(total / MODEL_WIDTH + EPSILON), (per, HEAD_SIZE))
        scale_ref[...] = scale
    else:
        scale = scale_in_ref[...]
    cos, sin = cos_ref[...], sin_ref[...]
    query_bias = qb_ref[...].astype(F32)
    key_bias = kb_ref[...].astype(F32)
    value_bias = vb_ref[...].astype(F32)
    for g in range(heads):
        rows = pl.ds(g * head_rows, head_rows)
        summed = part_ref[0, rows, :].astype(F32)
        for z in range(1, parts):
            summed = summed + part_ref[z, rows, :].astype(F32)
        head = chunk * heads + g
        for c in range(TILES):
            if c < QUERIES_PER_KV:
                at = head * QUERIES_PER_KV + c
                bias = query_bias[at : at + 1]
            else:
                bias = (key_bias if c == QUERIES_PER_KV else value_bias)[head : head + 1]
            tile = summed[c * per : (c + 1) * per] * scale + bias
            if c < TILES - 1:
                tile = tile * cos + pltpu.roll(tile, HEAD_SIZE // 2, 1) * sin
            fresh[pl.ds(g * head_rows + c * per, per), :] = tile.astype(BF16).astype(F32)

    positions = k_ref.shape[1]
    qrows = heads * QUERIES_PER_KV
    lanes = group * qrows
    extra = 16
    lane_block = lax.broadcasted_iota(jnp.int32, (HEAD_SIZE, lanes), 1) // QUERIES_PER_KV
    top_row = lax.broadcasted_iota(jnp.int32, (extra, HEAD_SIZE), 0) == 0
    lane_slot = lax.broadcasted_iota(jnp.int32, (1, lanes), 1) // qrows
    row = lax.broadcasted_iota(jnp.int32, (positions + extra, lanes), 0)
    base = (place_ref[0] * 2 + place_ref[1]) * per
    for start in range(0, per, group):
        slots = range(start, start + group)
        queries = jnp.concatenate(
            [
                fresh[pl.ds(g * head_rows + s, QUERIES_PER_KV, stride=per), :]
                for s in slots
                for g in range(heads)
            ],
            axis=0,
        )
        turned = queries.T
        scores = None
        for i, s in enumerate(slots):
            query, new_key = [], []
            for g in range(heads):
                query.append(jnp.where(lane_block == i * heads + g, turned, 0.0).astype(BF16))
                key = fresh[pl.ds(g * head_rows + QUERIES_PER_KV * per + s, 1), :]
                new_key.append(jnp.where(top_row, key, 0.0).astype(BF16))
            keys = jnp.concatenate([k_ref[s], jnp.concatenate(new_key, axis=1)], axis=0)
            term = jnp.dot(keys, jnp.concatenate(query, axis=0), preferred_element_type=F32)
            scores = term if scores is None else scores + term

        lengths = jnp.zeros((1, lanes), jnp.int32)
        for i, s in enumerate(slots):
            lengths = jnp.where(lane_slot == i, lengths_ref[base + s], lengths)
        valid = (row < lengths) | (row == positions)
        scores = jnp.where(valid, scores * (1.0 / math.sqrt(HEAD_SIZE)), -1e30)
        top = jnp.max(scores, axis=0, keepdims=True)
        exps = jnp.where(valid, jnp.exp(scores - top), 0.0)
        weights = exps * (1.0 / jnp.sum(exps, axis=0, keepdims=True))
        cache_weights = weights[:positions].T.astype(BF16)
        own_weights = weights[positions : positions + 8].T[:, 0:1].astype(BF16).astype(F32)
        for i, s in enumerate(slots):
            mixed = jnp.dot(
                cache_weights[i * qrows : (i + 1) * qrows], v_ref[s], preferred_element_type=F32
            )
            for g in range(heads):
                lo, hi = g * QUERIES_PER_KV, (g + 1) * QUERIES_PER_KV
                new_value = fresh[pl.ds(g * head_rows + (QUERIES_PER_KV + 1) * per + s, 1), :]
                result[pl.ds(g * QUERIES_PER_KV * per + s, QUERIES_PER_KV, stride=per), :] = (
                    mixed[lo:hi, g * HEAD_SIZE : (g + 1) * HEAD_SIZE]
                    + own_weights[i * qrows + lo : i * qrows + hi] * new_value
                )
    out_ref[...] = result[...].astype(BF16)


def attend(place, lengths, part, scale, biases, cos, sin, keys, values, *, chunk, heads):
    first = chunk == 0
    per, positions = keys.shape[0], keys.shape[1]
    ins = [part] + ([] if first else [scale]) + list(biases) + [cos, sin, keys, values]
    out_rows = heads * QUERIES_PER_KV * per
    out_shape = [jax.ShapeDtypeStruct((out_rows, HEAD_SIZE), BF16)]
    if first:
        out_shape.append(jax.ShapeDtypeStruct((per, HEAD_SIZE), F32))
    return pl.pallas_call(
        functools.partial(
            attend_kernel, first=first, heads=heads, per=per, group=SLOTS_PER_STEP, chunk=chunk
        ),
        in_specs=[SCALARS, SCALARS] + on_chip(len(ins)),
        out_specs=on_chip(len(out_shape)),
        out_shape=out_shape,
        scratch_shapes=[
            pltpu.VMEM((heads * TILES * per, HEAD_SIZE), F32),
            pltpu.VMEM((out_rows, HEAD_SIZE), F32),
        ],
        compiler_params=pltpu.CompilerParams(vmem_limit_bytes=VMEM_LIMIT),
        cost_estimate=pl.CostEstimate(
            flops=4 * per * heads * QUERIES_PER_KV * positions * HEAD_SIZE,
            bytes_accessed=4 * per * positions * heads * HEAD_SIZE,
            transcendentals=per * heads * QUERIES_PER_KV * positions,
        ),
        name="attend" + str(chunk),
    )(place, lengths, *ins)


def output_kernel(*refs, nz, per, first, last):
    place_ref, here_ref, there_ref, sor_ref, w_ref = refs[:5]
    rest = refs[5:]
    if not first:
        acc_in_ref, rest = rest[0], rest[1:]
    if last:
        mine_ref, send_ref, stacked, total = rest
    else:
        acc_out_ref, stacked = rest
    tiles = here_ref.shape[1] // per

    one_hot = slot_one_hot(place_ref, sor_ref[...], nz, per)
    wide = [ref[z].astype(F32) for ref in (here_ref, there_ref) for z in range(nz)]
    for c in range(tiles):
        stacked[:, c * HEAD_SIZE : (c + 1) * HEAD_SIZE] = jnp.concatenate(
            [block[c * per : (c + 1) * per] for block in wide], axis=0
        ).astype(BF16)
    permuted = lax.dot_general(
        one_hot, stacked[...], (((0,), (0,)), ((), ())), preferred_element_type=F32
    ).astype(BF16)
    stacked[...] = permuted
    product = jnp.dot(stacked[...], w_ref[...], preferred_element_type=F32)
    if not first:
        product = product + acc_in_ref[...]
    if last:
        half = product.shape[0] // 2
        total[...] = product
        mine_ref[...] = total[pl.ds(pl.multiple_of(place_ref[2] * half, half), half), :]
        send_ref[...] = total[
            pl.ds(pl.multiple_of((1 - place_ref[2]) * half, half), half), :
        ].astype(BF16)
    else:
        acc_out_ref[...] = product


def output(place, here, there, sor, w_out, acc, *, chunk, chunks, nz, per):
    first, last = chunk == 0, chunk == chunks - 1
    rows = 2 * nz * per
    depth, width = w_out.shape
    if last:
        out_shape = [
            jax.ShapeDtypeStruct((rows // 2, width), F32),
            jax.ShapeDtypeStruct((rows // 2, width), BF16),
        ]
    else:
        out_shape = [jax.ShapeDtypeStruct((rows, width), F32)]
    ins = [here, there, sor, w_out] + ([] if first else [acc])
    return pl.pallas_call(
        functools.partial(output_kernel, nz=nz, per=per, first=first, last=last),
        in_specs=[SCALARS] + on_chip(len(ins)),
        out_specs=on_chip(len(out_shape)),
        out_shape=out_shape,
        scratch_shapes=[pltpu.VMEM((rows, depth), BF16)]
        + ([pltpu.VMEM((rows, width), F32)] if last else []),
        compiler_params=pltpu.CompilerParams(vmem_limit_bytes=VMEM_LIMIT),
        cost_estimate=pl.CostEstimate(
            flops=2 * rows * depth * width, bytes_accessed=2 * depth * width, transcendentals=0
        ),
        name="output" + str(chunk),
    )(place, *ins)


def on_device(
    hidden_rows,
    norm_gain,
    w_query,
    key_weight,
    value_weight,
    query_bias,
    key_bias_vector,
    value_bias_vector,
    rotated_key_cache,
    stored_value_cache,
    slot_valid_lengths,
    slot_of_row,
    w_out,
    *,
    size,
):
    nz = size // 2
    per = rotated_key_cache.shape[0]
    kv_heads = key_weight.shape[1] // HEAD_SIZE
    heads = kv_heads // CHUNKS
    gx = lax.axis_index("gx")
    gy = lax.axis_index("gy")
    place = jnp.stack([gx // 2, gx % 2, gy]).astype(jnp.int32)

    other = lax.ppermute(hidden_rows, "gy", [(0, 1), (1, 0)])
    sor = slot_of_row[None, :]
    gain = norm_gain.reshape(-1, HEAD_SIZE)

    lengths = lax.dynamic_slice_in_dim(slot_valid_lengths, gx * per, per, 0)
    lane = jnp.arange(HEAD_SIZE)
    half_width = HEAD_SIZE // 2
    frequency = ROPE_BASE ** (-((lane % half_width).astype(F32) * 2.0 / HEAD_SIZE))
    angles = lengths.astype(F32)[:, None] * frequency[None, :]
    cos = jnp.cos(angles)
    sin = jnp.sin(angles) * jnp.where(lane < half_width, -1.0, 1.0)[None, :]
    biases = [b.reshape(-1, HEAD_SIZE) for b in (query_bias, key_bias_vector, value_bias_vector)]

    columns = heads * QUERIES_PER_KV * HEAD_SIZE
    narrow = heads * HEAD_SIZE
    everything = pl.ds(0, w_query.shape[0])
    positions = rotated_key_cache.shape[1]
    all_columns = pl.ds(0, w_out.shape[1])

    inputs = [hidden_rows, other, gain, sor]
    after = []
    kept, swapped = [], []
    for c in range(CHUNKS):
        weights = load(
            "load_weights" + str(c),
            [w_query, key_weight, value_weight],
            [(everything, pl.ds(c * n, n)) for n in (columns, narrow, narrow)],
            after,
        )
        outs = project(place, inputs, weights, chunk=c, heads=heads, nz=nz, per=per)
        if c == 0:
            inputs = [outs[2]]
        after = [outs[0]]
        kept.append(outs[0])
        swapped.append(lax.ppermute(outs[1], "gx", neighbour_pairs(nz)))
    caches, w_outs = [], []
    for c in range(CHUNKS):
        caches.append(
            load(
                "load_caches" + str(c),
                [rotated_key_cache, stored_value_cache],
                [(pl.ds(0, per), pl.ds(0, positions), pl.ds(c * narrow, narrow))] * 2,
                after,
            )
        )
        w_outs.append(
            load("load_out" + str(c), [w_out], [(pl.ds(c * columns, columns), all_columns)], after)
        )
    parts = []
    for c in range(CHUNKS):
        pair_sum = (kept[c].astype(F32) + swapped[c].astype(F32)).astype(BF16)
        parts.append(
            lax.all_to_all(pair_sum, "gx", 0, 0, axis_index_groups=column_groups(nz), tiled=True)
        )

    scale = None
    gathered = []
    for c in range(CHUNKS):
        outs = attend(
            place, slot_valid_lengths, parts[c], scale, biases, cos, sin, *caches[c],
            chunk=c, heads=heads,
        )
        if c == 0:
            scale = outs[1]
        spread = jnp.broadcast_to(outs[0][None], (nz,) + outs[0].shape)
        here = lax.all_to_all(
            spread, "gx", 0, 0, axis_index_groups=column_groups(nz), tiled=True
        )
        gathered.append((here, lax.ppermute(here, "gx", neighbour_pairs(nz))))

    acc = None
    for c in range(CHUNKS):
        outs = output(
            place, *gathered[c], sor, w_outs[c][0], acc, chunk=c, chunks=CHUNKS, nz=nz, per=per
        )
        acc = outs[0]
    mine, send = outs
    received = lax.ppermute(send, "gy", [(0, 1), (1, 0)])
    return (hidden_rows.astype(F32) + mine + received.astype(F32)).astype(BF16)


def solution(mesh):
    in_specs = (
        P(("grp", "gy"), "gx"),
        P("gx"),
        P("gx", "gy"),
        P("gx", "gy"),
        P("gx", "gy"),
        P("gy"),
        P("gy"),
        P("gy"),
        P(("grp", "gx"), None, "gy"),
        P(("grp", "gx"), None, "gy"),
        P("grp"),
        P("grp"),
        P("gy", "gx"),
    )
    out_specs = P(("grp", "gy"), "gx")
    return jax.shard_map(
        functools.partial(on_device, size=mesh.shape["gx"]),
        mesh=mesh,
        in_specs=in_specs,
        out_specs=out_specs,
        check_vma=False,
    )
```

```python
import functools
import math

import jax
import jax.numpy as jnp
from jax import lax
from jax.experimental import pallas as pl
from jax.experimental.pallas import tpu as pltpu
from jax.sharding import PartitionSpec as P

MODEL_WIDTH = 8192
QUERY_HEADS = 64
KEY_VALUE_HEADS = 8
HEAD_SIZE = 128
QUERIES_PER_KV = QUERY_HEADS // KEY_VALUE_HEADS
TILES = QUERIES_PER_KV + 2
SQUARE_ROWS = 32

EPSILON = 1e-06
ROPE_BASE = 1000000.0
CHUNKS = 2
SLOTS_PER_STEP = 8
VMEM_LIMIT = 16 * 1024 * 1024
ORDER = (
    ("project", 0),
    ("project", 1),
    ("load_caches", 0),
    ("far", 0),
    ("load_caches", 1),
    ("near", 0),
    ("load_out", 0),
    ("far", 1),
    ("attend", 0),
    ("near", 1),
    ("load_out", 1),
    ("gather", 0),
    ("attend", 1),
    ("gather", 1),
    ("output", 0),
    ("output", 1),
)
F32 = jnp.float32
BF16 = jnp.bfloat16


def neighbour_pairs(nz):
    return [(z * 2 + y, z * 2 + 1 - y) for z in range(nz) for y in range(2)]


def stride_pairs(nz, stride):
    return [(z * 2 + y, (z ^ stride) * 2 + y) for z in range(nz) for y in range(2)]


def strides(nz):
    return [1 << i for i in range(nz.bit_length() - 1)]


def place_order(nz):
    return sorted(range(nz), key=lambda q: [(q & b) != 0 for b in strides(nz)])


def slot_one_hot(place_ref, slot_of_row, nz, per):
    rows = slot_of_row.shape[1]
    base = lax.broadcasted_iota(jnp.int32, (per, rows), 0)
    blocks = []
    for h in range(2):
        for q in place_order(nz):
            owner = (place_ref[0] ^ q) * 2 + (place_ref[1] ^ h)
            blocks.append(jnp.where(base + owner * per == slot_of_row, 1.0, 0.0).astype(F32))
    return jnp.concatenate(blocks, axis=0).astype(BF16)


TOKEN = (8, HEAD_SIZE)


def call(kernel, name, token, scalars, arrays, out_shapes, scratch):
    def body(*refs):
        first_out = 1 + len(scalars) + len(arrays)
        refs[first_out][...] = jnp.zeros(TOKEN, F32)
        kernel(*refs[1:first_out], *refs[first_out + 1 :])

    vmem = pl.BlockSpec(memory_space=pltpu.VMEM)
    outs = pl.pallas_call(
        body,
        in_specs=[vmem]
        + [pl.BlockSpec(memory_space=pltpu.SMEM)] * len(scalars)
        + [vmem] * len(arrays),
        out_specs=[vmem] * (1 + len(out_shapes)),
        out_shape=[pltpu.VMEM(TOKEN, F32)]
        + [jax.ShapeDtypeStruct(shape, dtype) for shape, dtype in out_shapes],
        scratch_shapes=scratch,
        compiler_params=pltpu.CompilerParams(vmem_limit_bytes=VMEM_LIMIT),
        cost_estimate=pl.CostEstimate(flops=0, bytes_accessed=0, transcendentals=0),
        name=name,
    )(token, *scalars, *arrays)
    return outs[0], outs[1:]


def load_kernel(*refs, windows):
    count = len(windows)
    sources, token_ref, targets, sems = (
        refs[:count], refs[count + 1], refs[count + 2 : -1], refs[-1],
    )
    copies = [
        pltpu.make_async_copy(source.at[window], target, sems.at[i])
        for i, (source, target, window) in enumerate(zip(sources, targets, windows))
    ]
    for copy in copies:
        copy.start()
    token_ref[...] = jnp.zeros(TOKEN, F32)
    for copy in copies:
        copy.wait()


def load(name, token, arrays, windows):
    shapes = [
        tuple(w.size if isinstance(w, pl.Slice) else n for w, n in zip(window, a.shape))
        for a, window in zip(arrays, windows)
    ]
    vmem = pl.BlockSpec(memory_space=pltpu.VMEM)
    outs = pl.pallas_call(
        functools.partial(load_kernel, windows=windows),
        in_specs=[pl.BlockSpec(memory_space=pltpu.HBM)] * len(arrays) + [vmem],
        out_specs=[vmem] * (1 + len(arrays)),
        out_shape=[pltpu.VMEM(TOKEN, F32)]
        + [pltpu.VMEM(shape, a.dtype) for a, shape in zip(arrays, shapes)],
        scratch_shapes=[pltpu.SemaphoreType.DMA((len(arrays),))],
        compiler_params=pltpu.CompilerParams(vmem_limit_bytes=VMEM_LIMIT),
        cost_estimate=pl.CostEstimate(flops=0, bytes_accessed=0, transcendentals=0),
        name=name,
    )(*[pltpu.with_memory_space_constraint(a, pltpu.HBM) for a in arrays], token)
    return outs[0], outs[1:]


def project_kernel(*refs, nz, per, first, heads):
    place_ref = refs[0]
    if first:
        own_ref, other_ref, gain_ref, sor_ref, wq_ref, wk_ref, wv_ref = refs[1:8]
        *out_refs, slotted_ref, acc = refs[8:]
        one_hot = slot_one_hot(place_ref, sor_ref[...], nz, per)
        own, other = own_ref[...], other_ref[...]
        lower = place_ref[2] == 0
        rows = jnp.concatenate(
            [jnp.where(lower, own, other), jnp.where(lower, other, own)], axis=0
        )
        hidden = jnp.dot(one_hot, rows, preferred_element_type=F32)
        gain = gain_ref[...].astype(F32)
        gain = jnp.concatenate([gain[j : j + 1] for j in range(gain.shape[0])], axis=1)
        slotted_ref[...] = (hidden * gain).astype(BF16)
        squares = jnp.sum(hidden * hidden, axis=1, keepdims=True)
        high = squares.astype(BF16).astype(F32)
        low = squares - high
        lane = lax.broadcasted_iota(jnp.int32, (per, HEAD_SIZE), 1)
        lane_high = place_ref[1] * 2
        for b, ref in enumerate(out_refs):
            for z in range(nz // 2):
                at = (b * (nz // 2) + z) * per
                packed = jnp.where(
                    lane == lane_high,
                    high[at : at + per],
                    jnp.where(lane == lane_high + 1, low[at : at + per], 0.0),
                )
                packed = jnp.concatenate(
                    [packed, jnp.zeros((SQUARE_ROWS - per, HEAD_SIZE), F32)], axis=0
                )
                ref[z, heads * TILES * per :, :] = packed.astype(BF16)
    else:
        slotted_ref, wq_ref, wk_ref, wv_ref = refs[1:5]
        *out_refs, acc = refs[5:]

    columns = QUERIES_PER_KV * HEAD_SIZE
    slotted = slotted_ref[...]
    for g in range(heads):
        acc[:, :columns] = jnp.dot(
            slotted, wq_ref[:, g * columns : (g + 1) * columns], preferred_element_type=F32
        )
        narrow = slice(g * HEAD_SIZE, (g + 1) * HEAD_SIZE)
        acc[:, columns:] = jnp.dot(
            slotted,
            jnp.concatenate([wk_ref[:, narrow], wv_ref[:, narrow]], axis=1),
            preferred_element_type=F32,
        )
        for b, ref in enumerate(out_refs):
            for z in range(nz // 2):
                at = (b * (nz // 2) + z) * per
                block = jnp.concatenate(
                    [
                        acc[at : at + per, c * HEAD_SIZE : (c + 1) * HEAD_SIZE]
                        for c in range(TILES)
                    ],
                    axis=0,
                )
                ref[z, g * TILES * per : (g + 1) * TILES * per, :] = block.astype(BF16)


def project(token, place, inputs, weights, *, chunk, heads, nz, per):
    first = chunk == 0
    rows = 2 * nz * per
    depth = weights[0].shape[0]
    block_rows = heads * TILES * per + (SQUARE_ROWS if first else 0)
    out_shapes = [((nz // 2, block_rows, HEAD_SIZE), BF16)] * 4
    return call(
        functools.partial(project_kernel, nz=nz, per=per, first=first, heads=heads),
        "project" + str(chunk),
        token,
        [place],
        [*inputs, *weights],
        out_shapes + ([((rows, depth), BF16)] if first else []),
        [pltpu.VMEM((rows, TILES * HEAD_SIZE), F32)],
    )


def add_kernel(*refs, terms):
    outs = refs[terms:]
    each = outs[0].shape[0]
    for z in range(refs[0].shape[0]):
        total = refs[0][z].astype(F32)
        for ref in refs[1:terms]:
            total = total + ref[z].astype(F32)
        outs[z // each][z % each] = total.astype(BF16)


def add(name, token, arrays, parts):
    count, rows, width = arrays[0].shape
    shape = (count // parts, rows, width)
    return call(
        functools.partial(add_kernel, terms=len(arrays)),
        name,
        token,
        [],
        arrays,
        [(shape, BF16)] * parts,
        [],
    )


def join_kernel(a_ref, b_ref, out_ref):
    count = a_ref.shape[0]
    out_ref[:count] = a_ref[...]
    out_ref[count:] = b_ref[...]


def join(name, token, a, b):
    shape = (a.shape[0] + b.shape[0],) + a.shape[1:]
    token, (joined,) = call(join_kernel, name, token, [], [a, b], [(shape, BF16)], [])
    return token, joined


def attend_kernel(*refs, first, heads, per, group, chunk):
    place_ref, lengths_ref, mine_ref, last_ref = refs[:4]
    rest = refs[4:]
    if first:
        qb_ref, kb_ref, vb_ref, cos_ref, sin_ref, k_ref, v_ref, out_ref, scale_ref = rest[:9]
    else:
        scale_in_ref, qb_ref, kb_ref, vb_ref, cos_ref, sin_ref, k_ref, v_ref, out_ref = rest[:9]
    fresh, result = rest[9:]
    body = heads * TILES * per
    head_rows = TILES * per

    if first:
        squares = mine_ref[0, body:, :].astype(F32) + last_ref[0, body:, :].astype(F32)
        total = jnp.sum(squares[:per], axis=1, keepdims=True)
        scale = jnp.broadcast_to(lax.rsqrt(total / MODEL_WIDTH + EPSILON), (per, HEAD_SIZE))
        scale_ref[...] = scale
    else:
        scale = scale_in_ref[...]
    cos, sin = cos_ref[...], sin_ref[...]
    query_bias = qb_ref[...].astype(F32)
    key_bias = kb_ref[...].astype(F32)
    value_bias = vb_ref[...].astype(F32)
    for g in range(heads):
        rows = pl.ds(g * head_rows, head_rows)
        summed = mine_ref[0, rows, :].astype(F32) + last_ref[0, rows, :].astype(F32)
        head = chunk * heads + g
        for c in range(TILES):
            if c < QUERIES_PER_KV:
                at = head * QUERIES_PER_KV + c
                bias = query_bias[at : at + 1]
            else:
                bias = (key_bias if c == QUERIES_PER_KV else value_bias)[head : head + 1]
            tile = summed[c * per : (c + 1) * per] * scale + bias
            if c < TILES - 1:
                tile = tile * cos + pltpu.roll(tile, HEAD_SIZE // 2, 1) * sin
            fresh[pl.ds(g * head_rows + c * per, per), :] = tile.astype(BF16).astype(F32)

    positions = k_ref.shape[1]
    qrows = heads * QUERIES_PER_KV
    lanes = group * qrows
    extra = 16
    lane_block = lax.broadcasted_iota(jnp.int32, (HEAD_SIZE, lanes), 1) // QUERIES_PER_KV
    top_row = lax.broadcasted_iota(jnp.int32, (extra, HEAD_SIZE), 0) == 0
    lane_slot = lax.broadcasted_iota(jnp.int32, (1, lanes), 1) // qrows
    row = lax.broadcasted_iota(jnp.int32, (positions + extra, lanes), 0)
    base = (place_ref[0] * 2 + place_ref[1]) * per
    for start in range(0, per, group):
        slots = range(start, start + group)
        queries = jnp.concatenate(
            [
                fresh[pl.ds(g * head_rows + s, QUERIES_PER_KV, stride=per), :]
                for s in slots
                for g in range(heads)
            ],
            axis=0,
        )
        turned = queries.T
        scores = None
        for i, s in enumerate(slots):
            query, new_key = [], []
            for g in range(heads):
                query.append(jnp.where(lane_block == i * heads + g, turned, 0.0).astype(BF16))
                key = fresh[pl.ds(g * head_rows + QUERIES_PER_KV * per + s, 1), :]
                new_key.append(jnp.where(top_row, key, 0.0).astype(BF16))
            keys = jnp.concatenate([k_ref[s], jnp.concatenate(new_key, axis=1)], axis=0)
            term = jnp.dot(keys, jnp.concatenate(query, axis=0), preferred_element_type=F32)
            scores = term if scores is None else scores + term

        lengths = jnp.zeros((1, lanes), jnp.int32)
        for i, s in enumerate(slots):
            lengths = jnp.where(lane_slot == i, lengths_ref[base + s], lengths)
        valid = (row < lengths) | (row == positions)
        scores = jnp.where(valid, scores * (1.0 / math.sqrt(HEAD_SIZE)), -1e30)
        top = jnp.max(scores, axis=0, keepdims=True)
        exps = jnp.where(valid, jnp.exp(scores - top), 0.0)
        weights = exps * (1.0 / jnp.sum(exps, axis=0, keepdims=True))
        cache_weights = weights[:positions].T.astype(BF16)
        own_weights = weights[positions : positions + 8].T[:, 0:1].astype(BF16).astype(F32)
        for i, s in enumerate(slots):
            mixed = jnp.dot(
                cache_weights[i * qrows : (i + 1) * qrows], v_ref[s], preferred_element_type=F32
            )
            for g in range(heads):
                lo, hi = g * QUERIES_PER_KV, (g + 1) * QUERIES_PER_KV
                new_value = fresh[pl.ds(g * head_rows + (QUERIES_PER_KV + 1) * per + s, 1), :]
                result[pl.ds(g * QUERIES_PER_KV * per + s, QUERIES_PER_KV, stride=per), :] = (
                    mixed[lo:hi, g * HEAD_SIZE : (g + 1) * HEAD_SIZE]
                    + own_weights[i * qrows + lo : i * qrows + hi] * new_value
                )
    out_ref[0] = result[...].astype(BF16)


def attend(token, place, lengths, parts, scale, biases, cos, sin, keys, values, *, chunk, heads):
    first = chunk == 0
    per = keys.shape[0]
    out_rows = heads * QUERIES_PER_KV * per
    return call(
        functools.partial(
            attend_kernel, first=first, heads=heads, per=per, group=SLOTS_PER_STEP, chunk=chunk
        ),
        "attend" + str(chunk),
        token,
        [place, lengths],
        list(parts) + ([] if first else [scale]) + list(biases) + [cos, sin, keys, values],
        [((1, out_rows, HEAD_SIZE), BF16)] + ([((per, HEAD_SIZE), F32)] if first else []),
        [
            pltpu.VMEM((heads * TILES * per, HEAD_SIZE), F32),
            pltpu.VMEM((out_rows, HEAD_SIZE), F32),
        ],
    )


def output_kernel(*refs, nz, per, first, last):
    place_ref, block_refs, sor_ref, w_ref = refs[0], refs[1:5], refs[5], refs[6]
    rest = refs[7:]
    if not first:
        acc_in_ref, rest = rest[0], rest[1:]
    if last:
        mine_ref, send_ref, stacked, total = rest
    else:
        acc_out_ref, stacked = rest
    tiles = block_refs[0].shape[1] // per

    one_hot = slot_one_hot(place_ref, sor_ref[...], nz, per)
    wide = [ref[z].astype(F32) for ref in block_refs for z in range(nz // 2)]
    for c in range(tiles):
        stacked[:, c * HEAD_SIZE : (c + 1) * HEAD_SIZE] = jnp.concatenate(
            [block[c * per : (c + 1) * per] for block in wide], axis=0
        ).astype(BF16)
    permuted = lax.dot_general(
        one_hot, stacked[...], (((0,), (0,)), ((), ())), preferred_element_type=F32
    ).astype(BF16)
    stacked[...] = permuted
    product = jnp.dot(stacked[...], w_ref[...], preferred_element_type=F32)
    if not first:
        product = product + acc_in_ref[...]
    if last:
        half = product.shape[0] // 2
        total[...] = product
        mine_ref[...] = total[pl.ds(pl.multiple_of(place_ref[2] * half, half), half), :]
        send_ref[...] = total[
            pl.ds(pl.multiple_of((1 - place_ref[2]) * half, half), half), :
        ].astype(BF16)
    else:
        acc_out_ref[...] = product


def output(token, place, blocks, sor, w_out, acc, *, chunk, chunks, nz, per):
    first, last = chunk == 0, chunk == chunks - 1
    rows = 2 * nz * per
    depth, width = w_out.shape
    if last:
        out_shapes = [((rows // 2, width), F32), ((rows // 2, width), BF16)]
    else:
        out_shapes = [((rows, width), F32)]
    return call(
        functools.partial(output_kernel, nz=nz, per=per, first=first, last=last),
        "output" + str(chunk),
        token,
        [place],
        [*blocks, sor, w_out] + ([] if first else [acc]),
        out_shapes,
        [pltpu.VMEM((rows, depth), BF16)] + ([pltpu.VMEM((rows, width), F32)] if last else []),
    )


def on_device(
    hidden_rows,
    norm_gain,
    w_query,
    key_weight,
    value_weight,
    query_bias,
    key_bias_vector,
    value_bias_vector,
    rotated_key_cache,
    stored_value_cache,
    slot_valid_lengths,
    slot_of_row,
    w_out,
    *,
    size,
):
    nz = size // 2
    assert size % 2 == 0 and nz & (nz - 1) == 0 and nz > 2
    per = rotated_key_cache.shape[0]
    kv_heads = key_weight.shape[1] // HEAD_SIZE
    heads = kv_heads // CHUNKS
    gx = lax.axis_index("gx")
    gy = lax.axis_index("gy")
    place = jnp.stack([gx // 2, gx % 2, gy]).astype(jnp.int32)

    other = lax.ppermute(hidden_rows, "gy", [(0, 1), (1, 0)])
    sor = slot_of_row[None, :]
    gain = norm_gain.reshape(-1, HEAD_SIZE)

    lengths = lax.dynamic_slice_in_dim(slot_valid_lengths, gx * per, per, 0)
    lane = jnp.arange(HEAD_SIZE)
    half_width = HEAD_SIZE // 2
    frequency = ROPE_BASE ** (-((lane % half_width).astype(F32) * 2.0 / HEAD_SIZE))
    angles = lengths.astype(F32)[:, None] * frequency[None, :]
    cos = jnp.cos(angles)
    sin = jnp.sin(angles) * jnp.where(lane < half_width, -1.0, 1.0)[None, :]
    biases = [b.reshape(-1, HEAD_SIZE) for b in (query_bias, key_bias_vector, value_bias_vector)]

    columns = heads * QUERIES_PER_KV * HEAD_SIZE
    narrow = heads * HEAD_SIZE
    everything = pl.ds(0, w_query.shape[0])
    positions = rotated_key_cache.shape[1]
    all_columns = pl.ds(0, w_out.shape[1])
    same_z = neighbour_pairs(nz)
    scale = acc = None
    inputs = [hidden_rows, other, gain, sor]
    near, far, near_sent, far_sent = {}, {}, {}, {}
    caches, w_outs, held, partial = {}, {}, {}, {}

    def do_project(token, c):
        nonlocal inputs
        token, weights = load(
            "load_weights" + str(c),
            token,
            [w_query, key_weight, value_weight],
            [(everything, pl.ds(c * n, n)) for n in (columns, narrow, narrow)],
        )
        token, outs = project(
            token, place, inputs, weights, chunk=c, heads=heads, nz=nz, per=per
        )
        near[c], far[c], near_out, far_out = outs[:4]
        if c == 0:
            inputs = [outs[4]]
        far_sent[c] = lax.ppermute(far_out, "gx", same_z)
        near_sent[c] = lax.ppermute(near_out, "gx", same_z)
        return token

    def do_load_caches(token, c):
        token, caches[c] = load(
            "load_caches" + str(c),
            token,
            [rotated_key_cache, stored_value_cache],
            [(pl.ds(0, per), pl.ds(0, positions), pl.ds(c * narrow, narrow))] * 2,
        )
        return token

    def do_load_out(token, c):
        token, (w_outs[c],) = load(
            "load_out" + str(c), token, [w_out], [(pl.ds(c * columns, columns), all_columns)]
        )
        return token

    def do_far(token, c):
        token, (total,) = add("add_far" + str(c), token, [far[c], far_sent[c]], 1)
        far[c] = lax.ppermute(total, "gx", stride_pairs(nz, 1))
        return token

    def do_near(token, c):
        terms = [near[c], near_sent[c], far[c]]
        for stride in strides(nz)[1:]:
            token, (kept, sent) = add("add_near" + str(c) + "_" + str(stride), token, terms, 2)
            terms = [kept, lax.ppermute(sent, "gx", stride_pairs(nz, stride))]
        partial[c] = terms
        return token

    def do_attend(token, c):
        nonlocal scale
        token, outs = attend(
            token, place, slot_valid_lengths, partial[c], scale, biases, cos, sin, *caches[c],
            chunk=c, heads=heads,
        )
        if c == 0:
            scale = outs[1]
        stride = strides(nz)[-1]
        held[c] = outs[0], lax.ppermute(outs[0], "gx", stride_pairs(nz, stride))
        return token

    def do_gather(token, c):
        blocks, received = held[c]
        for stride in reversed(strides(nz)[:-1]):
            token, blocks = join("join" + str(c) + "_" + str(stride), token, blocks, received)
            received = lax.ppermute(blocks, "gx", stride_pairs(nz, stride))
        held[c] = [
            blocks,
            received,
            lax.ppermute(blocks, "gx", same_z),
            lax.ppermute(received, "gx", same_z),
        ]
        return token

    def do_output(token, c):
        nonlocal acc
        token, acc = output(
            token, place, held[c], sor, w_outs[c], acc if c == 0 else acc[0],
            chunk=c, chunks=CHUNKS, nz=nz, per=per,
        )
        return token

    token = jnp.zeros(TOKEN, F32)
    steps = {
        "project": do_project,
        "load_caches": do_load_caches,
        "load_out": do_load_out,
        "far": do_far,
        "near": do_near,
        "attend": do_attend,
        "gather": do_gather,
        "output": do_output,
    }
    for step, c in ORDER:
        token = steps[step](token, c)
    mine, send = acc
    received = lax.ppermute(send, "gy", [(0, 1), (1, 0)])
    return (hidden_rows.astype(F32) + mine + received.astype(F32)).astype(BF16)


def solution(mesh):
    in_specs = (
        P(("grp", "gy"), "gx"),
        P("gx"),
        P("gx", "gy"),
        P("gx", "gy"),
        P("gx", "gy"),
        P("gy"),
        P("gy"),
        P("gy"),
        P(("grp", "gx"), None, "gy"),
        P(("grp", "gx"), None, "gy"),
        P("grp"),
        P("grp"),
        P("gy", "gx"),
    )
    out_specs = P(("grp", "gy"), "gx")
    return jax.shard_map(
        functools.partial(on_device, size=mesh.shape["gx"]),
        mesh=mesh,
        in_specs=in_specs,
        out_specs=out_specs,
        check_vma=False,
    )
```

```python
import functools
import math

import jax
import jax.numpy as jnp
from jax import lax
from jax.experimental import pallas as pl
from jax.experimental.pallas import tpu as pltpu
from jax.sharding import PartitionSpec as P

MODEL_WIDTH = 8192
QUERY_HEADS = 64
KEY_VALUE_HEADS = 8
HEAD_SIZE = 128
QUERIES_PER_KV = QUERY_HEADS // KEY_VALUE_HEADS
TILES = QUERIES_PER_KV + 2
SQUARE_ROWS = 32

EPSILON = 1e-06
ROPE_BASE = 1000000.0
CHUNK_HEADS = (1, 2, 1)
F32 = jnp.float32
BF16 = jnp.bfloat16
MIB = 1024 * 1024
SLOTS_AT_ONCE = {1: 24, 2: 8, 3: 8, 4: 4}
COSTS = {'attend1': 3000, 'load_caches2': 300, 'load_weights1': 100000, 'project1': 30000, 'load_caches0': 10000, 'project2': 30000, 'attend2': 3000, 'join1': 3000, 'add_far1': 100000, 'add_near2_2': 300, 'load_out0': 100000, 'add_near1_2': 30000, 'output2': 3000, 'load_weights2': 10000, 'load_caches1': 3000}
GATHER = ('y halved', 'y halved', 'y halved')
ORDER = (
    ("project", 0),
    ("project", 1),
    ("far", 0),
    ("load_caches", 0),
    ("load_out", 0),
    ("near", 0),
    ("attend", 0),
    ("far", 1),
    ("gather", 0),
    ("project", 2),
    ("near", 1),
    ("load_caches", 1),
    ("far", 2),
    ("attend", 1),
    ("forward", 0),
    ("load_caches", 2),
    ("near", 2),
    ("gather", 1),
    ("attend", 2),
    ("forward", 1),
    ("output", 0),
    ("load_out", 2),
    ("gather", 2),
    ("load_out", 1),
    ("forward", 2),
    ("output", 1),
    ("output", 2),
)
F32 = jnp.float32
BF16 = jnp.bfloat16


def neighbour_pairs(nz):
    return [(z * 2 + y, z * 2 + 1 - y) for z in range(nz) for y in range(2)]


def stride_pairs(nz, stride):
    return [(z * 2 + y, (z ^ stride) * 2 + y) for z in range(nz) for y in range(2)]


def strides(nz):
    return [1 << i for i in range(nz.bit_length() - 1)]


def place_order(nz):
    return sorted(range(nz), key=lambda q: [(q & b) != 0 for b in strides(nz)])


def slot_one_hot(place_ref, slot_of_row, nz, per):
    rows = slot_of_row.shape[1]
    base = lax.broadcasted_iota(jnp.int32, (per, rows), 0)
    blocks = []
    for h in range(2):
        for q in place_order(nz):
            owner = (place_ref[0] ^ q) * 2 + (place_ref[1] ^ h)
            blocks.append(jnp.where(base + owner * per == slot_of_row, 1.0, 0.0).astype(F32))
    return jnp.concatenate(blocks, axis=0).astype(BF16)


TOKEN = (8, HEAD_SIZE)


def estimate(name):
    return pl.CostEstimate(flops=0, bytes_accessed=COSTS.get(name, 0) * 1000, transcendentals=0)


def call(kernel, name, token, scalars, arrays, out_shapes, scratch, vmem_mib):
    def body(*refs):
        first_out = 1 + len(scalars) + len(arrays)
        refs[first_out][...] = jnp.zeros(TOKEN, F32)
        kernel(*refs[1:first_out], *refs[first_out + 1 :])

    vmem = pl.BlockSpec(memory_space=pltpu.VMEM)
    outs = pl.pallas_call(
        body,
        in_specs=[vmem]
        + [pl.BlockSpec(memory_space=pltpu.SMEM)] * len(scalars)
        + [vmem] * len(arrays),
        out_specs=[vmem] * (1 + len(out_shapes)),
        out_shape=[pltpu.VMEM(TOKEN, F32)]
        + [pltpu.VMEM(shape, dtype) for shape, dtype in out_shapes],
        scratch_shapes=scratch,
        compiler_params=pltpu.CompilerParams(vmem_limit_bytes=vmem_mib * MIB),
        cost_estimate=estimate(name),
        name=name,
    )(token, *scalars, *arrays)
    return outs[0], outs[1:]


def load_kernel(*refs, windows):
    count = len(windows)
    sources, token_ref, targets, sems = (
        refs[:count], refs[count + 1], refs[count + 2 : -1], refs[-1],
    )
    copies = [
        pltpu.make_async_copy(source.at[window], target, sems.at[i])
        for i, (source, target, window) in enumerate(zip(sources, targets, windows))
    ]
    for copy in copies:
        copy.start()
    token_ref[...] = jnp.zeros(TOKEN, F32)
    for copy in copies:
        copy.wait()


def load(name, token, arrays, windows):
    shapes = [
        tuple(w.size if isinstance(w, pl.Slice) else n for w, n in zip(window, a.shape))
        for a, window in zip(arrays, windows)
    ]
    vmem = pl.BlockSpec(memory_space=pltpu.VMEM)
    outs = pl.pallas_call(
        functools.partial(load_kernel, windows=windows),
        in_specs=[pl.BlockSpec(memory_space=pltpu.HBM)] * len(arrays) + [vmem],
        out_specs=[vmem] * (1 + len(arrays)),
        out_shape=[pltpu.VMEM(TOKEN, F32)]
        + [pltpu.VMEM(shape, a.dtype) for a, shape in zip(arrays, shapes)],
        scratch_shapes=[pltpu.SemaphoreType.DMA((len(arrays),))],
        compiler_params=pltpu.CompilerParams(vmem_limit_bytes=MIB),
        cost_estimate=estimate(name),
        name=name,
    )(*[pltpu.with_memory_space_constraint(a, pltpu.HBM) for a in arrays], token)
    return outs[0], outs[1:]


def project_kernel(*refs, nz, per, first, heads):
    place_ref = refs[0]
    if first:
        own_ref, other_ref, gain_ref, sor_ref, wq_ref, wk_ref, wv_ref = refs[1:8]
        *out_refs, slotted_ref, acc = refs[8:]
        one_hot = slot_one_hot(place_ref, sor_ref[...], nz, per)
        own, other = own_ref[...], other_ref[...]
        lower = place_ref[2] == 0
        rows = jnp.concatenate(
            [jnp.where(lower, own, other), jnp.where(lower, other, own)], axis=0
        )
        hidden = jnp.dot(one_hot, rows, preferred_element_type=F32)
        gain = gain_ref[...].astype(F32)
        gain = jnp.concatenate([gain[j : j + 1] for j in range(gain.shape[0])], axis=1)
        slotted_ref[...] = (hidden * gain).astype(BF16)
        squares = jnp.sum(hidden * hidden, axis=1, keepdims=True)
        high = squares.astype(BF16).astype(F32)
        low = squares - high
        lane = lax.broadcasted_iota(jnp.int32, (per, HEAD_SIZE), 1)
        lane_high = place_ref[1] * 2
        for b, ref in enumerate(out_refs):
            for z in range(nz):
                at = (b * nz + z) * per
                packed = jnp.where(
                    lane == lane_high,
                    high[at : at + per],
                    jnp.where(lane == lane_high + 1, low[at : at + per], 0.0),
                )
                packed = jnp.concatenate(
                    [packed, jnp.zeros((SQUARE_ROWS - per, HEAD_SIZE), F32)], axis=0
                )
                ref[z, heads * TILES * per :, :] = packed.astype(BF16)
    else:
        slotted_ref, wq_ref, wk_ref, wv_ref = refs[1:5]
        *out_refs, acc = refs[5:]

    columns = QUERIES_PER_KV * HEAD_SIZE
    slotted = slotted_ref[...]
    for g in range(heads):
        acc[:, :columns] = jnp.dot(
            slotted, wq_ref[:, g * columns : (g + 1) * columns], preferred_element_type=F32
        )
        narrow = slice(g * HEAD_SIZE, (g + 1) * HEAD_SIZE)
        acc[:, columns:] = jnp.dot(
            slotted,
            jnp.concatenate([wk_ref[:, narrow], wv_ref[:, narrow]], axis=1),
            preferred_element_type=F32,
        )
        for b, ref in enumerate(out_refs):
            for z in range(nz):
                at = (b * nz + z) * per
                block = jnp.concatenate(
                    [
                        acc[at : at + per, c * HEAD_SIZE : (c + 1) * HEAD_SIZE]
                        for c in range(TILES)
                    ],
                    axis=0,
                )
                ref[z, g * TILES * per : (g + 1) * TILES * per, :] = block.astype(BF16)


def project(token, place, inputs, weights, *, chunk, heads, nz, per):
    first = chunk == 0
    rows = 2 * nz * per
    depth = weights[0].shape[0]
    block_rows = heads * TILES * per + (SQUARE_ROWS if first else 0)
    out_shapes = [((nz, block_rows, HEAD_SIZE), BF16)] * 2
    return call(
        functools.partial(project_kernel, nz=nz, per=per, first=first, heads=heads),
        "project" + str(chunk),
        token,
        [place],
        [*inputs, *weights],
        out_shapes + ([((rows, depth), BF16)] if first else []),
        [pltpu.VMEM((rows, TILES * HEAD_SIZE), F32)],
        12,
    )


def add_kernel(*refs, starts, count):
    terms = len(starts)
    outs = refs[terms:]
    each = outs[0].shape[0]
    for z in range(count):
        total = refs[0][starts[0] + z].astype(F32)
        for ref, start in zip(refs[1:terms], starts[1:]):
            total = total + ref[start + z].astype(F32)
        outs[z // each][z % each] = total.astype(BF16)


def add(name, token, arrays, starts, count, parts):
    shape = (count // parts,) + arrays[0].shape[1:]
    return call(
        functools.partial(add_kernel, starts=starts, count=count),
        name,
        token,
        [],
        arrays,
        [(shape, BF16)] * parts,
        [],
        2,
    )


def join_kernel(a_ref, b_ref, out_ref):
    count = a_ref.shape[0]
    out_ref[:count] = a_ref[...]
    out_ref[count:] = b_ref[...]


def join(name, token, a, b):
    shape = (a.shape[0] + b.shape[0],) + a.shape[1:]
    token, (joined,) = call(join_kernel, name, token, [], [a, b], [(shape, BF16)], [], 2)
    return token, joined


def attend_kernel(*refs, first, heads, per, group, start_head):
    place_ref, lengths_ref, mine_ref, last_ref = refs[:4]
    rest = refs[4:]
    if first:
        qb_ref, kb_ref, vb_ref, cos_ref, sin_ref, k_ref, v_ref, out_ref, scale_ref = rest[:9]
    else:
        scale_in_ref, qb_ref, kb_ref, vb_ref, cos_ref, sin_ref, k_ref, v_ref, out_ref = rest[:9]
    fresh, result = rest[9:]
    body = heads * TILES * per
    head_rows = TILES * per

    if first:
        squares = mine_ref[0, body:, :].astype(F32) + last_ref[0, body:, :].astype(F32)
        total = jnp.sum(squares[:per], axis=1, keepdims=True)
        scale = jnp.broadcast_to(lax.rsqrt(total / MODEL_WIDTH + EPSILON), (per, HEAD_SIZE))
        scale_ref[...] = scale
    else:
        scale = scale_in_ref[...]
    cos, sin = cos_ref[...], sin_ref[...]
    query_bias = qb_ref[...].astype(F32)
    key_bias = kb_ref[...].astype(F32)
    value_bias = vb_ref[...].astype(F32)
    for g in range(heads):
        rows = pl.ds(g * head_rows, head_rows)
        summed = mine_ref[0, rows, :].astype(F32) + last_ref[0, rows, :].astype(F32)
        head = start_head + g
        for c in range(TILES):
            if c < QUERIES_PER_KV:
                at = head * QUERIES_PER_KV + c
                bias = query_bias[at : at + 1]
            else:
                bias = (key_bias if c == QUERIES_PER_KV else value_bias)[head : head + 1]
            tile = summed[c * per : (c + 1) * per] * scale + bias
            if c < TILES - 1:
                tile = tile * cos + pltpu.roll(tile, HEAD_SIZE // 2, 1) * sin
            fresh[pl.ds(g * head_rows + c * per, per), :] = tile.astype(BF16).astype(F32)

    positions = k_ref.shape[1]
    qrows = heads * QUERIES_PER_KV
    lanes = group * qrows
    extra = 16
    lane_block = lax.broadcasted_iota(jnp.int32, (HEAD_SIZE, lanes), 1) // QUERIES_PER_KV
    top_row = lax.broadcasted_iota(jnp.int32, (extra, HEAD_SIZE), 0) == 0
    lane_slot = lax.broadcasted_iota(jnp.int32, (1, lanes), 1) // qrows
    row = lax.broadcasted_iota(jnp.int32, (positions + extra, lanes), 0)
    base = (place_ref[0] * 2 + place_ref[1]) * per
    for start in range(0, per, group):
        slots = range(start, start + group)
        queries = jnp.concatenate(
            [
                fresh[pl.ds(g * head_rows + s, QUERIES_PER_KV, stride=per), :]
                for s in slots
                for g in range(heads)
            ],
            axis=0,
        )
        turned = queries.T
        scores = None
        for i, s in enumerate(slots):
            query, new_key = [], []
            for g in range(heads):
                query.append(jnp.where(lane_block == i * heads + g, turned, 0.0).astype(BF16))
                key = fresh[pl.ds(g * head_rows + QUERIES_PER_KV * per + s, 1), :]
                new_key.append(jnp.where(top_row, key, 0.0).astype(BF16))
            keys = jnp.concatenate([k_ref[s], jnp.concatenate(new_key, axis=1)], axis=0)
            term = jnp.dot(keys, jnp.concatenate(query, axis=0), preferred_element_type=F32)
            scores = term if scores is None else scores + term

        lengths = jnp.zeros((1, lanes), jnp.int32)
        for i, s in enumerate(slots):
            lengths = jnp.where(lane_slot == i, lengths_ref[base + s], lengths)
        valid = (row < lengths) | (row == positions)
        scores = jnp.where(valid, scores * (1.0 / math.sqrt(HEAD_SIZE)), -1e30)
        top = jnp.max(scores, axis=0, keepdims=True)
        exps = jnp.where(valid, jnp.exp(scores - top), 0.0)
        weights = exps * (1.0 / jnp.sum(exps, axis=0, keepdims=True))
        cache_weights = weights[:positions].T
        own_weights = weights[positions : positions + 8].T[:, 0:1].astype(BF16).astype(F32)
        for i, s in enumerate(slots):
            mixed = jnp.dot(
                cache_weights[i * qrows : (i + 1) * qrows].astype(BF16),
                v_ref[s],
                preferred_element_type=F32,
            )
            for g in range(heads):
                lo, hi = g * QUERIES_PER_KV, (g + 1) * QUERIES_PER_KV
                new_value = fresh[pl.ds(g * head_rows + (QUERIES_PER_KV + 1) * per + s, 1), :]
                result[pl.ds(g * QUERIES_PER_KV * per + s, QUERIES_PER_KV, stride=per), :] = (
                    mixed[lo:hi, g * HEAD_SIZE : (g + 1) * HEAD_SIZE]
                    + own_weights[i * qrows + lo : i * qrows + hi] * new_value
                )
    out_ref[0] = result[...].astype(BF16)


def attend(token, place, lengths, parts, scale, biases, cos, sin, keys, values, *, chunk, heads):
    first = chunk == 0
    per = keys.shape[0]
    out_rows = heads * QUERIES_PER_KV * per
    return call(
        functools.partial(
            attend_kernel,
            first=first,
            heads=heads,
            per=per,
            group=SLOTS_AT_ONCE[heads],
            start_head=sum(CHUNK_HEADS[:chunk]),
        ),
        "attend" + str(chunk),
        token,
        [place, lengths],
        list(parts) + ([] if first else [scale]) + list(biases) + [cos, sin, keys, values],
        [((1, out_rows, HEAD_SIZE), BF16)] + ([((per, HEAD_SIZE), F32)] if first else []),
        [
            pltpu.VMEM((heads * TILES * per, HEAD_SIZE), F32),
            pltpu.VMEM((out_rows, HEAD_SIZE), F32),
        ],
        8,
    )


def output_kernel(*refs, labels, nz, per, first, last):
    count = len(labels)
    place_ref, block_refs, sor_ref, w_ref = refs[0], refs[1 : 1 + count], refs[1 + count], refs[2 + count]
    rest = refs[3 + count :]
    if not first:
        acc_in_ref, rest = rest[0], rest[1:]
    if last:
        mine_ref, send_ref, stacked, total = rest
    else:
        acc_out_ref, stacked = rest
    tiles = block_refs[0].shape[1] // per

    one_hot = slot_one_hot(place_ref, sor_ref[...], nz, per)
    wide = {
        label: ref[z].astype(F32)
        for ref, own in zip(block_refs, labels)
        for z, label in enumerate(own)
    }
    wide = [wide[h, q] for h in range(2) for q in place_order(nz)]
    for c in range(tiles):
        stacked[:, c * HEAD_SIZE : (c + 1) * HEAD_SIZE] = jnp.concatenate(
            [block[c * per : (c + 1) * per] for block in wide], axis=0
        ).astype(BF16)
    permuted = lax.dot_general(
        one_hot, stacked[...], (((0,), (0,)), ((), ())), preferred_element_type=F32
    ).astype(BF16)
    stacked[...] = permuted
    product = jnp.dot(stacked[...], w_ref[...], preferred_element_type=F32)
    if not first:
        product = product + acc_in_ref[...]
    if last:
        half = product.shape[0] // 2
        total[...] = product
        mine_ref[...] = total[pl.ds(pl.multiple_of(place_ref[2] * half, half), half), :]
        send_ref[...] = total[
            pl.ds(pl.multiple_of((1 - place_ref[2]) * half, half), half), :
        ].astype(BF16)
    else:
        acc_out_ref[...] = product


def output(token, place, blocks, labels, sor, w_out, acc, *, chunk, chunks, nz, per):
    first, last = chunk == 0, chunk == chunks - 1
    rows = 2 * nz * per
    depth, width = w_out.shape
    if last:
        out_shapes = [((rows // 2, width), F32), ((rows // 2, width), BF16)]
    else:
        out_shapes = [((rows, width), F32)]
    return call(
        functools.partial(
            output_kernel, labels=labels, nz=nz, per=per, first=first, last=last
        ),
        "output" + str(chunk),
        token,
        [place],
        [*blocks, sor, w_out] + ([] if first else [acc]),
        out_shapes,
        [pltpu.VMEM((rows, depth), BF16)] + ([pltpu.VMEM((rows, width), F32)] if last else []),
        12,
    )


def on_device(
    hidden_rows,
    norm_gain,
    w_query,
    key_weight,
    value_weight,
    query_bias,
    key_bias_vector,
    value_bias_vector,
    rotated_key_cache,
    stored_value_cache,
    slot_valid_lengths,
    slot_of_row,
    w_out,
    *,
    size,
):
    nz = size // 2
    assert size % 2 == 0 and nz & (nz - 1) == 0 and nz > 2
    per = rotated_key_cache.shape[0]
    kv_heads = key_weight.shape[1] // HEAD_SIZE
    assert sum(CHUNK_HEADS) == kv_heads and per == SLOTS_AT_ONCE[1]
    chunks = len(CHUNK_HEADS)
    gx = lax.axis_index("gx")
    gy = lax.axis_index("gy")
    place = jnp.stack([gx // 2, gx % 2, gy]).astype(jnp.int32)

    other = lax.ppermute(hidden_rows, "gy", [(0, 1), (1, 0)])
    sor = slot_of_row[None, :]
    gain = norm_gain.reshape(-1, HEAD_SIZE)

    lengths = lax.dynamic_slice_in_dim(slot_valid_lengths, gx * per, per, 0)
    lane = jnp.arange(HEAD_SIZE)
    half_width = HEAD_SIZE // 2
    frequency = ROPE_BASE ** (-((lane % half_width).astype(F32) * 2.0 / HEAD_SIZE))
    angles = lengths.astype(F32)[:, None] * frequency[None, :]
    cos = jnp.cos(angles)
    sin = jnp.sin(angles) * jnp.where(lane < half_width, -1.0, 1.0)[None, :]
    biases = [b.reshape(-1, HEAD_SIZE) for b in (query_bias, key_bias_vector, value_bias_vector)]

    def head_window(c, width):
        return pl.ds(sum(CHUNK_HEADS[:c]) * width, CHUNK_HEADS[c] * width)

    wide = QUERIES_PER_KV * HEAD_SIZE
    everything = pl.ds(0, w_query.shape[0])
    positions = rotated_key_cache.shape[1]
    all_columns = pl.ds(0, w_out.shape[1])
    same_z = neighbour_pairs(nz)
    scale = acc = None
    inputs = [hidden_rows, other, gain, sor]
    kept, swapped, reduced = {}, {}, {}
    caches, w_outs, gathered, waiting = {}, {}, {}, {}

    def over_y(blocks, labels):
        return lax.ppermute(blocks, "gx", same_z), [(1 - h, q) for h, q in labels]

    def over_z(blocks, labels, stride):
        moved = lax.ppermute(blocks, "gx", stride_pairs(nz, stride))
        return moved, [(h, q ^ stride) for h, q in labels]

    def do_project(token, c):
        nonlocal inputs
        token, weights = load(
            "load_weights" + str(c),
            token,
            [w_query, key_weight, value_weight],
            [(everything, head_window(c, n)) for n in (wide, HEAD_SIZE, HEAD_SIZE)],
        )
        token, outs = project(
            token, place, inputs, weights, chunk=c, heads=CHUNK_HEADS[c], nz=nz, per=per
        )
        kept[c] = outs[0]
        if c == 0:
            inputs = [outs[2]]
        swapped[c] = lax.ppermute(outs[1], "gx", same_z)
        return token

    def do_load_caches(token, c):
        token, caches[c] = load(
            "load_caches" + str(c),
            token,
            [rotated_key_cache, stored_value_cache],
            [(pl.ds(0, per), pl.ds(0, positions), head_window(c, HEAD_SIZE))] * 2,
        )
        return token

    def do_load_out(token, c):
        token, (w_outs[c],) = load(
            "load_out" + str(c), token, [w_out], [(head_window(c, wide), all_columns)]
        )
        return token

    def do_far(token, c):
        half = nz // 2
        token, (total,) = add(
            "add_far" + str(c), token, [kept[c], swapped[c]], [half, half], half, 1
        )
        reduced[c] = lax.ppermute(total, "gx", stride_pairs(nz, 1))
        return token

    def do_near(token, c):
        terms, starts, count = [kept[c], swapped[c], reduced[c]], [0, 0, 0], nz // 2
        for stride in strides(nz)[1:]:
            token, (mine, sent) = add(
                "add_near" + str(c) + "_" + str(stride), token, terms, starts, count, 2
            )
            terms = [mine, lax.ppermute(sent, "gx", stride_pairs(nz, stride))]
            starts, count = [0, 0], count // 2
        reduced[c] = terms
        return token

    def do_attend(token, c):
        nonlocal scale
        token, outs = attend(
            token, place, slot_valid_lengths, reduced[c], scale, biases, cos, sin, *caches[c],
            chunk=c, heads=CHUNK_HEADS[c],
        )
        if c == 0:
            scale = outs[1]
        own = outs[0], [(0, 0)]
        first_move = over_y(*own) if GATHER[c] == "y first" else over_z(*own, strides(nz)[-1])
        waiting[c] = own, first_move
        return token

    def do_gather(token, c):
        held, moved = waiting[c]
        for stride in reversed(strides(nz) if GATHER[c] == "y first" else strides(nz)[:-1]):
            if GATHER[c] == "y first" and stride == 1:
                break
            token, joined = join("join" + str(c) + "_" + str(stride), token, held[0], moved[0])
            held = joined, held[1] + moved[1]
            moved = over_z(*held, stride)
        waiting[c] = held, moved
        gathered[c] = [held, moved]
        if GATHER[c] == "y halved":
            gathered[c].append(over_y(*held))
        return token

    def do_forward(token, c):
        held, moved = waiting[c]
        if GATHER[c] == "y halved":
            gathered[c].append(over_y(*moved))
            return token
        token, joined = join("join" + str(c), token, held[0], moved[0])
        held = joined, held[1] + moved[1]
        gathered[c] = [held, over_z(*held, 1) if GATHER[c] == "y first" else over_y(*held)]
        return token

    def do_output(token, c):
        nonlocal acc
        token, acc = output(
            token, place, [a for a, _ in gathered[c]], [own for _, own in gathered[c]], sor,
            w_outs[c], acc if c == 0 else acc[0], chunk=c, chunks=chunks, nz=nz, per=per,
        )
        return token

    token = jnp.zeros(TOKEN, F32)
    steps = {
        "project": do_project,
        "load_caches": do_load_caches,
        "load_out": do_load_out,
        "far": do_far,
        "near": do_near,
        "attend": do_attend,
        "gather": do_gather,
        "forward": do_forward,
        "output": do_output,
    }
    for step, c in ORDER:
        token = steps[step](token, c)
    mine, send = acc
    received = lax.ppermute(send, "gy", [(0, 1), (1, 0)])
    return (hidden_rows.astype(F32) + mine + received.astype(F32)).astype(BF16)


def solution(mesh):
    in_specs = (
        P(("grp", "gy"), "gx"),
        P("gx"),
        P("gx", "gy"),
        P("gx", "gy"),
        P("gx", "gy"),
        P("gy"),
        P("gy"),
        P("gy"),
        P(("grp", "gx"), None, "gy"),
        P(("grp", "gx"), None, "gy"),
        P("grp"),
        P("grp"),
        P("gy", "gx"),
    )
    out_specs = P(("grp", "gy"), "gx")
    return jax.shard_map(
        functools.partial(on_device, size=mesh.shape["gx"]),
        mesh=mesh,
        in_specs=in_specs,
        out_specs=out_specs,
        check_vma=False,
    )
```

```python
import functools
import math

import jax
import jax.numpy as jnp
from jax import lax
from jax.experimental import pallas as pl
from jax.experimental.pallas import tpu as pltpu
from jax.sharding import PartitionSpec as P

MODEL_WIDTH = 8192
QUERY_HEADS = 64
KEY_VALUE_HEADS = 8
HEAD_SIZE = 128
QUERIES_PER_KV = QUERY_HEADS // KEY_VALUE_HEADS
TILES = QUERIES_PER_KV + 2
SQUARE_ROWS = 32

EPSILON = 1e-06
ROPE_BASE = 1000000.0
CHUNK_HEADS = (1, 2, 1)
F32 = jnp.float32
BF16 = jnp.bfloat16
MIB = 1024 * 1024
SLOTS_AT_ONCE = {1: 24, 2: 8, 3: 8, 4: 4}
PEAK_FLOP_PER_US = 1.1535e9
COSTS = {'project0': 1.35, 'load_caches0': 1.12, 'load_out0': 1.32, 'add_far0': 0.15, 'add_near0_2': 0.15, 'attend0': 2.1, 'join0_2': 0.1, 'join0': 0.1, 'output0': 2, 'load_weights1': 2.5, 'project1': 1, 'load_caches1': 1.9, 'load_out1': 2.3, 'add_far1': 0.15, 'add_near1_2': 0.15, 'attend1': 1, 'join1_2': 1, 'output1': 1.9, 'load_weights2': 1.42, 'project2': 1.35, 'load_caches2': 16, 'load_out2': 1.32, 'add_far2': 0.15, 'add_near2_2': 0.15, 'attend2': 2.1, 'join2_2': 8, 'join2': 8, 'output2': 1.28}
GATHER = ('y halved', 'y halved', 'y halved')
ORDER = (
    ("load_caches", 0),
    ("project", 0),
    ("project", 1),
    ("far", 0),
    ("load_out", 0),
    ("load_caches", 1),
    ("project", 2),
    ("near", 0),
    ("far", 1),
    ("attend", 0),
    ("far", 2),
    ("near", 1),
    ("gather", 0),
    ("forward", 0),
    ("load_caches", 2),
    ("attend", 1),
    ("near", 2),
    ("attend", 2),
    ("gather", 1),
    ("load_out", 2),
    ("gather", 2),
    ("forward", 1),
    ("forward", 2),
    ("output", 0),
    ("load_out", 1),
    ("output", 1),
    ("output", 2),
)
F32 = jnp.float32
BF16 = jnp.bfloat16


def neighbour_pairs(nz):
    return [(z * 2 + y, z * 2 + 1 - y) for z in range(nz) for y in range(2)]


def stride_pairs(nz, stride):
    return [(z * 2 + y, (z ^ stride) * 2 + y) for z in range(nz) for y in range(2)]


def strides(nz):
    return [1 << i for i in range(nz.bit_length() - 1)]


def place_order(nz):
    return sorted(range(nz), key=lambda q: [(q & b) != 0 for b in strides(nz)])


def slot_one_hot(place_ref, slot_of_row, nz, per):
    rows = slot_of_row.shape[1]
    base = lax.broadcasted_iota(jnp.int32, (per, rows), 0)
    blocks = []
    for h in range(2):
        for q in place_order(nz):
            owner = (place_ref[0] ^ q) * 2 + (place_ref[1] ^ h)
            blocks.append(jnp.where(base + owner * per == slot_of_row, 1.0, 0.0).astype(F32))
    return jnp.concatenate(blocks, axis=0).astype(BF16)


TOKEN = (8, HEAD_SIZE)


def estimate(name):
    flops = int(COSTS.get(name, 0) * PEAK_FLOP_PER_US)
    return pl.CostEstimate(flops=flops, bytes_accessed=0, transcendentals=0)


def call(kernel, name, token, scalars, arrays, out_shapes, scratch, vmem_mib):
    def body(*refs):
        first_out = 1 + len(scalars) + len(arrays)
        refs[first_out][...] = jnp.zeros(TOKEN, F32)
        kernel(*refs[1:first_out], *refs[first_out + 1 :])

    vmem = pl.BlockSpec(memory_space=pltpu.VMEM)
    outs = pl.pallas_call(
        body,
        in_specs=[vmem]
        + [pl.BlockSpec(memory_space=pltpu.SMEM)] * len(scalars)
        + [vmem] * len(arrays),
        out_specs=[vmem] * (1 + len(out_shapes)),
        out_shape=[pltpu.VMEM(TOKEN, F32)]
        + [pltpu.VMEM(shape, dtype) for shape, dtype in out_shapes],
        scratch_shapes=scratch,
        compiler_params=pltpu.CompilerParams(vmem_limit_bytes=vmem_mib * MIB),
        cost_estimate=estimate(name),
        name=name,
    )(token, *scalars, *arrays)
    return outs[0], outs[1:]


def load_kernel(*refs, windows):
    count = len(windows)
    sources, token_ref, targets, sems = (
        refs[:count], refs[count + 1], refs[count + 2 : -1], refs[-1],
    )
    copies = [
        pltpu.make_async_copy(source.at[window], target, sems.at[i])
        for i, (source, target, window) in enumerate(zip(sources, targets, windows))
    ]
    for copy in copies:
        copy.start()
    token_ref[...] = jnp.zeros(TOKEN, F32)
    for copy in copies:
        copy.wait()


def load(name, token, arrays, windows):
    shapes = [
        tuple(w.size if isinstance(w, pl.Slice) else n for w, n in zip(window, a.shape))
        for a, window in zip(arrays, windows)
    ]
    vmem = pl.BlockSpec(memory_space=pltpu.VMEM)
    outs = pl.pallas_call(
        functools.partial(load_kernel, windows=windows),
        in_specs=[pl.BlockSpec(memory_space=pltpu.HBM)] * len(arrays) + [vmem],
        out_specs=[vmem] * (1 + len(arrays)),
        out_shape=[pltpu.VMEM(TOKEN, F32)]
        + [pltpu.VMEM(shape, a.dtype) for a, shape in zip(arrays, shapes)],
        scratch_shapes=[pltpu.SemaphoreType.DMA((len(arrays),))],
        compiler_params=pltpu.CompilerParams(vmem_limit_bytes=MIB),
        cost_estimate=estimate(name),
        name=name,
    )(*[pltpu.with_memory_space_constraint(a, pltpu.HBM) for a in arrays], token)
    return outs[0], outs[1:]


def project_kernel(*refs, nz, per, first, heads):
    place_ref = refs[0]
    if first:
        own_ref, other_ref, gain_ref, sor_ref, wq_ref, wk_ref, wv_ref = refs[1:8]
        *out_refs, slotted_ref, acc = refs[8:]
        one_hot = slot_one_hot(place_ref, sor_ref[...], nz, per)
        own, other = own_ref[...], other_ref[...]
        lower = place_ref[2] == 0
        rows = jnp.concatenate(
            [jnp.where(lower, own, other), jnp.where(lower, other, own)], axis=0
        )
        hidden = jnp.dot(one_hot, rows, preferred_element_type=F32)
        gain = gain_ref[...].astype(F32)
        gain = jnp.concatenate([gain[j : j + 1] for j in range(gain.shape[0])], axis=1)
        slotted_ref[...] = (hidden * gain).astype(BF16)
        squares = jnp.sum(hidden * hidden, axis=1, keepdims=True)
        high = squares.astype(BF16).astype(F32)
        low = squares - high
        lane = lax.broadcasted_iota(jnp.int32, (per, HEAD_SIZE), 1)
        lane_high = place_ref[1] * 2
        for b, ref in enumerate(out_refs):
            for z in range(nz):
                at = (b * nz + z) * per
                packed = jnp.where(
                    lane == lane_high,
                    high[at : at + per],
                    jnp.where(lane == lane_high + 1, low[at : at + per], 0.0),
                )
                packed = jnp.concatenate(
                    [packed, jnp.zeros((SQUARE_ROWS - per, HEAD_SIZE), F32)], axis=0
                )
                ref[z, heads * TILES * per :, :] = packed.astype(BF16)
    else:
        slotted_ref, wq_ref, wk_ref, wv_ref = refs[1:5]
        *out_refs, acc = refs[5:]

    columns = QUERIES_PER_KV * HEAD_SIZE
    slotted = slotted_ref[...]
    for g in range(heads):
        acc[:, :columns] = jnp.dot(
            slotted, wq_ref[:, g * columns : (g + 1) * columns], preferred_element_type=F32
        )
        narrow = slice(g * HEAD_SIZE, (g + 1) * HEAD_SIZE)
        acc[:, columns:] = jnp.dot(
            slotted,
            jnp.concatenate([wk_ref[:, narrow], wv_ref[:, narrow]], axis=1),
            preferred_element_type=F32,
        )
        for b, ref in enumerate(out_refs):
            for z in range(nz):
                at = (b * nz + z) * per
                block = jnp.concatenate(
                    [
                        acc[at : at + per, c * HEAD_SIZE : (c + 1) * HEAD_SIZE]
                        for c in range(TILES)
                    ],
                    axis=0,
                )
                ref[z, g * TILES * per : (g + 1) * TILES * per, :] = block.astype(BF16)


def project(token, place, inputs, weights, *, chunk, heads, nz, per):
    first = chunk == 0
    rows = 2 * nz * per
    depth = weights[0].shape[0]
    block_rows = heads * TILES * per + (SQUARE_ROWS if first else 0)
    out_shapes = [((nz, block_rows, HEAD_SIZE), BF16)] * 2
    return call(
        functools.partial(project_kernel, nz=nz, per=per, first=first, heads=heads),
        "project" + str(chunk),
        token,
        [place],
        [*inputs, *weights],
        out_shapes + ([((rows, depth), BF16)] if first else []),
        [pltpu.VMEM((rows, TILES * HEAD_SIZE), F32)],
        12,
    )


def add_kernel(*refs, starts, count):
    terms = len(starts)
    outs = refs[terms:]
    each = outs[0].shape[0]
    for z in range(count):
        total = refs[0][starts[0] + z].astype(F32)
        for ref, start in zip(refs[1:terms], starts[1:]):
            total = total + ref[start + z].astype(F32)
        outs[z // each][z % each] = total.astype(BF16)


def add(name, token, arrays, starts, count, parts):
    shape = (count // parts,) + arrays[0].shape[1:]
    return call(
        functools.partial(add_kernel, starts=starts, count=count),
        name,
        token,
        [],
        arrays,
        [(shape, BF16)] * parts,
        [],
        2,
    )


def join_kernel(a_ref, b_ref, out_ref):
    count = a_ref.shape[0]
    out_ref[:count] = a_ref[...]
    out_ref[count:] = b_ref[...]


def join(name, token, a, b):
    shape = (a.shape[0] + b.shape[0],) + a.shape[1:]
    token, (joined,) = call(join_kernel, name, token, [], [a, b], [(shape, BF16)], [], 2)
    return token, joined


def attend_kernel(*refs, first, heads, per, group, start_head):
    place_ref, lengths_ref, mine_ref, last_ref = refs[:4]
    rest = refs[4:]
    if first:
        qb_ref, kb_ref, vb_ref, cos_ref, sin_ref, k_ref, v_ref, out_ref, scale_ref = rest[:9]
    else:
        scale_in_ref, qb_ref, kb_ref, vb_ref, cos_ref, sin_ref, k_ref, v_ref, out_ref = rest[:9]
    fresh, result = rest[9:]
    body = heads * TILES * per
    head_rows = TILES * per

    if first:
        squares = mine_ref[0, body:, :].astype(F32) + last_ref[0, body:, :].astype(F32)
        total = jnp.sum(squares[:per], axis=1, keepdims=True)
        scale = jnp.broadcast_to(lax.rsqrt(total / MODEL_WIDTH + EPSILON), (per, HEAD_SIZE))
        scale_ref[...] = scale
    else:
        scale = scale_in_ref[...]
    cos, sin = cos_ref[...], sin_ref[...]
    query_bias = qb_ref[...].astype(F32)
    key_bias = kb_ref[...].astype(F32)
    value_bias = vb_ref[...].astype(F32)
    for g in range(heads):
        rows = pl.ds(g * head_rows, head_rows)
        summed = mine_ref[0, rows, :].astype(F32) + last_ref[0, rows, :].astype(F32)
        head = start_head + g
        for c in range(TILES):
            if c < QUERIES_PER_KV:
                at = head * QUERIES_PER_KV + c
                bias = query_bias[at : at + 1]
            else:
                bias = (key_bias if c == QUERIES_PER_KV else value_bias)[head : head + 1]
            tile = summed[c * per : (c + 1) * per] * scale + bias
            if c < TILES - 1:
                tile = tile * cos + pltpu.roll(tile, HEAD_SIZE // 2, 1) * sin
            fresh[pl.ds(g * head_rows + c * per, per), :] = tile.astype(BF16).astype(F32)

    positions = k_ref.shape[1]
    qrows = heads * QUERIES_PER_KV
    lanes = group * qrows
    extra = 16
    lane_block = lax.broadcasted_iota(jnp.int32, (HEAD_SIZE, lanes), 1) // QUERIES_PER_KV
    top_row = lax.broadcasted_iota(jnp.int32, (extra, HEAD_SIZE), 0) == 0
    lane_slot = lax.broadcasted_iota(jnp.int32, (1, lanes), 1) // qrows
    row = lax.broadcasted_iota(jnp.int32, (positions + extra, lanes), 0)
    base = (place_ref[0] * 2 + place_ref[1]) * per
    for start in range(0, per, group):
        slots = range(start, start + group)
        queries = jnp.concatenate(
            [
                fresh[pl.ds(g * head_rows + s, QUERIES_PER_KV, stride=per), :]
                for s in slots
                for g in range(heads)
            ],
            axis=0,
        )
        turned = queries.T
        scores = None
        for i, s in enumerate(slots):
            query, new_key = [], []
            for g in range(heads):
                query.append(jnp.where(lane_block == i * heads + g, turned, 0.0).astype(BF16))
                key = fresh[pl.ds(g * head_rows + QUERIES_PER_KV * per + s, 1), :]
                new_key.append(jnp.where(top_row, key, 0.0).astype(BF16))
            keys = jnp.concatenate([k_ref[s], jnp.concatenate(new_key, axis=1)], axis=0)
            term = jnp.dot(keys, jnp.concatenate(query, axis=0), preferred_element_type=F32)
            scores = term if scores is None else scores + term

        lengths = jnp.zeros((1, lanes), jnp.int32)
        for i, s in enumerate(slots):
            lengths = jnp.where(lane_slot == i, lengths_ref[base + s], lengths)
        valid = (row < lengths) | (row == positions)
        scores = jnp.where(valid, scores * (1.0 / math.sqrt(HEAD_SIZE)), -1e30)
        top = jnp.max(scores, axis=0, keepdims=True)
        exps = jnp.where(valid, jnp.exp(scores - top), 0.0)
        weights = exps * (1.0 / jnp.sum(exps, axis=0, keepdims=True))
        cache_weights = weights[:positions].T
        own_weights = weights[positions : positions + 8].T[:, 0:1].astype(BF16).astype(F32)
        for i, s in enumerate(slots):
            mixed = jnp.dot(
                cache_weights[i * qrows : (i + 1) * qrows].astype(BF16),
                v_ref[s],
                preferred_element_type=F32,
            )
            for g in range(heads):
                lo, hi = g * QUERIES_PER_KV, (g + 1) * QUERIES_PER_KV
                new_value = fresh[pl.ds(g * head_rows + (QUERIES_PER_KV + 1) * per + s, 1), :]
                result[pl.ds(g * QUERIES_PER_KV * per + s, QUERIES_PER_KV, stride=per), :] = (
                    mixed[lo:hi, g * HEAD_SIZE : (g + 1) * HEAD_SIZE]
                    + own_weights[i * qrows + lo : i * qrows + hi] * new_value
                )
    out_ref[0] = result[...].astype(BF16)


def attend(token, place, lengths, parts, scale, biases, cos, sin, keys, values, *, chunk, heads):
    first = chunk == 0
    per = keys.shape[0]
    out_rows = heads * QUERIES_PER_KV * per
    return call(
        functools.partial(
            attend_kernel,
            first=first,
            heads=heads,
            per=per,
            group=SLOTS_AT_ONCE[heads],
            start_head=sum(CHUNK_HEADS[:chunk]),
        ),
        "attend" + str(chunk),
        token,
        [place, lengths],
        list(parts) + ([] if first else [scale]) + list(biases) + [cos, sin, keys, values],
        [((1, out_rows, HEAD_SIZE), BF16)] + ([((per, HEAD_SIZE), F32)] if first else []),
        [
            pltpu.VMEM((heads * TILES * per, HEAD_SIZE), F32),
            pltpu.VMEM((out_rows, HEAD_SIZE), F32),
        ],
        8,
    )


def output_kernel(*refs, labels, nz, per, first, last):
    count = len(labels)
    place_ref, block_refs, sor_ref, w_ref = refs[0], refs[1 : 1 + count], refs[1 + count], refs[2 + count]
    rest = refs[3 + count :]
    if not first:
        acc_in_ref, rest = rest[0], rest[1:]
    if last:
        mine_ref, send_ref, stacked, total = rest
    else:
        acc_out_ref, stacked = rest
    tiles = block_refs[0].shape[1] // per

    one_hot = slot_one_hot(place_ref, sor_ref[...], nz, per)
    wide = {
        label: ref[z].astype(F32)
        for ref, own in zip(block_refs, labels)
        for z, label in enumerate(own)
    }
    wide = [wide[h, q] for h in range(2) for q in place_order(nz)]
    for c in range(tiles):
        stacked[:, c * HEAD_SIZE : (c + 1) * HEAD_SIZE] = jnp.concatenate(
            [block[c * per : (c + 1) * per] for block in wide], axis=0
        ).astype(BF16)
    permuted = lax.dot_general(
        one_hot, stacked[...], (((0,), (0,)), ((), ())), preferred_element_type=F32
    ).astype(BF16)
    stacked[...] = permuted
    product = jnp.dot(stacked[...], w_ref[...], preferred_element_type=F32)
    if not first:
        product = product + acc_in_ref[...]
    if last:
        half = product.shape[0] // 2
        total[...] = product
        mine_ref[...] = total[pl.ds(pl.multiple_of(place_ref[2] * half, half), half), :]
        send_ref[...] = total[
            pl.ds(pl.multiple_of((1 - place_ref[2]) * half, half), half), :
        ].astype(BF16)
    else:
        acc_out_ref[...] = product


def output(token, place, blocks, labels, sor, w_out, acc, *, chunk, chunks, nz, per):
    first, last = chunk == 0, chunk == chunks - 1
    rows = 2 * nz * per
    depth, width = w_out.shape
    if last:
        out_shapes = [((rows // 2, width), F32), ((rows // 2, width), BF16)]
    else:
        out_shapes = [((rows, width), F32)]
    return call(
        functools.partial(
            output_kernel, labels=labels, nz=nz, per=per, first=first, last=last
        ),
        "output" + str(chunk),
        token,
        [place],
        [*blocks, sor, w_out] + ([] if first else [acc]),
        out_shapes,
        [pltpu.VMEM((rows, depth), BF16)] + ([pltpu.VMEM((rows, width), F32)] if last else []),
        12,
    )


def on_device(
    hidden_rows,
    norm_gain,
    w_query,
    key_weight,
    value_weight,
    query_bias,
    key_bias_vector,
    value_bias_vector,
    rotated_key_cache,
    stored_value_cache,
    slot_valid_lengths,
    slot_of_row,
    w_out,
    *,
    size,
):
    nz = size // 2
    assert size % 2 == 0 and nz & (nz - 1) == 0 and nz > 2
    per = rotated_key_cache.shape[0]
    kv_heads = key_weight.shape[1] // HEAD_SIZE
    assert sum(CHUNK_HEADS) == kv_heads and per == SLOTS_AT_ONCE[1]
    chunks = len(CHUNK_HEADS)
    gx = lax.axis_index("gx")
    gy = lax.axis_index("gy")
    place = jnp.stack([gx // 2, gx % 2, gy]).astype(jnp.int32)

    other = lax.ppermute(hidden_rows, "gy", [(0, 1), (1, 0)])
    sor = slot_of_row[None, :]
    gain = norm_gain.reshape(-1, HEAD_SIZE)

    lengths = lax.dynamic_slice_in_dim(slot_valid_lengths, gx * per, per, 0)
    lane = jnp.arange(HEAD_SIZE)
    half_width = HEAD_SIZE // 2
    frequency = ROPE_BASE ** (-((lane % half_width).astype(F32) * 2.0 / HEAD_SIZE))
    angles = lengths.astype(F32)[:, None] * frequency[None, :]
    cos = jnp.cos(angles)
    sin = jnp.sin(angles) * jnp.where(lane < half_width, -1.0, 1.0)[None, :]
    biases = [b.reshape(-1, HEAD_SIZE) for b in (query_bias, key_bias_vector, value_bias_vector)]

    def head_window(c, width):
        return pl.ds(sum(CHUNK_HEADS[:c]) * width, CHUNK_HEADS[c] * width)

    wide = QUERIES_PER_KV * HEAD_SIZE
    everything = pl.ds(0, w_query.shape[0])
    positions = rotated_key_cache.shape[1]
    all_columns = pl.ds(0, w_out.shape[1])
    same_z = neighbour_pairs(nz)
    scale = acc = None
    inputs = [hidden_rows, other, gain, sor]
    kept, swapped, reduced = {}, {}, {}
    caches, w_outs, gathered, waiting = {}, {}, {}, {}

    def over_y(blocks, labels):
        return lax.ppermute(blocks, "gx", same_z), [(1 - h, q) for h, q in labels]

    def over_z(blocks, labels, stride):
        moved = lax.ppermute(blocks, "gx", stride_pairs(nz, stride))
        return moved, [(h, q ^ stride) for h, q in labels]

    def do_project(token, c):
        nonlocal inputs
        token, weights = load(
            "load_weights" + str(c),
            token,
            [w_query, key_weight, value_weight],
            [(everything, head_window(c, n)) for n in (wide, HEAD_SIZE, HEAD_SIZE)],
        )
        token, outs = project(
            token, place, inputs, weights, chunk=c, heads=CHUNK_HEADS[c], nz=nz, per=per
        )
        kept[c] = outs[0]
        if c == 0:
            inputs = [outs[2]]
        swapped[c] = lax.ppermute(outs[1], "gx", same_z)
        return token

    def do_load_caches(token, c):
        token, caches[c] = load(
            "load_caches" + str(c),
            token,
            [rotated_key_cache, stored_value_cache],
            [(pl.ds(0, per), pl.ds(0, positions), head_window(c, HEAD_SIZE))] * 2,
        )
        return token

    def do_load_out(token, c):
        token, (w_outs[c],) = load(
            "load_out" + str(c), token, [w_out], [(head_window(c, wide), all_columns)]
        )
        return token

    def do_far(token, c):
        half = nz // 2
        token, (total,) = add(
            "add_far" + str(c), token, [kept[c], swapped[c]], [half, half], half, 1
        )
        reduced[c] = lax.ppermute(total, "gx", stride_pairs(nz, 1))
        return token

    def do_near(token, c):
        terms, starts, count = [kept[c], swapped[c], reduced[c]], [0, 0, 0], nz // 2
        for stride in strides(nz)[1:]:
            token, (mine, sent) = add(
                "add_near" + str(c) + "_" + str(stride), token, terms, starts, count, 2
            )
            terms = [mine, lax.ppermute(sent, "gx", stride_pairs(nz, stride))]
            starts, count = [0, 0], count // 2
        reduced[c] = terms
        return token

    def do_attend(token, c):
        nonlocal scale
        token, outs = attend(
            token, place, slot_valid_lengths, reduced[c], scale, biases, cos, sin, *caches[c],
            chunk=c, heads=CHUNK_HEADS[c],
        )
        if c == 0:
            scale = outs[1]
        own = outs[0], [(0, 0)]
        first_move = over_y(*own) if GATHER[c] == "y first" else over_z(*own, strides(nz)[-1])
        waiting[c] = own, first_move
        return token

    def do_gather(token, c):
        held, moved = waiting[c]
        for stride in reversed(strides(nz) if GATHER[c] == "y first" else strides(nz)[:-1]):
            if GATHER[c] == "y first" and stride == 1:
                break
            token, joined = join("join" + str(c) + "_" + str(stride), token, held[0], moved[0])
            held = joined, held[1] + moved[1]
            moved = over_z(*held, stride)
        waiting[c] = held, moved
        gathered[c] = [held, moved]
        if GATHER[c] == "y halved":
            gathered[c].append(over_y(*held))
        return token

    def do_forward(token, c):
        held, moved = waiting[c]
        if GATHER[c] == "y halved":
            gathered[c].append(over_y(*moved))
            return token
        token, joined = join("join" + str(c), token, held[0], moved[0])
        held = joined, held[1] + moved[1]
        gathered[c] = [held, over_z(*held, 1) if GATHER[c] == "y first" else over_y(*held)]
        return token

    def do_output(token, c):
        nonlocal acc
        token, acc = output(
            token, place, [a for a, _ in gathered[c]], [own for _, own in gathered[c]], sor,
            w_outs[c], acc if c == 0 else acc[0], chunk=c, chunks=chunks, nz=nz, per=per,
        )
        return token

    token = jnp.zeros(TOKEN, F32)
    steps = {
        "project": do_project,
        "load_caches": do_load_caches,
        "load_out": do_load_out,
        "far": do_far,
        "near": do_near,
        "attend": do_attend,
        "gather": do_gather,
        "forward": do_forward,
        "output": do_output,
    }
    for step, c in ORDER:
        token = steps[step](token, c)
    mine, send = acc
    received = lax.ppermute(send, "gy", [(0, 1), (1, 0)])
    return (hidden_rows.astype(F32) + mine + received.astype(F32)).astype(BF16)


def solution(mesh):
    in_specs = (
        P(("grp", "gy"), "gx"),
        P("gx"),
        P("gx", "gy"),
        P("gx", "gy"),
        P("gx", "gy"),
        P("gy"),
        P("gy"),
        P("gy"),
        P(("grp", "gx"), None, "gy"),
        P(("grp", "gx"), None, "gy"),
        P("grp"),
        P("grp"),
        P("gy", "gx"),
    )
    out_specs = P(("grp", "gy"), "gx")
    return jax.shard_map(
        functools.partial(on_device, size=mesh.shape["gx"]),
        mesh=mesh,
        in_specs=in_specs,
        out_specs=out_specs,
        check_vma=False,
    )
```

```python
import functools
import math

import jax
import jax.numpy as jnp
from jax import lax
from jax.experimental import pallas as pl
from jax.experimental.pallas import tpu as pltpu
from jax.sharding import PartitionSpec as P

MODEL_WIDTH = 8192
QUERY_HEADS = 64
KEY_VALUE_HEADS = 8
HEAD_SIZE = 128
QUERIES_PER_KV = QUERY_HEADS // KEY_VALUE_HEADS
TILES = QUERIES_PER_KV + 2
SQUARE_ROWS = 32

EPSILON = 1e-06
ROPE_BASE = 1000000.0
CHUNK_HEADS = (1, 2, 1)
F32 = jnp.float32
BF16 = jnp.bfloat16
MIB = 1024 * 1024
SLOTS_AT_ONCE = {1: 24, 2: 8, 3: 8, 4: 4}
PEAK_FLOP_PER_US = 1.1535e9
COSTS = {'project0': 1.35, 'attend0': 2.1, 'join0_2': 0.1, 'join0': 0.1, 'output0': 8, 'project1': 1, 'add_near1_2': 2, 'attend1': 1, 'join1_2': 1, 'output1': 8, 'project2': 1.35, 'add_far2': 0.15, 'add_near2_2': 0.3, 'attend2': 2.1, 'join2_2': 8, 'output2': 1.28, 'join1_1': 2, 'join2_1': 4, 'add_far0': 2, 'join2': 4}
GATHER = ("all_gather", "y halved", "y halved")
ORDER = (
    ("caches", 0),
    ("weights", 0),
    ("project", 0),
    ("weights", 1),
    ("project", 1),
    ("far", 0),
    ("out", 0),
    ("caches", 1),
    ("near", 0),
    ("weights", 2),
    ("project", 2),
    ("far", 1),
    ("attend", 0),
    ("far", 2),
    ("near", 1),
    ("gather", 0),
    ("caches", 2),
    ("near", 2),
    ("attend", 1),
    ("forward", 0),
    ("attend", 2),
    ("gather", 1),
    ("out", 2),
    ("gather", 2),
    ("output", 0),
    ("forward", 1),
    ("forward", 2),
    ("out", 1),
    ("output", 1),
    ("output", 2),
)
F32 = jnp.float32
BF16 = jnp.bfloat16


def neighbour_pairs(nz):
    return [(z * 2 + y, z * 2 + 1 - y) for z in range(nz) for y in range(2)]


def stride_pairs(nz, stride):
    return [(z * 2 + y, (z ^ stride) * 2 + y) for z in range(nz) for y in range(2)]


def strides(nz):
    return [1 << i for i in range(nz.bit_length() - 1)]


def place_order(nz):
    return sorted(range(nz), key=lambda q: [(q & b) != 0 for b in strides(nz)])


def slot_one_hot(place_ref, slot_of_row, nz, per, absolute=False):
    rows = slot_of_row.shape[1]
    base = lax.broadcasted_iota(jnp.int32, (per, rows), 0)
    blocks = []
    for h in range(2):
        for q in place_order(nz):
            if absolute:
                owner = len(blocks)
            else:
                owner = (place_ref[0] ^ q) * 2 + (place_ref[1] ^ h)
            blocks.append(jnp.where(base + owner * per == slot_of_row, 1.0, 0.0).astype(F32))
    return jnp.concatenate(blocks, axis=0).astype(BF16)


TOKEN = (8, HEAD_SIZE)


def estimate(name):
    flops = int(COSTS.get(name, 0) * PEAK_FLOP_PER_US)
    return pl.CostEstimate(flops=flops, bytes_accessed=0, transcendentals=0)


def copies_of(sources, windows, targets, sems):
    return [
        pltpu.make_async_copy(source.at[window], target, sems.at[i])
        for i, (source, window, target) in enumerate(zip(sources, windows, targets))
    ]


def call(kernel, name, token, scalars, arrays, out_shapes, scratch, vmem_mib, loads=()):
    sources = [array for array, _ in loads]
    windows = [window for _, window in loads]
    loaded_shapes = [
        tuple(w.size if isinstance(w, pl.Slice) else n for w, n in zip(window, array.shape))
        for array, window in loads
    ]

    def body(*refs):
        refs = list(refs)
        del refs[0]
        source_refs = [refs.pop(0) for _ in loads]
        in_refs = [refs.pop(0) for _ in range(len(scalars) + len(arrays))]
        token_ref = refs.pop(0)
        target_refs = [refs.pop(0) for _ in loads]
        copies = copies_of(source_refs, windows, target_refs, refs.pop() if loads else None)
        for copy in copies:
            copy.start()
        token_ref[...] = jnp.zeros(TOKEN, F32)
        kernel(*in_refs, *refs)
        for copy in copies:
            copy.wait()

    vmem = pl.BlockSpec(memory_space=pltpu.VMEM)
    outs = pl.pallas_call(
        body,
        in_specs=[vmem]
        + [pl.BlockSpec(memory_space=pltpu.HBM)] * len(loads)
        + [pl.BlockSpec(memory_space=pltpu.SMEM)] * len(scalars)
        + [vmem] * len(arrays),
        out_specs=[vmem] * (1 + len(loads) + len(out_shapes)),
        out_shape=[pltpu.VMEM(TOKEN, F32)]
        + [pltpu.VMEM(shape, array.dtype) for shape, array in zip(loaded_shapes, sources)]
        + [pltpu.VMEM(shape, dtype) for shape, dtype in out_shapes],
        scratch_shapes=list(scratch) + ([pltpu.SemaphoreType.DMA((len(loads),))] if loads else []),
        compiler_params=pltpu.CompilerParams(vmem_limit_bytes=vmem_mib * MIB),
        cost_estimate=estimate(name),
        name=name,
    )(
        token,
        *[pltpu.with_memory_space_constraint(array, pltpu.HBM) for array in sources],
        *scalars,
        *arrays,
    )
    return outs[0], outs[1 : 1 + len(loads)], outs[1 + len(loads) :]


def project_kernel(*refs, nz, per, first, heads):
    place_ref = refs[0]
    if first:
        own_ref, other_ref, gain_ref, sor_ref, wq_ref, wk_ref, wv_ref = refs[1:8]
        *out_refs, slotted_ref, acc = refs[8:]
        one_hot = slot_one_hot(place_ref, sor_ref[...], nz, per)
        own, other = own_ref[...], other_ref[...]
        lower = place_ref[2] == 0
        rows = jnp.concatenate(
            [jnp.where(lower, own, other), jnp.where(lower, other, own)], axis=0
        )
        hidden = jnp.dot(one_hot, rows, preferred_element_type=F32)
        gain = gain_ref[...].astype(F32)
        gain = jnp.concatenate([gain[j : j + 1] for j in range(gain.shape[0])], axis=1)
        slotted_ref[...] = (hidden * gain).astype(BF16)
        squares = jnp.sum(hidden * hidden, axis=1, keepdims=True)
        high = squares.astype(BF16).astype(F32)
        low = squares - high
        lane = lax.broadcasted_iota(jnp.int32, (per, HEAD_SIZE), 1)
        lane_high = place_ref[1] * 2
        for b, ref in enumerate(out_refs):
            for z in range(nz):
                at = (b * nz + z) * per
                packed = jnp.where(
                    lane == lane_high,
                    high[at : at + per],
                    jnp.where(lane == lane_high + 1, low[at : at + per], 0.0),
                )
                packed = jnp.concatenate(
                    [packed, jnp.zeros((SQUARE_ROWS - per, HEAD_SIZE), F32)], axis=0
                )
                ref[z, heads * TILES * per :, :] = packed.astype(BF16)
    else:
        slotted_ref, wq_ref, wk_ref, wv_ref = refs[1:5]
        *out_refs, acc = refs[5:]

    columns = QUERIES_PER_KV * HEAD_SIZE
    slotted = slotted_ref[...]
    for g in range(heads):
        acc[:, :columns] = jnp.dot(
            slotted, wq_ref[:, g * columns : (g + 1) * columns], preferred_element_type=F32
        )
        narrow = slice(g * HEAD_SIZE, (g + 1) * HEAD_SIZE)
        acc[:, columns:] = jnp.dot(
            slotted,
            jnp.concatenate([wk_ref[:, narrow], wv_ref[:, narrow]], axis=1),
            preferred_element_type=F32,
        )
        for b, ref in enumerate(out_refs):
            for z in range(nz):
                at = (b * nz + z) * per
                block = jnp.concatenate(
                    [
                        acc[at : at + per, c * HEAD_SIZE : (c + 1) * HEAD_SIZE]
                        for c in range(TILES)
                    ],
                    axis=0,
                )
                ref[z, g * TILES * per : (g + 1) * TILES * per, :] = block.astype(BF16)


def project(token, place, inputs, weights, loads, *, chunk, heads, nz, per):
    first = chunk == 0
    rows = 2 * nz * per
    depth = weights[0].shape[0]
    block_rows = heads * TILES * per + (SQUARE_ROWS if first else 0)
    out_shapes = [((nz, block_rows, HEAD_SIZE), BF16)] * 2
    return call(
        functools.partial(project_kernel, nz=nz, per=per, first=first, heads=heads),
        "project" + str(chunk),
        token,
        [place],
        [*inputs, *weights],
        out_shapes + ([((rows, depth), BF16)] if first else []),
        [pltpu.VMEM((rows, TILES * HEAD_SIZE), F32)],
        12,
        loads,
    )


def add_kernel(*refs, starts, count):
    terms = len(starts)
    outs = refs[terms:]
    each = outs[0].shape[0]
    for z in range(count):
        total = refs[0][starts[0] + z].astype(F32)
        for ref, start in zip(refs[1:terms], starts[1:]):
            total = total + ref[start + z].astype(F32)
        outs[z // each][z % each] = total.astype(BF16)


def add(name, token, arrays, starts, count, parts):
    shape = (count // parts,) + arrays[0].shape[1:]
    token, _, sums = call(
        functools.partial(add_kernel, starts=starts, count=count),
        name,
        token,
        [],
        arrays,
        [(shape, BF16)] * parts,
        [],
        2,
    )
    return token, sums


def join_kernel(a_ref, b_ref, out_ref):
    count = a_ref.shape[0]
    out_ref[:count] = a_ref[...]
    out_ref[count:] = b_ref[...]


def join(name, token, a, b):
    shape = (a.shape[0] + b.shape[0],) + a.shape[1:]
    token, _, (joined,) = call(join_kernel, name, token, [], [a, b], [(shape, BF16)], [], 2)
    return token, joined


def attend_kernel(*refs, first, heads, per, group, start_head):
    place_ref, lengths_ref, mine_ref, last_ref = refs[:4]
    rest = refs[4:]
    if first:
        qb_ref, kb_ref, vb_ref, cos_ref, sin_ref, k_ref, v_ref, out_ref, scale_ref = rest[:9]
    else:
        scale_in_ref, qb_ref, kb_ref, vb_ref, cos_ref, sin_ref, k_ref, v_ref, out_ref = rest[:9]
    fresh, result = rest[9:]
    body = heads * TILES * per
    head_rows = TILES * per

    if first:
        squares = mine_ref[0, body:, :].astype(F32) + last_ref[0, body:, :].astype(F32)
        total = jnp.sum(squares[:per], axis=1, keepdims=True)
        scale = jnp.broadcast_to(lax.rsqrt(total / MODEL_WIDTH + EPSILON), (per, HEAD_SIZE))
        scale_ref[...] = scale
    else:
        scale = scale_in_ref[...]
    cos, sin = cos_ref[...], sin_ref[...]
    query_bias = qb_ref[...].astype(F32)
    key_bias = kb_ref[...].astype(F32)
    value_bias = vb_ref[...].astype(F32)
    for g in range(heads):
        rows = pl.ds(g * head_rows, head_rows)
        summed = mine_ref[0, rows, :].astype(F32) + last_ref[0, rows, :].astype(F32)
        head = start_head + g
        for c in range(TILES):
            if c < QUERIES_PER_KV:
                at = head * QUERIES_PER_KV + c
                bias = query_bias[at : at + 1]
            else:
                bias = (key_bias if c == QUERIES_PER_KV else value_bias)[head : head + 1]
            tile = summed[c * per : (c + 1) * per] * scale + bias
            if c < TILES - 1:
                tile = tile * cos + pltpu.roll(tile, HEAD_SIZE // 2, 1) * sin
            fresh[pl.ds(g * head_rows + c * per, per), :] = tile.astype(BF16).astype(F32)

    positions = k_ref.shape[1]
    qrows = heads * QUERIES_PER_KV
    lanes = group * qrows
    extra = 16
    lane_block = lax.broadcasted_iota(jnp.int32, (HEAD_SIZE, lanes), 1) // QUERIES_PER_KV
    top_row = lax.broadcasted_iota(jnp.int32, (extra, HEAD_SIZE), 0) == 0
    lane_slot = lax.broadcasted_iota(jnp.int32, (1, lanes), 1) // qrows
    row = lax.broadcasted_iota(jnp.int32, (positions + extra, lanes), 0)
    row_slot = lax.broadcasted_iota(jnp.int32, (lanes, positions), 0) // qrows
    base = (place_ref[0] * 2 + place_ref[1]) * per
    for start in range(0, per, group):
        slots = range(start, start + group)
        queries = jnp.concatenate(
            [
                fresh[pl.ds(g * head_rows + s, QUERIES_PER_KV, stride=per), :]
                for s in slots
                for g in range(heads)
            ],
            axis=0,
        )
        turned = queries.T
        query, new_key = [], []
        for i, s in enumerate(slots):
            for g in range(heads):
                query.append(jnp.where(lane_block == i * heads + g, turned, 0.0).astype(BF16))
                key = fresh[pl.ds(g * head_rows + QUERIES_PER_KV * per + s, 1), :]
                new_key.append(jnp.where(top_row, key, 0.0).astype(BF16))
        keys = jnp.concatenate(
            [
                jnp.concatenate([k_ref[s] for s in slots], axis=1),
                jnp.concatenate(new_key, axis=1),
            ],
            axis=0,
        )
        scores = jnp.dot(keys, jnp.concatenate(query, axis=0), preferred_element_type=F32)

        lengths = jnp.zeros((1, lanes), jnp.int32)
        for i, s in enumerate(slots):
            lengths = jnp.where(lane_slot == i, lengths_ref[base + s], lengths)
        valid = (row < lengths) | (row == positions)
        scores = jnp.where(valid, scores * (1.0 / math.sqrt(HEAD_SIZE)), -1e30)
        top = jnp.max(scores, axis=0, keepdims=True)
        exps = jnp.where(valid, jnp.exp(scores - top), 0.0)
        weights = exps * (1.0 / jnp.sum(exps, axis=0, keepdims=True))
        cache_weights = weights[:positions].T
        own_weights = weights[positions : positions + 8].T[:, 0:1].astype(BF16).astype(F32)
        spread = jnp.concatenate(
            [jnp.where(row_slot == i, cache_weights, 0.0).astype(BF16) for i in range(group)],
            axis=1,
        )
        values = v_ref[start : start + group].reshape(group * positions, heads * HEAD_SIZE)
        mixed = jnp.dot(spread, values, preferred_element_type=F32)
        for i, s in enumerate(slots):
            for g in range(heads):
                lo = i * qrows + g * QUERIES_PER_KV
                hi = lo + QUERIES_PER_KV
                new_value = fresh[pl.ds(g * head_rows + (QUERIES_PER_KV + 1) * per + s, 1), :]
                result[pl.ds(g * QUERIES_PER_KV * per + s, QUERIES_PER_KV, stride=per), :] = (
                    mixed[lo:hi, g * HEAD_SIZE : (g + 1) * HEAD_SIZE]
                    + own_weights[lo:hi] * new_value
                )
    out_ref[0] = result[...].astype(BF16)


def attend(
    token, place, lengths, parts, scale, biases, cos, sin, keys, values, loads, *, chunk, heads
):
    first = chunk == 0
    per = keys.shape[0]
    out_rows = heads * QUERIES_PER_KV * per
    return call(
        functools.partial(
            attend_kernel,
            first=first,
            heads=heads,
            per=per,
            group=SLOTS_AT_ONCE[heads],
            start_head=sum(CHUNK_HEADS[:chunk]),
        ),
        "attend" + str(chunk),
        token,
        [place, lengths],
        list(parts) + ([] if first else [scale]) + list(biases) + [cos, sin, keys, values],
        [((1, out_rows, HEAD_SIZE), BF16)] + ([((per, HEAD_SIZE), F32)] if first else []),
        [
            pltpu.VMEM((heads * TILES * per, HEAD_SIZE), F32),
            pltpu.VMEM((out_rows, HEAD_SIZE), F32),
        ],
        8,
        loads,
    )


def output_kernel(*refs, labels, nz, per, first, last, absolute):
    count = len(labels)
    place_ref, block_refs, sor_ref, w_ref = refs[0], refs[1 : 1 + count], refs[1 + count], refs[2 + count]
    rest = refs[3 + count :]
    if not first:
        acc_in_ref, rest = rest[0], rest[1:]
    if last:
        mine_ref, send_ref, stacked = rest
    else:
        acc_out_ref, stacked = rest
    tiles = block_refs[0].shape[1] // per

    half = sor_ref.shape[1] // 2
    slot_of_row = sor_ref[...]
    swapped = jnp.concatenate([slot_of_row[:, half:], slot_of_row[:, :half]], axis=1)
    slot_of_row = jnp.where(place_ref[2] == 0, slot_of_row, swapped)
    one_hot = slot_one_hot(place_ref, slot_of_row, nz, per, absolute)
    wide = {
        label: ref[z].astype(F32)
        for ref, own in zip(block_refs, labels)
        for z, label in enumerate(own)
    }
    if absolute:
        wide = [wide[owner] for owner in range(2 * nz)]
    else:
        wide = [wide[h, q] for h in range(2) for q in place_order(nz)]
    for c in range(tiles):
        stacked[:, c * HEAD_SIZE : (c + 1) * HEAD_SIZE] = jnp.concatenate(
            [block[c * per : (c + 1) * per] for block in wide], axis=0
        ).astype(BF16)
    permuted = lax.dot_general(
        one_hot, stacked[...], (((0,), (0,)), ((), ())), preferred_element_type=F32
    ).astype(BF16)
    stacked[...] = permuted
    product = jnp.dot(stacked[...], w_ref[...], preferred_element_type=F32)
    if not first:
        product = product + acc_in_ref[...]
    if last:
        mine_ref[...] = product[:half]
        send_ref[...] = product[half:].astype(BF16)
    else:
        acc_out_ref[...] = product


def output(token, place, blocks, labels, sor, w_out, acc, loads, *, chunk, chunks, nz, per):
    first, last = chunk == 0, chunk == chunks - 1
    rows = 2 * nz * per
    depth, width = w_out.shape
    if last:
        out_shapes = [((rows // 2, width), F32), ((rows // 2, width), BF16)]
    else:
        out_shapes = [((rows, width), F32)]
    return call(
        functools.partial(
            output_kernel,
            labels=labels,
            nz=nz,
            per=per,
            first=first,
            last=last,
            absolute=GATHER[chunk] == "all_gather",
        ),
        "output" + str(chunk),
        token,
        [place],
        [*blocks, sor, w_out] + ([] if first else [acc]),
        out_shapes,
        [pltpu.VMEM((rows, depth), BF16)],
        12,
        loads,
    )


def on_device(
    hidden_rows,
    norm_gain,
    w_query,
    key_weight,
    value_weight,
    query_bias,
    key_bias_vector,
    value_bias_vector,
    rotated_key_cache,
    stored_value_cache,
    slot_valid_lengths,
    slot_of_row,
    w_out,
    *,
    size,
):
    nz = size // 2
    assert size % 2 == 0 and nz & (nz - 1) == 0 and nz > 2
    per = rotated_key_cache.shape[0]
    kv_heads = key_weight.shape[1] // HEAD_SIZE
    assert sum(CHUNK_HEADS) == kv_heads and per == SLOTS_AT_ONCE[1]
    chunks = len(CHUNK_HEADS)
    gx = lax.axis_index("gx")
    gy = lax.axis_index("gy")
    place = jnp.stack([gx // 2, gx % 2, gy]).astype(jnp.int32)

    other = lax.ppermute(hidden_rows, "gy", [(0, 1), (1, 0)])
    sor = slot_of_row[None, :]
    gain = norm_gain.reshape(-1, HEAD_SIZE)

    lengths = lax.dynamic_slice_in_dim(slot_valid_lengths, gx * per, per, 0)
    lane = jnp.arange(HEAD_SIZE)
    half_width = HEAD_SIZE // 2
    frequency = ROPE_BASE ** (-((lane % half_width).astype(F32) * 2.0 / HEAD_SIZE))
    angles = lengths.astype(F32)[:, None] * frequency[None, :]
    cos = jnp.cos(angles)
    sin = jnp.sin(angles) * jnp.where(lane < half_width, -1.0, 1.0)[None, :]
    biases = [b.reshape(-1, HEAD_SIZE) for b in (query_bias, key_bias_vector, value_bias_vector)]

    def head_window(c, width):
        return pl.ds(sum(CHUNK_HEADS[:c]) * width, CHUNK_HEADS[c] * width)

    wide = QUERIES_PER_KV * HEAD_SIZE
    everything = pl.ds(0, w_query.shape[0])
    positions = rotated_key_cache.shape[1]
    all_columns = pl.ds(0, w_out.shape[1])
    same_z = neighbour_pairs(nz)
    scale = acc = None
    inputs = [hidden_rows, other, gain, sor]
    kept, swapped, reduced = {}, {}, {}
    loaded, gathered, waiting = {}, {}, {}

    def over_y(blocks, labels):
        return lax.ppermute(blocks, "gx", same_z), [(1 - h, q) for h, q in labels]

    def over_z(blocks, labels, stride):
        moved = lax.ppermute(blocks, "gx", stride_pairs(nz, stride))
        return moved, [(h, q ^ stride) for h, q in labels]

    def windows_of(kind, c):
        if kind == "weights":
            return [
                (array, (everything, head_window(c, n)))
                for array, n in (
                    (w_query, wide), (key_weight, HEAD_SIZE), (value_weight, HEAD_SIZE),
                )
            ]
        if kind == "caches":
            window = (pl.ds(0, per), pl.ds(0, positions), head_window(c, HEAD_SIZE))
            return [(rotated_key_cache, window), (stored_value_cache, window)]
        return [(w_out, (head_window(c, wide), all_columns))]

    def file_loaded(wanted, arrays):
        arrays = list(arrays)
        for kind, c in wanted:
            loaded[kind, c] = [arrays.pop(0) for _ in windows_of(kind, c)]

    def loads_of(wanted):
        return [pair for kind, c in wanted for pair in windows_of(kind, c)]

    def do_load(token, wanted):
        name = "load" + "".join("_" + kind + str(c) for kind, c in wanted)
        token, arrays, _ = call(lambda: None, name, token, [], [], [], [], 1, loads_of(wanted))
        file_loaded(wanted, arrays)
        return token

    def do_project(token, c, wanted):
        nonlocal inputs
        token, arrays, outs = project(
            token, place, inputs, loaded["weights", c], loads_of(wanted),
            chunk=c, heads=CHUNK_HEADS[c], nz=nz, per=per,
        )
        file_loaded(wanted, arrays)
        kept[c] = outs[0]
        if c == 0:
            inputs = [outs[2]]
        swapped[c] = lax.ppermute(outs[1], "gx", same_z)
        return token

    def do_far(token, c, wanted):
        half = nz // 2
        token, (total,) = add(
            "add_far" + str(c), token, [kept[c], swapped[c]], [half, half], half, 1
        )
        reduced[c] = lax.ppermute(total, "gx", stride_pairs(nz, 1))
        return token

    def do_near(token, c, wanted):
        terms, starts, count = [kept[c], swapped[c], reduced[c]], [0, 0, 0], nz // 2
        for stride in strides(nz)[1:]:
            token, (mine, sent) = add(
                "add_near" + str(c) + "_" + str(stride), token, terms, starts, count, 2
            )
            terms = [mine, lax.ppermute(sent, "gx", stride_pairs(nz, stride))]
            starts, count = [0, 0], count // 2
        reduced[c] = terms
        return token

    def do_attend(token, c, wanted):
        nonlocal scale
        token, arrays, outs = attend(
            token, place, slot_valid_lengths, reduced[c], scale, biases, cos, sin, *loaded["caches", c],
            loads_of(wanted), chunk=c, heads=CHUNK_HEADS[c],
        )
        file_loaded(wanted, arrays)
        if c == 0:
            scale = outs[1]
        if GATHER[c] == "all_gather":
            whole = lax.all_gather(outs[0], "gx", axis=0, tiled=True)
            gathered[c] = [(whole, list(range(2 * nz)))]
            return token
        own = outs[0], [(0, 0)]
        first_move = over_y(*own) if GATHER[c] == "y first" else over_z(*own, strides(nz)[-1])
        waiting[c] = own, first_move
        return token

    def do_gather(token, c, wanted):
        if GATHER[c] == "all_gather":
            return token
        held, moved = waiting[c]
        for stride in reversed(strides(nz) if GATHER[c] == "y first" else strides(nz)[:-1]):
            if GATHER[c] == "y first" and stride == 1:
                break
            token, joined = join("join" + str(c) + "_" + str(stride), token, held[0], moved[0])
            held = joined, held[1] + moved[1]
            moved = over_z(*held, stride)
        waiting[c] = held, moved
        gathered[c] = [held, moved]
        if GATHER[c] == "y halved":
            gathered[c].append(over_y(*held))
        return token

    def do_forward(token, c, wanted):
        if GATHER[c] == "all_gather":
            return token
        held, moved = waiting[c]
        if GATHER[c] == "y halved":
            gathered[c].append(over_y(*moved))
            return token
        token, joined = join("join" + str(c), token, held[0], moved[0])
        held = joined, held[1] + moved[1]
        gathered[c] = [held, over_z(*held, 1) if GATHER[c] == "y first" else over_y(*held)]
        return token

    def do_output(token, c, wanted):
        nonlocal acc
        token, arrays, acc = output(
            token, place, [a for a, _ in gathered[c]], [own for _, own in gathered[c]], sor,
            *loaded["out", c], acc if c == 0 else acc[0], loads_of(wanted),
            chunk=c, chunks=chunks, nz=nz, per=per,
        )
        file_loaded(wanted, arrays)
        return token

    token = jnp.zeros(TOKEN, F32)
    steps = {
        "project": do_project,
        "far": do_far,
        "near": do_near,
        "attend": do_attend,
        "gather": do_gather,
        "forward": do_forward,
        "output": do_output,
    }
    needs = {"project": "weights", "attend": "caches", "output": "out"}
    wanted = []
    for step, c in ORDER:
        if step not in steps:
            wanted.append((step, c))
            continue
        if step not in needs or (needs[step], c) in wanted:
            if wanted:
                token = do_load(token, wanted)
            wanted = []
        token = steps[step](token, c, wanted)
        wanted = []
    mine, send = acc
    received = lax.ppermute(send, "gy", [(0, 1), (1, 0)])
    return (hidden_rows.astype(F32) + mine + received.astype(F32)).astype(BF16)


def solution(mesh):
    in_specs = (
        P(("grp", "gy"), "gx"),
        P("gx"),
        P("gx", "gy"),
        P("gx", "gy"),
        P("gx", "gy"),
        P("gy"),
        P("gy"),
        P("gy"),
        P(("grp", "gx"), None, "gy"),
        P(("grp", "gx"), None, "gy"),
        P("grp"),
        P("grp"),
        P("gy", "gx"),
    )
    out_specs = P(("grp", "gy"), "gx")
    return jax.shard_map(
        functools.partial(on_device, size=mesh.shape["gx"]),
        mesh=mesh,
        in_specs=in_specs,
        out_specs=out_specs,
        check_vma=False,
    )
```

```python
import functools
import math

import jax
import jax.numpy as jnp
from jax import lax
from jax.experimental import pallas as pl
from jax.experimental.pallas import tpu as pltpu
from jax.sharding import PartitionSpec as P

MODEL_WIDTH = 8192
QUERY_HEADS = 64
KEY_VALUE_HEADS = 8
HEAD_SIZE = 128
QUERIES_PER_KV = QUERY_HEADS // KEY_VALUE_HEADS
TILES = QUERIES_PER_KV + 2
SQUARE_ROWS = 32

EPSILON = 1e-06
ROPE_BASE = 1000000.0
CHUNK_HEADS = (1, 2, 1)
F32 = jnp.float32
BF16 = jnp.bfloat16
MIB = 1024 * 1024
SLOTS_AT_ONCE = {1: 24, 2: 8, 3: 8, 4: 4}
PEAK_FLOP_PER_US = 1.1535e9
COSTS = {'attend0': 4, 'output0': 4, 'project1': 1, 'attend1': 8, 'attend2': 1, 'join0_1': 4, 'add_far0': 1, 'add_far2': 1, 'add_near0_2': 1, 'project2': 4, 'join0': 1, 'project0': 1, 'join2': 2}
GATHER = ('y halved', 'y halved', 'y halved')
ORDER = (
    ("weights", 2),
    ("weights", 0),
    ("project", 0),
    ("weights", 1),
    ("caches", 0),
    ("project", 1),
    ("project", 2),
    ("out", 0),
    ("far", 0),
    ("caches", 1),
    ("near", 0),
    ("far", 1),
    ("attend", 0),
    ("far", 2),
    ("near", 1),
    ("gather", 0),
    ("caches", 2),
    ("forward", 0),
    ("near", 2),
    ("out", 2),
    ("attend", 1),
    ("out", 1),
    ("attend", 2),
    ("gather", 1),
    ("output", 0),
    ("gather", 2),
    ("forward", 2),
    ("forward", 1),
    ("output", 1),
    ("output", 2),
)
F32 = jnp.float32
BF16 = jnp.bfloat16


def neighbour_pairs(nz):
    return [(z * 2 + y, z * 2 + 1 - y) for z in range(nz) for y in range(2)]


def stride_pairs(nz, stride):
    return [(z * 2 + y, (z ^ stride) * 2 + y) for z in range(nz) for y in range(2)]


def strides(nz):
    return [1 << i for i in range(nz.bit_length() - 1)]


def place_order(nz):
    return sorted(range(nz), key=lambda q: [(q & b) != 0 for b in strides(nz)])


def slot_one_hot(place_ref, slot_of_row, nz, per, absolute=False):
    rows = slot_of_row.shape[1]
    base = lax.broadcasted_iota(jnp.int32, (per, rows), 0)
    blocks = []
    for h in range(2):
        for q in place_order(nz):
            if absolute:
                owner = len(blocks)
            else:
                owner = (place_ref[0] ^ q) * 2 + (place_ref[1] ^ h)
            blocks.append(jnp.where(base + owner * per == slot_of_row, 1.0, 0.0).astype(F32))
    return jnp.concatenate(blocks, axis=0).astype(BF16)


TOKEN = (8, HEAD_SIZE)


def estimate(name):
    flops = int(COSTS.get(name, 0) * PEAK_FLOP_PER_US)
    return pl.CostEstimate(flops=flops, bytes_accessed=0, transcendentals=0)


def copies_of(sources, windows, targets, sems):
    return [
        pltpu.make_async_copy(source.at[window], target, sems.at[i])
        for i, (source, window, target) in enumerate(zip(sources, windows, targets))
    ]


def call(kernel, name, token, scalars, arrays, out_shapes, scratch, vmem_mib, loads=()):
    sources = [array for array, _ in loads]
    windows = [window for _, window in loads]
    loaded_shapes = [
        tuple(w.size if isinstance(w, pl.Slice) else n for w, n in zip(window, array.shape))
        for array, window in loads
    ]

    def body(*refs):
        refs = list(refs)
        del refs[0]
        source_refs = [refs.pop(0) for _ in loads]
        in_refs = [refs.pop(0) for _ in range(len(scalars) + len(arrays))]
        token_ref = refs.pop(0)
        target_refs = [refs.pop(0) for _ in loads]
        copies = copies_of(source_refs, windows, target_refs, refs.pop() if loads else None)
        for copy in copies:
            copy.start()
        token_ref[...] = jnp.zeros(TOKEN, F32)
        kernel(*in_refs, *refs)
        for copy in copies:
            copy.wait()

    vmem = pl.BlockSpec(memory_space=pltpu.VMEM)
    outs = pl.pallas_call(
        body,
        in_specs=[vmem]
        + [pl.BlockSpec(memory_space=pltpu.HBM)] * len(loads)
        + [pl.BlockSpec(memory_space=pltpu.SMEM)] * len(scalars)
        + [vmem] * len(arrays),
        out_specs=[vmem] * (1 + len(loads) + len(out_shapes)),
        out_shape=[pltpu.VMEM(TOKEN, F32)]
        + [pltpu.VMEM(shape, array.dtype) for shape, array in zip(loaded_shapes, sources)]
        + [pltpu.VMEM(shape, dtype) for shape, dtype in out_shapes],
        scratch_shapes=list(scratch) + ([pltpu.SemaphoreType.DMA((len(loads),))] if loads else []),
        compiler_params=pltpu.CompilerParams(vmem_limit_bytes=vmem_mib * MIB),
        cost_estimate=estimate(name),
        name=name,
    )(
        token,
        *[pltpu.with_memory_space_constraint(array, pltpu.HBM) for array in sources],
        *scalars,
        *arrays,
    )
    return outs[0], outs[1 : 1 + len(loads)], outs[1 + len(loads) :]


def project_kernel(*refs, nz, per, first, heads):
    place_ref = refs[0]
    if first:
        own_ref, other_ref, gain_ref, sor_ref, wq_ref, wk_ref, wv_ref = refs[1:8]
        *out_refs, slotted_ref, acc = refs[8:]
        one_hot = slot_one_hot(place_ref, sor_ref[...], nz, per)
        own, other = own_ref[...], other_ref[...]
        lower = place_ref[2] == 0
        rows = jnp.concatenate(
            [jnp.where(lower, own, other), jnp.where(lower, other, own)], axis=0
        )
        hidden = jnp.dot(one_hot, rows, preferred_element_type=F32)
        gain = gain_ref[...].astype(F32)
        gain = jnp.concatenate([gain[j : j + 1] for j in range(gain.shape[0])], axis=1)
        slotted_ref[...] = (hidden * gain).astype(BF16)
        squares = jnp.sum(hidden * hidden, axis=1, keepdims=True)
        high = squares.astype(BF16).astype(F32)
        low = squares - high
        lane = lax.broadcasted_iota(jnp.int32, (per, HEAD_SIZE), 1)
        lane_high = place_ref[1] * 2
        for b, ref in enumerate(out_refs):
            for z in range(nz):
                at = (b * nz + z) * per
                packed = jnp.where(
                    lane == lane_high,
                    high[at : at + per],
                    jnp.where(lane == lane_high + 1, low[at : at + per], 0.0),
                )
                packed = jnp.concatenate(
                    [packed, jnp.zeros((SQUARE_ROWS - per, HEAD_SIZE), F32)], axis=0
                )
                ref[z, heads * TILES * per :, :] = packed.astype(BF16)
    else:
        slotted_ref, wq_ref, wk_ref, wv_ref = refs[1:5]
        *out_refs, acc = refs[5:]

    columns = QUERIES_PER_KV * HEAD_SIZE
    slotted = slotted_ref[...]
    for g in range(heads):
        acc[:, :columns] = jnp.dot(
            slotted, wq_ref[:, g * columns : (g + 1) * columns], preferred_element_type=F32
        )
        narrow = slice(g * HEAD_SIZE, (g + 1) * HEAD_SIZE)
        acc[:, columns:] = jnp.dot(
            slotted,
            jnp.concatenate([wk_ref[:, narrow], wv_ref[:, narrow]], axis=1),
            preferred_element_type=F32,
        )
        for b, ref in enumerate(out_refs):
            for z in range(nz):
                at = (b * nz + z) * per
                block = jnp.concatenate(
                    [
                        acc[at : at + per, c * HEAD_SIZE : (c + 1) * HEAD_SIZE]
                        for c in range(TILES)
                    ],
                    axis=0,
                )
                ref[z, g * TILES * per : (g + 1) * TILES * per, :] = block.astype(BF16)


def project(token, place, inputs, weights, loads, *, chunk, heads, nz, per):
    first = chunk == 0
    rows = 2 * nz * per
    depth = weights[0].shape[0]
    block_rows = heads * TILES * per + (SQUARE_ROWS if first else 0)
    out_shapes = [((nz, block_rows, HEAD_SIZE), BF16)] * 2
    return call(
        functools.partial(project_kernel, nz=nz, per=per, first=first, heads=heads),
        "project" + str(chunk),
        token,
        [place],
        [*inputs, *weights],
        out_shapes + ([((rows, depth), BF16)] if first else []),
        [pltpu.VMEM((rows, TILES * HEAD_SIZE), F32)],
        12,
        loads,
    )


def add_kernel(*refs, starts, count):
    terms = len(starts)
    outs = refs[terms:]
    each = outs[0].shape[0]
    for z in range(count):
        total = refs[0][starts[0] + z].astype(F32)
        for ref, start in zip(refs[1:terms], starts[1:]):
            total = total + ref[start + z].astype(F32)
        outs[z // each][z % each] = total.astype(BF16)


def add(name, token, arrays, starts, count, parts):
    shape = (count // parts,) + arrays[0].shape[1:]
    token, _, sums = call(
        functools.partial(add_kernel, starts=starts, count=count),
        name,
        token,
        [],
        arrays,
        [(shape, BF16)] * parts,
        [],
        2,
    )
    return token, sums


def join_kernel(a_ref, b_ref, out_ref):
    count = a_ref.shape[0]
    out_ref[:count] = a_ref[...]
    out_ref[count:] = b_ref[...]


def join(name, token, a, b):
    shape = (a.shape[0] + b.shape[0],) + a.shape[1:]
    token, _, (joined,) = call(join_kernel, name, token, [], [a, b], [(shape, BF16)], [], 2)
    return token, joined


def attend_kernel(*refs, first, heads, per, group, start_head):
    place_ref, lengths_ref, mine_ref, last_ref = refs[:4]
    rest = refs[4:]
    if first:
        qb_ref, kb_ref, vb_ref, cos_ref, sin_ref, k_ref, v_ref, out_ref, scale_ref = rest[:9]
    else:
        scale_in_ref, qb_ref, kb_ref, vb_ref, cos_ref, sin_ref, k_ref, v_ref, out_ref = rest[:9]
    fresh, result = rest[9:]
    body = heads * TILES * per
    head_rows = TILES * per

    if first:
        squares = mine_ref[0, body:, :].astype(F32) + last_ref[0, body:, :].astype(F32)
        total = jnp.sum(squares[:per], axis=1, keepdims=True)
        scale = jnp.broadcast_to(lax.rsqrt(total / MODEL_WIDTH + EPSILON), (per, HEAD_SIZE))
        scale_ref[...] = scale
    else:
        scale = scale_in_ref[...]
    cos, sin = cos_ref[...], sin_ref[...]
    query_bias = qb_ref[...].astype(F32)
    key_bias = kb_ref[...].astype(F32)
    value_bias = vb_ref[...].astype(F32)
    for g in range(heads):
        rows = pl.ds(g * head_rows, head_rows)
        summed = mine_ref[0, rows, :].astype(F32) + last_ref[0, rows, :].astype(F32)
        head = start_head + g
        for c in range(TILES):
            if c < QUERIES_PER_KV:
                at = head * QUERIES_PER_KV + c
                bias = query_bias[at : at + 1]
            else:
                bias = (key_bias if c == QUERIES_PER_KV else value_bias)[head : head + 1]
            tile = summed[c * per : (c + 1) * per] * scale + bias
            if c < TILES - 1:
                tile = tile * cos + pltpu.roll(tile, HEAD_SIZE // 2, 1) * sin
            fresh[pl.ds(g * head_rows + c * per, per), :] = tile.astype(BF16).astype(F32)

    positions = k_ref.shape[1]
    qrows = heads * QUERIES_PER_KV
    lanes = group * qrows
    extra = 16
    lane_block = lax.broadcasted_iota(jnp.int32, (HEAD_SIZE, lanes), 1) // QUERIES_PER_KV
    top_row = lax.broadcasted_iota(jnp.int32, (extra, HEAD_SIZE), 0) == 0
    lane_slot = lax.broadcasted_iota(jnp.int32, (1, lanes), 1) // qrows
    row = lax.broadcasted_iota(jnp.int32, (positions + extra, lanes), 0)
    row_slot = lax.broadcasted_iota(jnp.int32, (lanes, positions), 0) // qrows
    base = (place_ref[0] * 2 + place_ref[1]) * per
    for start in range(0, per, group):
        slots = range(start, start + group)
        queries = jnp.concatenate(
            [
                fresh[pl.ds(g * head_rows + s, QUERIES_PER_KV, stride=per), :]
                for s in slots
                for g in range(heads)
            ],
            axis=0,
        )
        turned = queries.T
        query, new_key = [], []
        for i, s in enumerate(slots):
            for g in range(heads):
                query.append(jnp.where(lane_block == i * heads + g, turned, 0.0).astype(BF16))
                key = fresh[pl.ds(g * head_rows + QUERIES_PER_KV * per + s, 1), :]
                new_key.append(jnp.where(top_row, key, 0.0).astype(BF16))
        keys = jnp.concatenate(
            [
                jnp.concatenate([k_ref[s] for s in slots], axis=1),
                jnp.concatenate(new_key, axis=1),
            ],
            axis=0,
        )
        scores = jnp.dot(keys, jnp.concatenate(query, axis=0), preferred_element_type=F32)

        lengths = jnp.zeros((1, lanes), jnp.int32)
        for i, s in enumerate(slots):
            lengths = jnp.where(lane_slot == i, lengths_ref[base + s], lengths)
        valid = (row < lengths) | (row == positions)
        scores = jnp.where(valid, scores * (1.0 / math.sqrt(HEAD_SIZE)), -1e30)
        top = jnp.max(scores, axis=0, keepdims=True)
        exps = jnp.where(valid, jnp.exp(scores - top), 0.0)
        weights = exps * (1.0 / jnp.sum(exps, axis=0, keepdims=True))
        cache_weights = weights[:positions].T
        own_weights = weights[positions : positions + 8].T[:, 0:1].astype(BF16).astype(F32)
        spread = jnp.concatenate(
            [jnp.where(row_slot == i, cache_weights, 0.0).astype(BF16) for i in range(group)],
            axis=1,
        )
        values = v_ref[start : start + group].reshape(group * positions, heads * HEAD_SIZE)
        mixed = jnp.dot(spread, values, preferred_element_type=F32)
        for i, s in enumerate(slots):
            for g in range(heads):
                lo = i * qrows + g * QUERIES_PER_KV
                hi = lo + QUERIES_PER_KV
                new_value = fresh[pl.ds(g * head_rows + (QUERIES_PER_KV + 1) * per + s, 1), :]
                result[pl.ds(g * QUERIES_PER_KV * per + s, QUERIES_PER_KV, stride=per), :] = (
                    mixed[lo:hi, g * HEAD_SIZE : (g + 1) * HEAD_SIZE]
                    + own_weights[lo:hi] * new_value
                )
    out_ref[0] = result[...].astype(BF16)


def attend(
    token, place, lengths, parts, scale, biases, cos, sin, keys, values, loads, *, chunk, heads
):
    first = chunk == 0
    per = keys.shape[0]
    out_rows = heads * QUERIES_PER_KV * per
    return call(
        functools.partial(
            attend_kernel,
            first=first,
            heads=heads,
            per=per,
            group=SLOTS_AT_ONCE[heads],
            start_head=sum(CHUNK_HEADS[:chunk]),
        ),
        "attend" + str(chunk),
        token,
        [place, lengths],
        list(parts) + ([] if first else [scale]) + list(biases) + [cos, sin, keys, values],
        [((1, out_rows, HEAD_SIZE), BF16)] + ([((per, HEAD_SIZE), F32)] if first else []),
        [
            pltpu.VMEM((heads * TILES * per, HEAD_SIZE), F32),
            pltpu.VMEM((out_rows, HEAD_SIZE), F32),
        ],
        8,
        loads,
    )


def output_kernel(*refs, labels, nz, per, first, last, absolute):
    count = len(labels)
    place_ref, block_refs, sor_ref, w_ref = refs[0], refs[1 : 1 + count], refs[1 + count], refs[2 + count]
    rest = refs[3 + count :]
    if not first:
        acc_in_ref, rest = rest[0], rest[1:]
    if last:
        mine_ref, send_ref, stacked = rest
    else:
        acc_out_ref, stacked = rest
    tiles = block_refs[0].shape[1] // per

    half = sor_ref.shape[1] // 2
    slot_of_row = sor_ref[...]
    swapped = jnp.concatenate([slot_of_row[:, half:], slot_of_row[:, :half]], axis=1)
    slot_of_row = jnp.where(place_ref[2] == 0, slot_of_row, swapped)
    one_hot = slot_one_hot(place_ref, slot_of_row, nz, per, absolute)
    wide = {
        label: ref[z].astype(F32)
        for ref, own in zip(block_refs, labels)
        for z, label in enumerate(own)
    }
    if absolute:
        wide = [wide[owner] for owner in range(2 * nz)]
    else:
        wide = [wide[h, q] for h in range(2) for q in place_order(nz)]
    for c in range(tiles):
        stacked[:, c * HEAD_SIZE : (c + 1) * HEAD_SIZE] = jnp.concatenate(
            [block[c * per : (c + 1) * per] for block in wide], axis=0
        ).astype(BF16)
    permuted = lax.dot_general(
        one_hot, stacked[...], (((0,), (0,)), ((), ())), preferred_element_type=F32
    ).astype(BF16)
    stacked[...] = permuted
    product = jnp.dot(stacked[...], w_ref[...], preferred_element_type=F32)
    if not first:
        product = product + acc_in_ref[...]
    if last:
        mine_ref[...] = product[:half]
        send_ref[...] = product[half:].astype(BF16)
    else:
        acc_out_ref[...] = product


def output(token, place, blocks, labels, sor, w_out, acc, loads, *, chunk, chunks, nz, per):
    first, last = chunk == 0, chunk == chunks - 1
    rows = 2 * nz * per
    depth, width = w_out.shape
    if last:
        out_shapes = [((rows // 2, width), F32), ((rows // 2, width), BF16)]
    else:
        out_shapes = [((rows, width), F32)]
    return call(
        functools.partial(
            output_kernel,
            labels=labels,
            nz=nz,
            per=per,
            first=first,
            last=last,
            absolute=GATHER[chunk] == "all_gather",
        ),
        "output" + str(chunk),
        token,
        [place],
        [*blocks, sor, w_out] + ([] if first else [acc]),
        out_shapes,
        [pltpu.VMEM((rows, depth), BF16)],
        12,
        loads,
    )


def on_device(
    hidden_rows,
    norm_gain,
    w_query,
    key_weight,
    value_weight,
    query_bias,
    key_bias_vector,
    value_bias_vector,
    rotated_key_cache,
    stored_value_cache,
    slot_valid_lengths,
    slot_of_row,
    w_out,
    *,
    size,
):
    nz = size // 2
    assert size % 2 == 0 and nz & (nz - 1) == 0 and nz > 2
    per = rotated_key_cache.shape[0]
    kv_heads = key_weight.shape[1] // HEAD_SIZE
    assert sum(CHUNK_HEADS) == kv_heads and per == SLOTS_AT_ONCE[1]
    chunks = len(CHUNK_HEADS)
    gx = lax.axis_index("gx")
    gy = lax.axis_index("gy")
    place = jnp.stack([gx // 2, gx % 2, gy]).astype(jnp.int32)

    other = lax.ppermute(hidden_rows, "gy", [(0, 1), (1, 0)])
    sor = slot_of_row[None, :]
    gain = norm_gain.reshape(-1, HEAD_SIZE)

    lengths = lax.dynamic_slice_in_dim(slot_valid_lengths, gx * per, per, 0)
    lane = jnp.arange(HEAD_SIZE)
    half_width = HEAD_SIZE // 2
    frequency = ROPE_BASE ** (-((lane % half_width).astype(F32) * 2.0 / HEAD_SIZE))
    angles = lengths.astype(F32)[:, None] * frequency[None, :]
    cos = jnp.cos(angles)
    sin = jnp.sin(angles) * jnp.where(lane < half_width, -1.0, 1.0)[None, :]
    biases = [b.reshape(-1, HEAD_SIZE) for b in (query_bias, key_bias_vector, value_bias_vector)]

    def head_window(c, width):
        return pl.ds(sum(CHUNK_HEADS[:c]) * width, CHUNK_HEADS[c] * width)

    wide = QUERIES_PER_KV * HEAD_SIZE
    everything = pl.ds(0, w_query.shape[0])
    positions = rotated_key_cache.shape[1]
    all_columns = pl.ds(0, w_out.shape[1])
    same_z = neighbour_pairs(nz)
    scale = acc = None
    inputs = [hidden_rows, other, gain, sor]
    kept, swapped, reduced = {}, {}, {}
    loaded, gathered, waiting = {}, {}, {}

    def over_y(blocks, labels):
        return lax.ppermute(blocks, "gx", same_z), [(1 - h, q) for h, q in labels]

    def over_z(blocks, labels, stride):
        moved = lax.ppermute(blocks, "gx", stride_pairs(nz, stride))
        return moved, [(h, q ^ stride) for h, q in labels]

    def windows_of(kind, c):
        if kind == "weights":
            return [
                (array, (everything, head_window(c, n)))
                for array, n in (
                    (w_query, wide), (key_weight, HEAD_SIZE), (value_weight, HEAD_SIZE),
                )
            ]
        if kind == "caches":
            window = (pl.ds(0, per), pl.ds(0, positions), head_window(c, HEAD_SIZE))
            return [(rotated_key_cache, window), (stored_value_cache, window)]
        return [(w_out, (head_window(c, wide), all_columns))]

    def file_loaded(wanted, arrays):
        arrays = list(arrays)
        for kind, c in wanted:
            loaded[kind, c] = [arrays.pop(0) for _ in windows_of(kind, c)]

    def loads_of(wanted):
        return [pair for kind, c in wanted for pair in windows_of(kind, c)]

    def do_load(token, wanted):
        name = "load" + "".join("_" + kind + str(c) for kind, c in wanted)
        token, arrays, _ = call(lambda: None, name, token, [], [], [], [], 1, loads_of(wanted))
        file_loaded(wanted, arrays)
        return token

    def do_project(token, c, wanted):
        nonlocal inputs
        token, arrays, outs = project(
            token, place, inputs, loaded["weights", c], loads_of(wanted),
            chunk=c, heads=CHUNK_HEADS[c], nz=nz, per=per,
        )
        file_loaded(wanted, arrays)
        kept[c] = outs[0]
        if c == 0:
            inputs = [outs[2]]
        swapped[c] = lax.ppermute(outs[1], "gx", same_z)
        return token

    def do_far(token, c, wanted):
        half = nz // 2
        token, (total,) = add(
            "add_far" + str(c), token, [kept[c], swapped[c]], [half, half], half, 1
        )
        reduced[c] = lax.ppermute(total, "gx", stride_pairs(nz, 1))
        return token

    def do_near(token, c, wanted):
        terms, starts, count = [kept[c], swapped[c], reduced[c]], [0, 0, 0], nz // 2
        for stride in strides(nz)[1:]:
            token, (mine, sent) = add(
                "add_near" + str(c) + "_" + str(stride), token, terms, starts, count, 2
            )
            terms = [mine, lax.ppermute(sent, "gx", stride_pairs(nz, stride))]
            starts, count = [0, 0], count // 2
        reduced[c] = terms
        return token

    def do_attend(token, c, wanted):
        nonlocal scale
        token, arrays, outs = attend(
            token, place, slot_valid_lengths, reduced[c], scale, biases, cos, sin, *loaded["caches", c],
            loads_of(wanted), chunk=c, heads=CHUNK_HEADS[c],
        )
        file_loaded(wanted, arrays)
        if c == 0:
            scale = outs[1]
        if GATHER[c] == "all_gather":
            whole = lax.all_gather(outs[0], "gx", axis=0, tiled=True)
            gathered[c] = [(whole, list(range(2 * nz)))]
            return token
        own = outs[0], [(0, 0)]
        first_move = over_y(*own) if GATHER[c] == "y first" else over_z(*own, strides(nz)[-1])
        waiting[c] = own, first_move
        return token

    def do_gather(token, c, wanted):
        if GATHER[c] == "all_gather":
            return token
        held, moved = waiting[c]
        for stride in reversed(strides(nz) if GATHER[c] == "y first" else strides(nz)[:-1]):
            if GATHER[c] == "y first" and stride == 1:
                break
            token, joined = join("join" + str(c) + "_" + str(stride), token, held[0], moved[0])
            held = joined, held[1] + moved[1]
            moved = over_z(*held, stride)
        waiting[c] = held, moved
        gathered[c] = [held, moved]
        if GATHER[c] == "y halved":
            gathered[c].append(over_y(*held))
        return token

    def do_forward(token, c, wanted):
        if GATHER[c] == "all_gather":
            return token
        held, moved = waiting[c]
        if GATHER[c] == "y halved":
            gathered[c].append(over_y(*moved))
            return token
        token, joined = join("join" + str(c), token, held[0], moved[0])
        held = joined, held[1] + moved[1]
        gathered[c] = [held, over_z(*held, 1) if GATHER[c] == "y first" else over_y(*held)]
        return token

    def do_output(token, c, wanted):
        nonlocal acc
        token, arrays, acc = output(
            token, place, [a for a, _ in gathered[c]], [own for _, own in gathered[c]], sor,
            *loaded["out", c], acc if c == 0 else acc[0], loads_of(wanted),
            chunk=c, chunks=chunks, nz=nz, per=per,
        )
        file_loaded(wanted, arrays)
        return token

    token = jnp.zeros(TOKEN, F32)
    steps = {
        "project": do_project,
        "far": do_far,
        "near": do_near,
        "attend": do_attend,
        "gather": do_gather,
        "forward": do_forward,
        "output": do_output,
    }
    needs = {"project": "weights", "attend": "caches", "output": "out"}
    wanted = []
    for step, c in ORDER:
        if step not in steps:
            wanted.append((step, c))
            continue
        if step not in needs or (needs[step], c) in wanted:
            if wanted:
                token = do_load(token, wanted)
            wanted = []
        token = steps[step](token, c, wanted)
        wanted = []
    mine, send = acc
    received = lax.ppermute(send, "gy", [(0, 1), (1, 0)])
    return (hidden_rows.astype(F32) + mine + received.astype(F32)).astype(BF16)


def solution(mesh):
    in_specs = (
        P(("grp", "gy"), "gx"),
        P("gx"),
        P("gx", "gy"),
        P("gx", "gy"),
        P("gx", "gy"),
        P("gy"),
        P("gy"),
        P("gy"),
        P(("grp", "gx"), None, "gy"),
        P(("grp", "gx"), None, "gy"),
        P("grp"),
        P("grp"),
        P("gy", "gx"),
    )
    out_specs = P(("grp", "gy"), "gx")
    return jax.shard_map(
        functools.partial(on_device, size=mesh.shape["gx"]),
        mesh=mesh,
        in_specs=in_specs,
        out_specs=out_specs,
        check_vma=False,
    )
```

```python
import functools
import math

import jax
import jax.numpy as jnp
from jax import lax
from jax.experimental import pallas as pl
from jax.experimental.pallas import tpu as pltpu
from jax.sharding import PartitionSpec as P

MODEL_WIDTH = 8192
QUERY_HEADS = 64
KEY_VALUE_HEADS = 8
HEAD_SIZE = 128
QUERIES_PER_KV = QUERY_HEADS // KEY_VALUE_HEADS
TILES = QUERIES_PER_KV + 2
SQUARE_ROWS = 32

EPSILON = 1e-06
ROPE_BASE = 1000000.0
CHUNK_HEADS = (1, 2, 1)
F32 = jnp.float32
BF16 = jnp.bfloat16
MIB = 1024 * 1024
SLOTS_AT_ONCE = {1: 24, 2: 8, 3: 8, 4: 4}
PEAK_FLOP_PER_US = 1.1535e9
COSTS = {'project0': 1.22, 'add_far0': 0.1, 'add_near0_2': 0.1, 'attend0': 1.9, 'join0_1': 0.1, 'join0': 0.1, 'output0': 1.4, 'project1': 1.8, 'add_far1': 0.1, 'add_near1_2': 0.1, 'attend1': 2.35, 'join1_1': 0.1, 'join1': 0.1, 'output1': 2, 'project2': 1.22, 'add_far2': 0.1, 'add_near2_2': 0.1, 'attend2': 1.9, 'join2': 0.1, 'output2': 4}
Y_IN_HALVES = (True, True, True)
GATHER = ('y halved', 'y halved', 'y halved')
ORDER = (
    ("weights", 0),
    ("weights", 1),
    ("project", 0),
    ("project", 1),
    ("far", 0),
    ("weights", 2),
    ("far", 1),
    ("near", 0),
    ("project", 2),
    ("near", 1),
    ("far", 2),
    ("attend", 0),
    ("attend", 1),
    ("near", 2),
    ("gather", 0),
    ("gather", 1),
    ("attend", 2),
    ("forward", 1),
    ("forward", 0),
    ("output", 0),
    ("gather", 2),
    ("forward", 2),
    ("output", 1),
    ("output", 2),
)
F32 = jnp.float32
BF16 = jnp.bfloat16


def neighbour_pairs(nz):
    return [(z * 2 + y, z * 2 + 1 - y) for z in range(nz) for y in range(2)]


def stride_pairs(nz, stride):
    return [(z * 2 + y, (z ^ stride) * 2 + y) for z in range(nz) for y in range(2)]


def strides(nz):
    return [1 << i for i in range(nz.bit_length() - 1)]


def place_order(nz):
    return sorted(range(nz), key=lambda q: [(q & b) != 0 for b in strides(nz)])


def slot_one_hot(place_ref, slot_of_row, nz, per):
    rows = slot_of_row.shape[1]
    base = lax.broadcasted_iota(jnp.int32, (per, rows), 0)
    blocks = []
    for h in range(2):
        for q in place_order(nz):
            owner = (place_ref[0] ^ q) * 2 + (place_ref[1] ^ h)
            blocks.append(jnp.where(base + owner * per == slot_of_row, 1.0, 0.0).astype(F32))
    return jnp.concatenate(blocks, axis=0).astype(BF16)


TOKEN = (8, HEAD_SIZE)


def estimate(name):
    flops = int(COSTS.get(name, 0) * PEAK_FLOP_PER_US)
    return pl.CostEstimate(flops=flops, bytes_accessed=0, transcendentals=0)


def copies_of(sources, windows, targets, sems):
    return [
        pltpu.make_async_copy(source.at[window], target, sems.at[i])
        for i, (source, window, target) in enumerate(zip(sources, windows, targets))
    ]


def call(
    kernel, name, token, scalars, arrays, out_shapes, scratch, vmem_mib, loads=(), resident=()
):
    arrays = list(arrays) + [
        pltpu.with_memory_space_constraint(array, pltpu.VMEM) for array in resident
    ]
    sources = [array for array, _ in loads]
    windows = [window for _, window in loads]
    loaded_shapes = [
        tuple(w.size if isinstance(w, pl.Slice) else n for w, n in zip(window, array.shape))
        for array, window in loads
    ]

    def body(*refs):
        refs = list(refs)
        del refs[0]
        source_refs = [refs.pop(0) for _ in loads]
        in_refs = [refs.pop(0) for _ in range(len(scalars) + len(arrays))]
        token_ref = refs.pop(0)
        target_refs = [refs.pop(0) for _ in loads]
        copies = copies_of(source_refs, windows, target_refs, refs.pop() if loads else None)
        for copy in copies:
            copy.start()
        token_ref[...] = jnp.zeros(TOKEN, F32)
        kernel(*in_refs, *refs)
        for copy in copies:
            copy.wait()

    vmem = pl.BlockSpec(memory_space=pltpu.VMEM)
    outs = pl.pallas_call(
        body,
        in_specs=[vmem]
        + [pl.BlockSpec(memory_space=pltpu.HBM)] * len(loads)
        + [pl.BlockSpec(memory_space=pltpu.SMEM)] * len(scalars)
        + [vmem] * len(arrays),
        out_specs=[vmem] * (1 + len(loads) + len(out_shapes)),
        out_shape=[pltpu.VMEM(TOKEN, F32)]
        + [pltpu.VMEM(shape, array.dtype) for shape, array in zip(loaded_shapes, sources)]
        + [pltpu.VMEM(shape, dtype) for shape, dtype in out_shapes],
        scratch_shapes=list(scratch) + ([pltpu.SemaphoreType.DMA((len(loads),))] if loads else []),
        compiler_params=pltpu.CompilerParams(vmem_limit_bytes=vmem_mib * MIB),
        cost_estimate=estimate(name),
        name=name,
    )(
        token,
        *[pltpu.with_memory_space_constraint(array, pltpu.HBM) for array in sources],
        *scalars,
        *arrays,
    )
    return outs[0], outs[1 : 1 + len(loads)], outs[1 + len(loads) :]


def places_of(refs, per):
    blocks = [(ref, z) for ref in refs for z in range(ref.shape[0])]
    return [(i * per, ref, z) for i, (ref, z) in enumerate(blocks)]


def project_kernel(*refs, nz, per, first, heads):
    place_ref = refs[0]
    if first:
        own_ref, other_ref, gain_ref, sor_ref, wq_ref, wk_ref, wv_ref = refs[1:8]
        *out_refs, slotted_ref, acc = refs[8:]
        places = places_of(out_refs, per)
        one_hot = slot_one_hot(place_ref, sor_ref[...], nz, per)
        own, other = own_ref[...], other_ref[...]
        lower = place_ref[2] == 0
        rows = jnp.concatenate(
            [jnp.where(lower, own, other), jnp.where(lower, other, own)], axis=0
        )
        hidden = jnp.dot(one_hot, rows, preferred_element_type=F32)
        gain = gain_ref[...].astype(F32)
        gain = jnp.concatenate([gain[j : j + 1] for j in range(gain.shape[0])], axis=1)
        slotted_ref[...] = (hidden * gain).astype(BF16)
        squares = jnp.sum(hidden * hidden, axis=1, keepdims=True)
        high = squares.astype(BF16).astype(F32)
        low = squares - high
        lane = lax.broadcasted_iota(jnp.int32, (per, HEAD_SIZE), 1)
        lane_high = place_ref[1] * 2
        for at, ref, z in places:
            packed = jnp.where(
                lane == lane_high,
                high[at : at + per],
                jnp.where(lane == lane_high + 1, low[at : at + per], 0.0),
            )
            packed = jnp.concatenate(
                [packed, jnp.zeros((SQUARE_ROWS - per, HEAD_SIZE), F32)], axis=0
            )
            ref[z, heads * TILES * per :, :] = packed.astype(BF16)
    else:
        slotted_ref, wq_ref, wk_ref, wv_ref = refs[1:5]
        *out_refs, acc = refs[5:]
        places = places_of(out_refs, per)

    columns = QUERIES_PER_KV * HEAD_SIZE
    slotted = slotted_ref[...]
    for g in range(heads):
        acc[:, :columns] = jnp.dot(
            slotted, wq_ref[:, g * columns : (g + 1) * columns], preferred_element_type=F32
        )
        narrow = slice(g * HEAD_SIZE, (g + 1) * HEAD_SIZE)
        acc[:, columns:] = jnp.dot(
            slotted,
            jnp.concatenate([wk_ref[:, narrow], wv_ref[:, narrow]], axis=1),
            preferred_element_type=F32,
        )
        for at, ref, z in places:
            block = jnp.concatenate(
                [
                    acc[at : at + per, c * HEAD_SIZE : (c + 1) * HEAD_SIZE]
                    for c in range(TILES)
                ],
                axis=0,
            )
            ref[z, g * TILES * per : (g + 1) * TILES * per, :] = block.astype(BF16)


def project(token, place, inputs, weights, loads, *, chunk, heads, nz, per):
    first = chunk == 0
    rows = 2 * nz * per
    depth = weights[0].shape[0]
    block_rows = heads * TILES * per + (SQUARE_ROWS if first else 0)
    counts = [nz, nz // 2, nz // 2] if Y_IN_HALVES[chunk] else [nz, nz]
    out_shapes = [((count, block_rows, HEAD_SIZE), BF16) for count in counts]
    return call(
        functools.partial(project_kernel, nz=nz, per=per, first=first, heads=heads),
        "project" + str(chunk),
        token,
        [place],
        [*inputs, *weights],
        out_shapes + ([((rows, depth), BF16)] if first else []),
        [pltpu.VMEM((rows, TILES * HEAD_SIZE), F32)],
        12,
        loads,
    )


def add_kernel(*refs, starts, count):
    terms = len(starts)
    outs = refs[terms:]
    each = outs[0].shape[0]
    for z in range(count):
        total = refs[0][starts[0] + z].astype(F32)
        for ref, start in zip(refs[1:terms], starts[1:]):
            total = total + ref[start + z].astype(F32)
        outs[z // each][z % each] = total.astype(BF16)


def add(name, token, arrays, starts, count, parts):
    shape = (count // parts,) + arrays[0].shape[1:]
    token, _, sums = call(
        functools.partial(add_kernel, starts=starts, count=count),
        name,
        token,
        [],
        arrays,
        [(shape, BF16)] * parts,
        [],
        2,
    )
    return token, sums


def join_kernel(a_ref, b_ref, out_ref):
    count = a_ref.shape[0]
    out_ref[:count] = a_ref[...]
    out_ref[count:] = b_ref[...]


def join(name, token, a, b):
    shape = (a.shape[0] + b.shape[0],) + a.shape[1:]
    token, _, (joined,) = call(join_kernel, name, token, [], [a, b], [(shape, BF16)], [], 2)
    return token, joined


def attend_kernel(*refs, first, heads, per, group, start_head):
    place_ref, lengths_ref, mine_ref, last_ref = refs[:4]
    rest = refs[4:]
    if first:
        qb_ref, kb_ref, vb_ref, cos_ref, sin_ref, k_ref, v_ref, out_ref, scale_ref = rest[:9]
    else:
        scale_in_ref, qb_ref, kb_ref, vb_ref, cos_ref, sin_ref, k_ref, v_ref, out_ref = rest[:9]
    fresh, result = rest[9:]
    body = heads * TILES * per
    head_rows = TILES * per

    if first:
        squares = mine_ref[0, body:, :].astype(F32) + last_ref[0, body:, :].astype(F32)
        total = jnp.sum(squares[:per], axis=1, keepdims=True)
        scale = jnp.broadcast_to(lax.rsqrt(total / MODEL_WIDTH + EPSILON), (per, HEAD_SIZE))
        scale_ref[...] = scale
    else:
        scale = scale_in_ref[...]
    cos, sin = cos_ref[...], sin_ref[...]
    query_bias = qb_ref[...].astype(F32)
    key_bias = kb_ref[...].astype(F32)
    value_bias = vb_ref[...].astype(F32)
    for g in range(heads):
        rows = pl.ds(g * head_rows, head_rows)
        summed = mine_ref[0, rows, :].astype(F32) + last_ref[0, rows, :].astype(F32)
        head = start_head + g
        for c in range(TILES):
            if c < QUERIES_PER_KV:
                at = head * QUERIES_PER_KV + c
                bias = query_bias[at : at + 1]
            else:
                bias = (key_bias if c == QUERIES_PER_KV else value_bias)[head : head + 1]
            tile = summed[c * per : (c + 1) * per] * scale + bias
            if c < TILES - 1:
                tile = tile * cos + pltpu.roll(tile, HEAD_SIZE // 2, 1) * sin
            fresh[pl.ds(g * head_rows + c * per, per), :] = tile.astype(BF16).astype(F32)

    positions = k_ref.shape[1]
    columns = slice(start_head * HEAD_SIZE, (start_head + heads) * HEAD_SIZE)
    qrows = heads * QUERIES_PER_KV
    lanes = group * qrows
    extra = 16
    lane_block = lax.broadcasted_iota(jnp.int32, (HEAD_SIZE, lanes), 1) // QUERIES_PER_KV
    top_row = lax.broadcasted_iota(jnp.int32, (extra, HEAD_SIZE), 0) == 0
    lane_slot = lax.broadcasted_iota(jnp.int32, (1, lanes), 1) // qrows
    row = lax.broadcasted_iota(jnp.int32, (positions + extra, lanes), 0)
    row_slot = lax.broadcasted_iota(jnp.int32, (lanes, positions), 0) // qrows
    base = (place_ref[0] * 2 + place_ref[1]) * per
    for start in range(0, per, group):
        slots = range(start, start + group)
        queries = jnp.concatenate(
            [
                fresh[pl.ds(g * head_rows + s, QUERIES_PER_KV, stride=per), :]
                for s in slots
                for g in range(heads)
            ],
            axis=0,
        )
        turned = queries.T
        query, new_key = [], []
        for i, s in enumerate(slots):
            for g in range(heads):
                query.append(jnp.where(lane_block == i * heads + g, turned, 0.0).astype(BF16))
                key = fresh[pl.ds(g * head_rows + QUERIES_PER_KV * per + s, 1), :]
                new_key.append(jnp.where(top_row, key, 0.0).astype(BF16))
        keys = jnp.concatenate(
            [
                jnp.concatenate([k_ref[s, :, columns] for s in slots], axis=1),
                jnp.concatenate(new_key, axis=1),
            ],
            axis=0,
        )
        scores = jnp.dot(keys, jnp.concatenate(query, axis=0), preferred_element_type=F32)

        lengths = jnp.zeros((1, lanes), jnp.int32)
        for i, s in enumerate(slots):
            lengths = jnp.where(lane_slot == i, lengths_ref[base + s], lengths)
        valid = (row < lengths) | (row == positions)
        scores = jnp.where(valid, scores * (1.0 / math.sqrt(HEAD_SIZE)), -1e30)
        top = jnp.max(scores, axis=0, keepdims=True)
        exps = jnp.where(valid, jnp.exp(scores - top), 0.0)
        weights = exps * (1.0 / jnp.sum(exps, axis=0, keepdims=True))
        cache_weights = weights[:positions].T
        own_weights = weights[positions : positions + 8].T[:, 0:1].astype(BF16).astype(F32)
        spread = jnp.concatenate(
            [jnp.where(row_slot == i, cache_weights, 0.0).astype(BF16) for i in range(group)],
            axis=1,
        )
        values = v_ref[start : start + group, :, columns].reshape(group * positions, heads * HEAD_SIZE)
        mixed = jnp.dot(spread, values, preferred_element_type=F32)
        for i, s in enumerate(slots):
            for g in range(heads):
                lo = i * qrows + g * QUERIES_PER_KV
                hi = lo + QUERIES_PER_KV
                new_value = fresh[pl.ds(g * head_rows + (QUERIES_PER_KV + 1) * per + s, 1), :]
                result[pl.ds(g * QUERIES_PER_KV * per + s, QUERIES_PER_KV, stride=per), :] = (
                    mixed[lo:hi, g * HEAD_SIZE : (g + 1) * HEAD_SIZE]
                    + own_weights[lo:hi] * new_value
                )
    out_ref[0] = result[...].astype(BF16)


def attend(
    token, place, lengths, parts, scale, biases, cos, sin, keys, values, loads, *, chunk, heads
):
    first = chunk == 0
    per = keys.shape[0]
    out_rows = heads * QUERIES_PER_KV * per
    return call(
        functools.partial(
            attend_kernel,
            first=first,
            heads=heads,
            per=per,
            group=SLOTS_AT_ONCE[heads],
            start_head=sum(CHUNK_HEADS[:chunk]),
        ),
        "attend" + str(chunk),
        token,
        [place, lengths],
        list(parts) + ([] if first else [scale]) + list(biases) + [cos, sin],
        [((1, out_rows, HEAD_SIZE), BF16)] + ([((per, HEAD_SIZE), F32)] if first else []),
        [
            pltpu.VMEM((heads * TILES * per, HEAD_SIZE), F32),
            pltpu.VMEM((out_rows, HEAD_SIZE), F32),
        ],
        8,
        loads,
        [keys, values],
    )


def output_kernel(*refs, labels, nz, per, first, last, start_depth):
    count = len(labels)
    place_ref, block_refs, order_ref = refs[0], refs[1 : 1 + count], refs[1 + count]
    rest = refs[2 + count :]
    if not first:
        acc_in_ref, rest = rest[0], rest[1:]
    w_ref, rest = rest[0], rest[1:]
    if last:
        mine_ref, send_ref, stacked = rest
    else:
        acc_out_ref, *rest, stacked = rest
    tiles = block_refs[0].shape[1] // per
    depth = tiles * HEAD_SIZE

    if first:
        slot_of_row = order_ref[...]
        half = slot_of_row.shape[1] // 2
        swapped = jnp.concatenate([slot_of_row[:, half:], slot_of_row[:, :half]], axis=1)
        slot_of_row = jnp.where(place_ref[2] == 0, slot_of_row, swapped)
        one_hot = slot_one_hot(place_ref, slot_of_row, nz, per).astype(F32).T.astype(BF16)
        rest[0][...] = one_hot
    else:
        one_hot = order_ref[...]
    wide = {
        label: ref[z].astype(F32)
        for ref, own in zip(block_refs, labels)
        for z, label in enumerate(own)
    }
    wide = [wide[h, q] for h in range(2) for q in place_order(nz)]
    for c in range(tiles):
        stacked[:, c * HEAD_SIZE : (c + 1) * HEAD_SIZE] = jnp.concatenate(
            [block[c * per : (c + 1) * per] for block in wide], axis=0
        ).astype(BF16)
    stacked[...] = jnp.dot(one_hot, stacked[...], preferred_element_type=F32).astype(BF16)
    product = jnp.dot(
        stacked[...], w_ref[start_depth : start_depth + depth, :], preferred_element_type=F32
    )
    if not first:
        product = product + acc_in_ref[...]
    if last:
        half = product.shape[0] // 2
        mine_ref[...] = product[:half]
        send_ref[...] = product[half:].astype(BF16)
    else:
        acc_out_ref[...] = product


def output(token, place, blocks, labels, order, w_out, acc, loads, *, chunk, chunks, nz, per):
    first, last = chunk == 0, chunk == chunks - 1
    rows = 2 * nz * per
    width = w_out.shape[1]
    depth = CHUNK_HEADS[chunk] * QUERIES_PER_KV * HEAD_SIZE
    if last:
        out_shapes = [((rows // 2, width), F32), ((rows // 2, width), BF16)]
    else:
        out_shapes = [((rows, width), F32)] + ([((rows, rows), BF16)] if first else [])
    return call(
        functools.partial(
            output_kernel,
            labels=labels,
            nz=nz,
            per=per,
            first=first,
            last=last,
            start_depth=sum(CHUNK_HEADS[:chunk]) * QUERIES_PER_KV * HEAD_SIZE,
        ),
        "output" + str(chunk),
        token,
        [place],
        [*blocks, order] + ([] if first else [acc]),
        out_shapes,
        [pltpu.VMEM((rows, depth), BF16)],
        12,
        loads,
        [w_out],
    )


def on_device(
    hidden_rows,
    norm_gain,
    w_query,
    key_weight,
    value_weight,
    query_bias,
    key_bias_vector,
    value_bias_vector,
    rotated_key_cache,
    stored_value_cache,
    slot_valid_lengths,
    slot_of_row,
    w_out,
    *,
    size,
):
    nz = size // 2
    assert size % 2 == 0 and nz & (nz - 1) == 0 and nz > 2
    per = rotated_key_cache.shape[0]
    kv_heads = key_weight.shape[1] // HEAD_SIZE
    assert sum(CHUNK_HEADS) == kv_heads and per == SLOTS_AT_ONCE[1]
    chunks = len(CHUNK_HEADS)
    gx = lax.axis_index("gx")
    gy = lax.axis_index("gy")
    place = jnp.stack([gx // 2, gx % 2, gy]).astype(jnp.int32)

    other = lax.ppermute(hidden_rows, "gy", [(0, 1), (1, 0)])
    sor = slot_of_row[None, :]
    gain = norm_gain.reshape(-1, HEAD_SIZE)

    lengths = lax.dynamic_slice_in_dim(slot_valid_lengths, gx * per, per, 0)
    lane = jnp.arange(HEAD_SIZE)
    half_width = HEAD_SIZE // 2
    frequency = ROPE_BASE ** (-((lane % half_width).astype(F32) * 2.0 / HEAD_SIZE))
    angles = lengths.astype(F32)[:, None] * frequency[None, :]
    cos = jnp.cos(angles)
    sin = jnp.sin(angles) * jnp.where(lane < half_width, -1.0, 1.0)[None, :]
    biases = [b.reshape(-1, HEAD_SIZE) for b in (query_bias, key_bias_vector, value_bias_vector)]

    def head_window(c, width):
        return pl.ds(sum(CHUNK_HEADS[:c]) * width, CHUNK_HEADS[c] * width)

    wide = QUERIES_PER_KV * HEAD_SIZE
    everything = pl.ds(0, w_query.shape[0])
    positions = rotated_key_cache.shape[1]
    all_columns = pl.ds(0, w_out.shape[1])
    same_z = neighbour_pairs(nz)
    scale = acc = None
    order = sor
    inputs = [hidden_rows, other, gain, sor]
    kept, swapped, reduced = {}, {}, {}
    loaded, gathered, waiting = {}, {}, {}

    def over_y(blocks, labels):
        return lax.ppermute(blocks, "gx", same_z), [(1 - h, q) for h, q in labels]

    def over_z(blocks, labels, stride):
        moved = lax.ppermute(blocks, "gx", stride_pairs(nz, stride))
        return moved, [(h, q ^ stride) for h, q in labels]

    def windows_of(kind, c):
        return [
            (array, (everything, head_window(c, n)))
            for array, n in ((w_query, wide), (key_weight, HEAD_SIZE), (value_weight, HEAD_SIZE))
        ]

    def file_loaded(wanted, arrays):
        arrays = list(arrays)
        for kind, c in wanted:
            loaded[kind, c] = [arrays.pop(0) for _ in windows_of(kind, c)]

    def loads_of(wanted):
        return [pair for kind, c in wanted for pair in windows_of(kind, c)]

    def do_load(token, wanted):
        name = "load" + "".join("_" + kind + str(c) for kind, c in wanted)
        token, arrays, _ = call(lambda: None, name, token, [], [], [], [], 1, loads_of(wanted))
        file_loaded(wanted, arrays)
        return token

    def do_project(token, c, wanted):
        nonlocal inputs
        token, arrays, outs = project(
            token, place, inputs, loaded["weights", c], loads_of(wanted),
            chunk=c, heads=CHUNK_HEADS[c], nz=nz, per=per,
        )
        file_loaded(wanted, arrays)
        kept[c] = outs[0]
        if c == 0:
            inputs = [outs[-1]]
        if Y_IN_HALVES[c]:
            far = lax.ppermute(outs[2], "gx", same_z)
            swapped[c] = (lax.ppermute(outs[1], "gx", same_z), 0), (far, 0)
        else:
            both = lax.ppermute(outs[1], "gx", same_z)
            swapped[c] = (both, 0), (both, nz // 2)
        return token

    def do_far(token, c, wanted):
        half = nz // 2
        token, (total,) = add(
            "add_far" + str(c), token, [kept[c], swapped[c][1][0]], [half, swapped[c][1][1]], half, 1
        )
        reduced[c] = lax.ppermute(total, "gx", stride_pairs(nz, 1))
        return token

    def do_near(token, c, wanted):
        terms, starts, count = [kept[c], swapped[c][0][0], reduced[c]], [0, 0, 0], nz // 2
        for stride in strides(nz)[1:]:
            token, (mine, sent) = add(
                "add_near" + str(c) + "_" + str(stride), token, terms, starts, count, 2
            )
            terms = [mine, lax.ppermute(sent, "gx", stride_pairs(nz, stride))]
            starts, count = [0, 0], count // 2
        reduced[c] = terms
        return token

    def do_attend(token, c, wanted):
        nonlocal scale
        token, arrays, outs = attend(
            token, place, slot_valid_lengths, reduced[c], scale, biases, cos, sin, rotated_key_cache, stored_value_cache,
            loads_of(wanted), chunk=c, heads=CHUNK_HEADS[c],
        )
        file_loaded(wanted, arrays)
        if c == 0:
            scale = outs[1]
        own = outs[0], [(0, 0)]
        first_move = over_y(*own) if GATHER[c] == "y first" else over_z(*own, strides(nz)[-1])
        waiting[c] = own, first_move
        return token

    def do_gather(token, c, wanted):
        held, moved = waiting[c]
        for stride in reversed(strides(nz) if GATHER[c] == "y first" else strides(nz)[:-1]):
            if GATHER[c] == "y first" and stride == 1:
                break
            token, joined = join("join" + str(c) + "_" + str(stride), token, held[0], moved[0])
            held = joined, held[1] + moved[1]
            moved = over_z(*held, stride)
        waiting[c] = held, moved
        gathered[c] = [held, moved]
        if GATHER[c] == "y halved":
            gathered[c].append(over_y(*held))
        return token

    def do_forward(token, c, wanted):
        held, moved = waiting[c]
        if GATHER[c] == "y halved":
            gathered[c].append(over_y(*moved))
            return token
        token, joined = join("join" + str(c), token, held[0], moved[0])
        held = joined, held[1] + moved[1]
        gathered[c] = [held, over_z(*held, 1) if GATHER[c] == "y first" else over_y(*held)]
        return token

    def do_output(token, c, wanted):
        nonlocal acc, order
        token, arrays, outs = output(
            token, place, [a for a, _ in gathered[c]], [own for _, own in gathered[c]], order,
            w_out, acc, loads_of(wanted),
            chunk=c, chunks=chunks, nz=nz, per=per,
        )
        file_loaded(wanted, arrays)
        acc = outs[0]
        if c == 0:
            order = outs[1]
        if c == chunks - 1:
            acc = outs
        return token

    token = jnp.zeros(TOKEN, F32)
    steps = {
        "project": do_project,
        "far": do_far,
        "near": do_near,
        "attend": do_attend,
        "gather": do_gather,
        "forward": do_forward,
        "output": do_output,
    }
    needs = {"project": "weights", "attend": "caches", "output": "out"}
    wanted = []
    for step, c in ORDER:
        if step not in steps:
            wanted.append((step, c))
            continue
        if step not in needs or (needs[step], c) in wanted:
            if wanted:
                token = do_load(token, wanted)
            wanted = []
        token = steps[step](token, c, wanted)
        wanted = []
    mine, send = acc
    received = lax.ppermute(send, "gy", [(0, 1), (1, 0)])
    return (hidden_rows.astype(F32) + mine + received.astype(F32)).astype(BF16)


def solution(mesh):
    in_specs = (
        P(("grp", "gy"), "gx"),
        P("gx"),
        P("gx", "gy"),
        P("gx", "gy"),
        P("gx", "gy"),
        P("gy"),
        P("gy"),
        P("gy"),
        P(("grp", "gx"), None, "gy"),
        P(("grp", "gx"), None, "gy"),
        P("grp"),
        P("grp"),
        P("gy", "gx"),
    )
    out_specs = P(("grp", "gy"), "gx")
    return jax.shard_map(
        functools.partial(on_device, size=mesh.shape["gx"]),
        mesh=mesh,
        in_specs=in_specs,
        out_specs=out_specs,
        check_vma=False,
    )
```

```python
import functools
import math

import jax
import jax.numpy as jnp
from jax import lax
from jax.experimental import pallas as pl
from jax.experimental.pallas import tpu as pltpu
from jax.sharding import PartitionSpec as P

MODEL_WIDTH = 8192
QUERY_HEADS = 64
KEY_VALUE_HEADS = 8
HEAD_SIZE = 128
QUERIES_PER_KV = QUERY_HEADS // KEY_VALUE_HEADS
TILES = QUERIES_PER_KV + 2
SQUARE_ROWS = 32

EPSILON = 1e-06
ROPE_BASE = 1000000.0
CHUNK_HEADS = (1, 2, 1)
F32 = jnp.float32
BF16 = jnp.bfloat16
MIB = 1024 * 1024
SLOTS_AT_ONCE = {1: 24, 2: 8, 3: 8, 4: 4}
PEAK_FLOP_PER_US = 1.1535e9
COSTS = {'add_far0': 8, 'add_near0_2': 0.1, 'attend0': 2, 'output0': 1.4, 'project1': 1, 'add_far1': 1, 'attend1': 4, 'join1': 16, 'output1': 1, 'project2': 1, 'attend2': 4, 'join2': 16, 'join0': 2, 'join0_1': 0.3}
Y_IN_HALVES = (True, True, True)
GATHER = ('y halved', 'y halved', 'y halved')
ORDER = (
    ("weights", 0),
    ("project", 0),
    ("project", 1),
    ("far", 0),
    ("project", 2),
    ("far", 1),
    ("near", 0),
    ("near", 1),
    ("far", 2),
    ("attend", 0),
    ("attend", 1),
    ("near", 2),
    ("gather", 0),
    ("gather", 1),
    ("attend", 2),
    ("forward", 0),
    ("forward", 1),
    ("output", 0),
    ("gather", 2),
    ("forward", 2),
    ("output", 1),
    ("output", 2),
)
F32 = jnp.float32
BF16 = jnp.bfloat16


def neighbour_pairs(nz):
    return [(z * 2 + y, z * 2 + 1 - y) for z in range(nz) for y in range(2)]


def stride_pairs(nz, stride):
    return [(z * 2 + y, (z ^ stride) * 2 + y) for z in range(nz) for y in range(2)]


def strides(nz):
    return [1 << i for i in range(nz.bit_length() - 1)]


def place_order(nz):
    return sorted(range(nz), key=lambda q: [(q & b) != 0 for b in strides(nz)])


def slot_one_hot(place_ref, slot_of_row, nz, per):
    rows = slot_of_row.shape[1]
    base = lax.broadcasted_iota(jnp.int32, (per, rows), 0)
    blocks = []
    for h in range(2):
        for q in place_order(nz):
            owner = (place_ref[0] ^ q) * 2 + (place_ref[1] ^ h)
            blocks.append(jnp.where(base + owner * per == slot_of_row, 1.0, 0.0).astype(F32))
    return jnp.concatenate(blocks, axis=0).astype(BF16)


TOKEN = (8, HEAD_SIZE)


def estimate(name):
    flops = int(COSTS.get(name, 0) * PEAK_FLOP_PER_US)
    return pl.CostEstimate(flops=flops, bytes_accessed=0, transcendentals=0)


def copies_of(sources, windows, targets, sems):
    return [
        pltpu.make_async_copy(source.at[window], target, sems.at[i])
        for i, (source, window, target) in enumerate(zip(sources, windows, targets))
    ]


def call(
    kernel, name, token, scalars, arrays, out_shapes, scratch, vmem_mib, loads=(), resident=()
):
    arrays = list(arrays) + [
        pltpu.with_memory_space_constraint(array, pltpu.VMEM) for array in resident
    ]
    sources = [array for array, _ in loads]
    windows = [window for _, window in loads]
    loaded_shapes = [
        tuple(w.size if isinstance(w, pl.Slice) else n for w, n in zip(window, array.shape))
        for array, window in loads
    ]

    def body(*refs):
        refs = list(refs)
        del refs[0]
        source_refs = [refs.pop(0) for _ in loads]
        in_refs = [refs.pop(0) for _ in range(len(scalars) + len(arrays))]
        token_ref = refs.pop(0)
        target_refs = [refs.pop(0) for _ in loads]
        copies = copies_of(source_refs, windows, target_refs, refs.pop() if loads else None)
        for copy in copies:
            copy.start()
        token_ref[...] = jnp.zeros(TOKEN, F32)
        kernel(*in_refs, *refs)
        for copy in copies:
            copy.wait()

    vmem = pl.BlockSpec(memory_space=pltpu.VMEM)
    outs = pl.pallas_call(
        body,
        in_specs=[vmem]
        + [pl.BlockSpec(memory_space=pltpu.HBM)] * len(loads)
        + [pl.BlockSpec(memory_space=pltpu.SMEM)] * len(scalars)
        + [vmem] * len(arrays),
        out_specs=[vmem] * (1 + len(loads) + len(out_shapes)),
        out_shape=[pltpu.VMEM(TOKEN, F32)]
        + [pltpu.VMEM(shape, array.dtype) for shape, array in zip(loaded_shapes, sources)]
        + [pltpu.VMEM(shape, dtype) for shape, dtype in out_shapes],
        scratch_shapes=list(scratch) + ([pltpu.SemaphoreType.DMA((len(loads),))] if loads else []),
        compiler_params=pltpu.CompilerParams(vmem_limit_bytes=vmem_mib * MIB),
        cost_estimate=estimate(name),
        name=name,
    )(
        token,
        *[pltpu.with_memory_space_constraint(array, pltpu.HBM) for array in sources],
        *scalars,
        *arrays,
    )
    return outs[0], outs[1 : 1 + len(loads)], outs[1 + len(loads) :]


def places_of(refs, per):
    blocks = [(ref, z) for ref in refs for z in range(ref.shape[0])]
    return [(i * per, ref, z) for i, (ref, z) in enumerate(blocks)]


def project_kernel(*refs, nz, per, first, heads, start_head):
    place_ref = refs[0]
    if first:
        own_ref, other_ref, gain_ref, sor_ref, wq_ref, wk_ref, wv_ref = refs[1:8]
        *out_refs, slotted_ref, acc = refs[8:]
        places = places_of(out_refs, per)
        one_hot = slot_one_hot(place_ref, sor_ref[...], nz, per)
        own, other = own_ref[...], other_ref[...]
        lower = place_ref[2] == 0
        rows = jnp.concatenate(
            [jnp.where(lower, own, other), jnp.where(lower, other, own)], axis=0
        )
        hidden = jnp.dot(one_hot, rows, preferred_element_type=F32)
        gain = gain_ref[...].astype(F32)
        gain = jnp.concatenate([gain[j : j + 1] for j in range(gain.shape[0])], axis=1)
        slotted_ref[...] = (hidden * gain).astype(BF16)
        squares = jnp.sum(hidden * hidden, axis=1, keepdims=True)
        high = squares.astype(BF16).astype(F32)
        low = squares - high
        lane = lax.broadcasted_iota(jnp.int32, (per, HEAD_SIZE), 1)
        lane_high = place_ref[1] * 2
        for at, ref, z in places:
            packed = jnp.where(
                lane == lane_high,
                high[at : at + per],
                jnp.where(lane == lane_high + 1, low[at : at + per], 0.0),
            )
            packed = jnp.concatenate(
                [packed, jnp.zeros((SQUARE_ROWS - per, HEAD_SIZE), F32)], axis=0
            )
            ref[z, heads * TILES * per :, :] = packed.astype(BF16)
    else:
        slotted_ref, wq_ref, wk_ref, wv_ref = refs[1:5]
        *out_refs, acc = refs[5:]
        places = places_of(out_refs, per)

    columns = QUERIES_PER_KV * HEAD_SIZE
    slotted = slotted_ref[...]
    for g in range(heads):
        head = start_head + g
        acc[:, :columns] = jnp.dot(
            slotted, wq_ref[:, head * columns : (head + 1) * columns], preferred_element_type=F32
        )
        narrow = slice(head * HEAD_SIZE, (head + 1) * HEAD_SIZE)
        acc[:, columns:] = jnp.dot(
            slotted,
            jnp.concatenate([wk_ref[:, narrow], wv_ref[:, narrow]], axis=1),
            preferred_element_type=F32,
        )
        for at, ref, z in places:
            block = jnp.concatenate(
                [
                    acc[at : at + per, c * HEAD_SIZE : (c + 1) * HEAD_SIZE]
                    for c in range(TILES)
                ],
                axis=0,
            )
            ref[z, g * TILES * per : (g + 1) * TILES * per, :] = block.astype(BF16)


def project(token, place, inputs, weights, loads, *, chunk, heads, nz, per):
    first = chunk == 0
    rows = 2 * nz * per
    depth = weights[0].shape[0]
    block_rows = heads * TILES * per + (SQUARE_ROWS if first else 0)
    counts = [nz, nz // 2, nz // 2] if Y_IN_HALVES[chunk] else [nz, nz]
    out_shapes = [((count, block_rows, HEAD_SIZE), BF16) for count in counts]
    return call(
        functools.partial(
            project_kernel,
            nz=nz,
            per=per,
            first=first,
            heads=heads,
            start_head=sum(CHUNK_HEADS[:chunk]),
        ),
        "project" + str(chunk),
        token,
        [place],
        [*inputs, *weights] if first else inputs,
        out_shapes + ([((rows, depth), BF16)] if first else []),
        [pltpu.VMEM((rows, TILES * HEAD_SIZE), F32)],
        12,
        loads,
        () if first else weights,
    )


def add_kernel(*refs, starts, count):
    terms = len(starts)
    outs = refs[terms:]
    each = outs[0].shape[0]
    for z in range(count):
        total = refs[0][starts[0] + z].astype(F32)
        for ref, start in zip(refs[1:terms], starts[1:]):
            total = total + ref[start + z].astype(F32)
        outs[z // each][z % each] = total.astype(BF16)


def add(name, token, arrays, starts, count, parts):
    shape = (count // parts,) + arrays[0].shape[1:]
    token, _, sums = call(
        functools.partial(add_kernel, starts=starts, count=count),
        name,
        token,
        [],
        arrays,
        [(shape, BF16)] * parts,
        [],
        2,
    )
    return token, sums


def join_kernel(a_ref, b_ref, out_ref):
    count = a_ref.shape[0]
    out_ref[:count] = a_ref[...]
    out_ref[count:] = b_ref[...]


def join(name, token, a, b):
    shape = (a.shape[0] + b.shape[0],) + a.shape[1:]
    token, _, (joined,) = call(join_kernel, name, token, [], [a, b], [(shape, BF16)], [], 2)
    return token, joined


def attend_kernel(*refs, first, heads, per, group, start_head):
    place_ref, lengths_ref, mine_ref, last_ref = refs[:4]
    rest = refs[4:]
    if first:
        qb_ref, kb_ref, vb_ref, cos_ref, sin_ref, k_ref, v_ref, out_ref, scale_ref = rest[:9]
    else:
        scale_in_ref, qb_ref, kb_ref, vb_ref, cos_ref, sin_ref, k_ref, v_ref, out_ref = rest[:9]
    fresh, result = rest[9:]
    body = heads * TILES * per
    head_rows = TILES * per

    if first:
        squares = mine_ref[0, body:, :].astype(F32) + last_ref[0, body:, :].astype(F32)
        total = jnp.sum(squares[:per], axis=1, keepdims=True)
        scale = jnp.broadcast_to(lax.rsqrt(total / MODEL_WIDTH + EPSILON), (per, HEAD_SIZE))
        scale_ref[...] = scale
    else:
        scale = scale_in_ref[...]
    cos, sin = cos_ref[...], sin_ref[...]
    query_bias = qb_ref[...].astype(F32)
    key_bias = kb_ref[...].astype(F32)
    value_bias = vb_ref[...].astype(F32)
    for g in range(heads):
        rows = pl.ds(g * head_rows, head_rows)
        summed = mine_ref[0, rows, :].astype(F32) + last_ref[0, rows, :].astype(F32)
        head = start_head + g
        for c in range(TILES):
            if c < QUERIES_PER_KV:
                at = head * QUERIES_PER_KV + c
                bias = query_bias[at : at + 1]
            else:
                bias = (key_bias if c == QUERIES_PER_KV else value_bias)[head : head + 1]
            tile = summed[c * per : (c + 1) * per] * scale + bias
            if c < TILES - 1:
                tile = tile * cos + pltpu.roll(tile, HEAD_SIZE // 2, 1) * sin
            fresh[pl.ds(g * head_rows + c * per, per), :] = tile.astype(BF16).astype(F32)

    positions = k_ref.shape[1]
    columns = slice(start_head * HEAD_SIZE, (start_head + heads) * HEAD_SIZE)
    qrows = heads * QUERIES_PER_KV
    lanes = group * qrows
    extra = 16
    lane_block = lax.broadcasted_iota(jnp.int32, (HEAD_SIZE, lanes), 1) // QUERIES_PER_KV
    top_row = lax.broadcasted_iota(jnp.int32, (extra, HEAD_SIZE), 0) == 0
    lane_slot = lax.broadcasted_iota(jnp.int32, (1, lanes), 1) // qrows
    row = lax.broadcasted_iota(jnp.int32, (positions + extra, lanes), 0)
    row_slot = lax.broadcasted_iota(jnp.int32, (lanes, positions), 0) // qrows
    base = (place_ref[0] * 2 + place_ref[1]) * per
    for start in range(0, per, group):
        slots = range(start, start + group)
        queries = jnp.concatenate(
            [
                fresh[pl.ds(g * head_rows + s, QUERIES_PER_KV, stride=per), :]
                for s in slots
                for g in range(heads)
            ],
            axis=0,
        )
        turned = queries.T
        query, new_key = [], []
        for i, s in enumerate(slots):
            for g in range(heads):
                query.append(jnp.where(lane_block == i * heads + g, turned, 0.0).astype(BF16))
                key = fresh[pl.ds(g * head_rows + QUERIES_PER_KV * per + s, 1), :]
                new_key.append(jnp.where(top_row, key, 0.0).astype(BF16))
        keys = jnp.concatenate(
            [
                jnp.concatenate([k_ref[s, :, columns] for s in slots], axis=1),
                jnp.concatenate(new_key, axis=1),
            ],
            axis=0,
        )
        scores = jnp.dot(keys, jnp.concatenate(query, axis=0), preferred_element_type=F32)

        lengths = jnp.zeros((1, lanes), jnp.int32)
        for i, s in enumerate(slots):
            lengths = jnp.where(lane_slot == i, lengths_ref[base + s], lengths)
        valid = (row < lengths) | (row == positions)
        scores = jnp.where(valid, scores * (1.0 / math.sqrt(HEAD_SIZE)), -1e30)
        top = jnp.max(scores, axis=0, keepdims=True)
        exps = jnp.where(valid, jnp.exp(scores - top), 0.0)
        weights = exps * (1.0 / jnp.sum(exps, axis=0, keepdims=True))
        cache_weights = weights[:positions].T
        own_weights = weights[positions : positions + 8].T[:, 0:1].astype(BF16).astype(F32)
        spread = jnp.concatenate(
            [jnp.where(row_slot == i, cache_weights, 0.0).astype(BF16) for i in range(group)],
            axis=1,
        )
        values = v_ref[start : start + group, :, columns].reshape(group * positions, heads * HEAD_SIZE)
        mixed = jnp.dot(spread, values, preferred_element_type=F32)
        for i, s in enumerate(slots):
            for g in range(heads):
                lo = i * qrows + g * QUERIES_PER_KV
                hi = lo + QUERIES_PER_KV
                new_value = fresh[pl.ds(g * head_rows + (QUERIES_PER_KV + 1) * per + s, 1), :]
                result[pl.ds(g * QUERIES_PER_KV * per + s, QUERIES_PER_KV, stride=per), :] = (
                    mixed[lo:hi, g * HEAD_SIZE : (g + 1) * HEAD_SIZE]
                    + own_weights[lo:hi] * new_value
                )
    out_ref[0] = result[...].astype(BF16)


def attend(
    token, place, lengths, parts, scale, biases, cos, sin, keys, values, loads, *, chunk, heads
):
    first = chunk == 0
    per = keys.shape[0]
    out_rows = heads * QUERIES_PER_KV * per
    return call(
        functools.partial(
            attend_kernel,
            first=first,
            heads=heads,
            per=per,
            group=SLOTS_AT_ONCE[heads],
            start_head=sum(CHUNK_HEADS[:chunk]),
        ),
        "attend" + str(chunk),
        token,
        [place, lengths],
        list(parts) + ([] if first else [scale]) + list(biases) + [cos, sin],
        [((1, out_rows, HEAD_SIZE), BF16)] + ([((per, HEAD_SIZE), F32)] if first else []),
        [
            pltpu.VMEM((heads * TILES * per, HEAD_SIZE), F32),
            pltpu.VMEM((out_rows, HEAD_SIZE), F32),
        ],
        8,
        loads,
        [keys, values],
    )


def output_kernel(*refs, labels, nz, per, first, last, start_depth):
    count = len(labels)
    place_ref, block_refs, order_ref = refs[0], refs[1 : 1 + count], refs[1 + count]
    rest = refs[2 + count :]
    if not first:
        acc_in_ref, rest = rest[0], rest[1:]
    w_ref, rest = rest[0], rest[1:]
    if last:
        mine_ref, send_ref, stacked = rest
    else:
        acc_out_ref, *rest, stacked = rest
    tiles = block_refs[0].shape[1] // per
    depth = tiles * HEAD_SIZE

    if first:
        slot_of_row = order_ref[...]
        half = slot_of_row.shape[1] // 2
        swapped = jnp.concatenate([slot_of_row[:, half:], slot_of_row[:, :half]], axis=1)
        slot_of_row = jnp.where(place_ref[2] == 0, slot_of_row, swapped)
        one_hot = slot_one_hot(place_ref, slot_of_row, nz, per).astype(F32).T.astype(BF16)
        rest[0][...] = one_hot
    else:
        one_hot = order_ref[...]
    wide = {
        label: ref[z].astype(F32)
        for ref, own in zip(block_refs, labels)
        for z, label in enumerate(own)
    }
    wide = [wide[h, q] for h in range(2) for q in place_order(nz)]
    for c in range(tiles):
        stacked[:, c * HEAD_SIZE : (c + 1) * HEAD_SIZE] = jnp.concatenate(
            [block[c * per : (c + 1) * per] for block in wide], axis=0
        ).astype(BF16)
    stacked[...] = jnp.dot(one_hot, stacked[...], preferred_element_type=F32).astype(BF16)
    product = jnp.dot(
        stacked[...], w_ref[start_depth : start_depth + depth, :], preferred_element_type=F32
    )
    if not first:
        product = product + acc_in_ref[...]
    if last:
        half = product.shape[0] // 2
        mine_ref[...] = product[:half]
        send_ref[...] = product[half:].astype(BF16)
    else:
        acc_out_ref[...] = product


def output(token, place, blocks, labels, order, w_out, acc, loads, *, chunk, chunks, nz, per):
    first, last = chunk == 0, chunk == chunks - 1
    rows = 2 * nz * per
    width = w_out.shape[1]
    depth = CHUNK_HEADS[chunk] * QUERIES_PER_KV * HEAD_SIZE
    if last:
        out_shapes = [((rows // 2, width), F32), ((rows // 2, width), BF16)]
    else:
        out_shapes = [((rows, width), F32)] + ([((rows, rows), BF16)] if first else [])
    return call(
        functools.partial(
            output_kernel,
            labels=labels,
            nz=nz,
            per=per,
            first=first,
            last=last,
            start_depth=sum(CHUNK_HEADS[:chunk]) * QUERIES_PER_KV * HEAD_SIZE,
        ),
        "output" + str(chunk),
        token,
        [place],
        [*blocks, order] + ([] if first else [acc]),
        out_shapes,
        [pltpu.VMEM((rows, depth), BF16)],
        12,
        loads,
        [w_out],
    )


def on_device(
    hidden_rows,
    norm_gain,
    w_query,
    key_weight,
    value_weight,
    query_bias,
    key_bias_vector,
    value_bias_vector,
    rotated_key_cache,
    stored_value_cache,
    slot_valid_lengths,
    slot_of_row,
    w_out,
    *,
    size,
):
    nz = size // 2
    assert size % 2 == 0 and nz & (nz - 1) == 0 and nz > 2
    per = rotated_key_cache.shape[0]
    kv_heads = key_weight.shape[1] // HEAD_SIZE
    assert sum(CHUNK_HEADS) == kv_heads and per == SLOTS_AT_ONCE[1]
    chunks = len(CHUNK_HEADS)
    gx = lax.axis_index("gx")
    gy = lax.axis_index("gy")
    place = jnp.stack([gx // 2, gx % 2, gy]).astype(jnp.int32)

    other = lax.ppermute(hidden_rows, "gy", [(0, 1), (1, 0)])
    sor = slot_of_row[None, :]
    gain = norm_gain.reshape(-1, HEAD_SIZE)

    lengths = lax.dynamic_slice_in_dim(slot_valid_lengths, gx * per, per, 0)
    lane = jnp.arange(HEAD_SIZE)
    half_width = HEAD_SIZE // 2
    frequency = ROPE_BASE ** (-((lane % half_width).astype(F32) * 2.0 / HEAD_SIZE))
    angles = lengths.astype(F32)[:, None] * frequency[None, :]
    cos = jnp.cos(angles)
    sin = jnp.sin(angles) * jnp.where(lane < half_width, -1.0, 1.0)[None, :]
    biases = [b.reshape(-1, HEAD_SIZE) for b in (query_bias, key_bias_vector, value_bias_vector)]

    def head_window(c, width):
        return pl.ds(sum(CHUNK_HEADS[:c]) * width, CHUNK_HEADS[c] * width)

    wide = QUERIES_PER_KV * HEAD_SIZE
    everything = pl.ds(0, w_query.shape[0])
    positions = rotated_key_cache.shape[1]
    all_columns = pl.ds(0, w_out.shape[1])
    same_z = neighbour_pairs(nz)
    scale = acc = None
    order = sor
    inputs = [hidden_rows, other, gain, sor]
    kept, swapped, reduced = {}, {}, {}
    loaded, gathered, waiting = {}, {}, {}

    def over_y(blocks, labels):
        return lax.ppermute(blocks, "gx", same_z), [(1 - h, q) for h, q in labels]

    def over_z(blocks, labels, stride):
        moved = lax.ppermute(blocks, "gx", stride_pairs(nz, stride))
        return moved, [(h, q ^ stride) for h, q in labels]

    def windows_of(kind, c):
        return [
            (array, (everything, head_window(c, n)))
            for array, n in ((w_query, wide), (key_weight, HEAD_SIZE), (value_weight, HEAD_SIZE))
        ]

    def file_loaded(wanted, arrays):
        arrays = list(arrays)
        for kind, c in wanted:
            loaded[kind, c] = [arrays.pop(0) for _ in windows_of(kind, c)]

    def loads_of(wanted):
        return [pair for kind, c in wanted for pair in windows_of(kind, c)]

    def do_load(token, wanted):
        name = "load" + "".join("_" + kind + str(c) for kind, c in wanted)
        token, arrays, _ = call(lambda: None, name, token, [], [], [], [], 1, loads_of(wanted))
        file_loaded(wanted, arrays)
        return token

    def do_project(token, c, wanted):
        nonlocal inputs
        token, arrays, outs = project(
            token, place, inputs,
            loaded["weights", 0] if c == 0 else [w_query, key_weight, value_weight],
            loads_of(wanted),
            chunk=c, heads=CHUNK_HEADS[c], nz=nz, per=per,
        )
        file_loaded(wanted, arrays)
        kept[c] = outs[0]
        if c == 0:
            inputs = [outs[-1]]
        if Y_IN_HALVES[c]:
            far = lax.ppermute(outs[2], "gx", same_z)
            swapped[c] = (lax.ppermute(outs[1], "gx", same_z), 0), (far, 0)
        else:
            both = lax.ppermute(outs[1], "gx", same_z)
            swapped[c] = (both, 0), (both, nz // 2)
        return token

    def do_far(token, c, wanted):
        half = nz // 2
        token, (total,) = add(
            "add_far" + str(c), token, [kept[c], swapped[c][1][0]], [half, swapped[c][1][1]], half, 1
        )
        reduced[c] = lax.ppermute(total, "gx", stride_pairs(nz, 1))
        return token

    def do_near(token, c, wanted):
        terms, starts, count = [kept[c], swapped[c][0][0], reduced[c]], [0, 0, 0], nz // 2
        for stride in strides(nz)[1:]:
            token, (mine, sent) = add(
                "add_near" + str(c) + "_" + str(stride), token, terms, starts, count, 2
            )
            terms = [mine, lax.ppermute(sent, "gx", stride_pairs(nz, stride))]
            starts, count = [0, 0], count // 2
        reduced[c] = terms
        return token

    def do_attend(token, c, wanted):
        nonlocal scale
        token, arrays, outs = attend(
            token, place, slot_valid_lengths, reduced[c], scale, biases, cos, sin, rotated_key_cache, stored_value_cache,
            loads_of(wanted), chunk=c, heads=CHUNK_HEADS[c],
        )
        file_loaded(wanted, arrays)
        if c == 0:
            scale = outs[1]
        own = outs[0], [(0, 0)]
        first_move = over_y(*own) if GATHER[c] == "y first" else over_z(*own, strides(nz)[-1])
        waiting[c] = own, first_move
        return token

    def do_gather(token, c, wanted):
        held, moved = waiting[c]
        for stride in reversed(strides(nz) if GATHER[c] == "y first" else strides(nz)[:-1]):
            if GATHER[c] == "y first" and stride == 1:
                break
            token, joined = join("join" + str(c) + "_" + str(stride), token, held[0], moved[0])
            held = joined, held[1] + moved[1]
            moved = over_z(*held, stride)
        waiting[c] = held, moved
        gathered[c] = [held, moved]
        if GATHER[c] == "y halved":
            gathered[c].append(over_y(*held))
        return token

    def do_forward(token, c, wanted):
        held, moved = waiting[c]
        if GATHER[c] == "y halved":
            gathered[c].append(over_y(*moved))
            return token
        token, joined = join("join" + str(c), token, held[0], moved[0])
        held = joined, held[1] + moved[1]
        gathered[c] = [held, over_z(*held, 1) if GATHER[c] == "y first" else over_y(*held)]
        return token

    def do_output(token, c, wanted):
        nonlocal acc, order
        token, arrays, outs = output(
            token, place, [a for a, _ in gathered[c]], [own for _, own in gathered[c]], order,
            w_out, acc, loads_of(wanted),
            chunk=c, chunks=chunks, nz=nz, per=per,
        )
        file_loaded(wanted, arrays)
        acc = outs[0]
        if c == 0:
            order = outs[1]
        if c == chunks - 1:
            acc = outs
        return token

    token = jnp.zeros(TOKEN, F32)
    steps = {
        "project": do_project,
        "far": do_far,
        "near": do_near,
        "attend": do_attend,
        "gather": do_gather,
        "forward": do_forward,
        "output": do_output,
    }
    needs = {"project": "weights", "attend": "caches", "output": "out"}
    wanted = []
    for step, c in ORDER:
        if step not in steps:
            wanted.append((step, c))
            continue
        if step not in needs or (needs[step], c) in wanted:
            if wanted:
                token = do_load(token, wanted)
            wanted = []
        token = steps[step](token, c, wanted)
        wanted = []
    mine, send = acc
    received = lax.ppermute(send, "gy", [(0, 1), (1, 0)])
    return (hidden_rows.astype(F32) + mine + received.astype(F32)).astype(BF16)


def solution(mesh):
    in_specs = (
        P(("grp", "gy"), "gx"),
        P("gx"),
        P("gx", "gy"),
        P("gx", "gy"),
        P("gx", "gy"),
        P("gy"),
        P("gy"),
        P("gy"),
        P(("grp", "gx"), None, "gy"),
        P(("grp", "gx"), None, "gy"),
        P("grp"),
        P("grp"),
        P("gy", "gx"),
    )
    out_specs = P(("grp", "gy"), "gx")
    return jax.shard_map(
        functools.partial(on_device, size=mesh.shape["gx"]),
        mesh=mesh,
        in_specs=in_specs,
        out_specs=out_specs,
        check_vma=False,
    )
```

```python
import functools
import math

import jax
import jax.numpy as jnp
from jax import lax
from jax.experimental import pallas as pl
from jax.experimental.pallas import tpu as pltpu
from jax.sharding import PartitionSpec as P

MODEL_WIDTH = 8192
QUERY_HEADS = 64
KEY_VALUE_HEADS = 8
HEAD_SIZE = 128
QUERIES_PER_KV = QUERY_HEADS // KEY_VALUE_HEADS
TILES = QUERIES_PER_KV + 2
SQUARE_ROWS = 32

EPSILON = 1e-06
ROPE_BASE = 1000000.0
CHUNK_HEADS = (1, 2, 1)
F32 = jnp.float32
BF16 = jnp.bfloat16
MIB = 1024 * 1024
SLOTS_AT_ONCE = {1: 8, 2: 8, 3: 8, 4: 4}
PEAK_FLOP_PER_US = 1.1535e9
COSTS = {'project0': 1.22, 'add_far0': 0.1, 'add_near0_2': 0.1, 'attend0': 1.9, 'join0_1': 0.1, 'join0': 0.1, 'output0': 1.4, 'project1': 1.8, 'add_far1': 0.1, 'add_near1_2': 0.1, 'attend1': 2.35, 'join1_1': 0.1, 'join1': 0.1, 'output1': 2, 'project2': 1.22, 'add_far2': 0.1, 'add_near2_2': 0.1, 'attend2': 1.9, 'join2': 0.1, 'output2': 4}
Y_IN_HALVES = (True, True, True)
GATHER = ('y halved', 'y halved', 'y halved')
ORDER = (
    ("weights", 0),
    ("weights", 1),
    ("project", 0),
    ("project", 1),
    ("far", 0),
    ("weights", 2),
    ("far", 1),
    ("near", 0),
    ("project", 2),
    ("near", 1),
    ("far", 2),
    ("attend", 0),
    ("attend", 1),
    ("near", 2),
    ("gather", 0),
    ("gather", 1),
    ("attend", 2),
    ("forward", 1),
    ("forward", 0),
    ("output", 0),
    ("gather", 2),
    ("forward", 2),
    ("output", 1),
    ("output", 2),
)
F32 = jnp.float32
BF16 = jnp.bfloat16


def neighbour_pairs(nz):
    return [(z * 2 + y, z * 2 + 1 - y) for z in range(nz) for y in range(2)]


def stride_pairs(nz, stride):
    return [(z * 2 + y, (z ^ stride) * 2 + y) for z in range(nz) for y in range(2)]


def strides(nz):
    return [1 << i for i in range(nz.bit_length() - 1)]


def place_order(nz):
    return sorted(range(nz), key=lambda q: [(q & b) != 0 for b in strides(nz)])


def slot_one_hot(place_ref, slot_of_row, nz, per):
    rows = slot_of_row.shape[1]
    base = lax.broadcasted_iota(jnp.int32, (per, rows), 0)
    blocks = []
    for h in range(2):
        for q in place_order(nz):
            owner = (place_ref[0] ^ q) * 2 + (place_ref[1] ^ h)
            blocks.append(jnp.where(base + owner * per == slot_of_row, 1.0, 0.0).astype(F32))
    return jnp.concatenate(blocks, axis=0).astype(BF16)


TOKEN = (8, HEAD_SIZE)


def estimate(name):
    flops = int(COSTS.get(name, 0) * PEAK_FLOP_PER_US)
    return pl.CostEstimate(flops=flops, bytes_accessed=0, transcendentals=0)


def copies_of(sources, windows, targets, sems):
    return [
        pltpu.make_async_copy(source.at[window], target, sems.at[i])
        for i, (source, window, target) in enumerate(zip(sources, windows, targets))
    ]


def call(
    kernel, name, token, scalars, arrays, out_shapes, scratch, vmem_mib, loads=(), resident=()
):
    arrays = list(arrays) + [
        pltpu.with_memory_space_constraint(array, pltpu.VMEM) for array in resident
    ]
    sources = [array for array, _ in loads]
    windows = [window for _, window in loads]
    loaded_shapes = [
        tuple(w.size if isinstance(w, pl.Slice) else n for w, n in zip(window, array.shape))
        for array, window in loads
    ]

    def body(*refs):
        refs = list(refs)
        del refs[0]
        source_refs = [refs.pop(0) for _ in loads]
        in_refs = [refs.pop(0) for _ in range(len(scalars) + len(arrays))]
        token_ref = refs.pop(0)
        target_refs = [refs.pop(0) for _ in loads]
        copies = copies_of(source_refs, windows, target_refs, refs.pop() if loads else None)
        for copy in copies:
            copy.start()
        token_ref[...] = jnp.zeros(TOKEN, F32)
        kernel(*in_refs, *refs)
        for copy in copies:
            copy.wait()

    vmem = pl.BlockSpec(memory_space=pltpu.VMEM)
    outs = pl.pallas_call(
        body,
        in_specs=[vmem]
        + [pl.BlockSpec(memory_space=pltpu.HBM)] * len(loads)
        + [pl.BlockSpec(memory_space=pltpu.SMEM)] * len(scalars)
        + [vmem] * len(arrays),
        out_specs=[vmem] * (1 + len(loads) + len(out_shapes)),
        out_shape=[pltpu.VMEM(TOKEN, F32)]
        + [pltpu.VMEM(shape, array.dtype) for shape, array in zip(loaded_shapes, sources)]
        + [pltpu.VMEM(shape, dtype) for shape, dtype in out_shapes],
        scratch_shapes=list(scratch) + ([pltpu.SemaphoreType.DMA((len(loads),))] if loads else []),
        compiler_params=pltpu.CompilerParams(vmem_limit_bytes=vmem_mib * MIB),
        cost_estimate=estimate(name),
        name=name,
    )(
        token,
        *[pltpu.with_memory_space_constraint(array, pltpu.HBM) for array in sources],
        *scalars,
        *arrays,
    )
    return outs[0], outs[1 : 1 + len(loads)], outs[1 + len(loads) :]


def places_of(refs, per):
    blocks = [(ref, z) for ref in refs for z in range(ref.shape[0])]
    return [(i * per, ref, z) for i, (ref, z) in enumerate(blocks)]


def project_kernel(*refs, nz, per, first, heads):
    place_ref = refs[0]
    if first:
        own_ref, other_ref, gain_ref, sor_ref, wq_ref, wk_ref, wv_ref = refs[1:8]
        *out_refs, slotted_ref, acc = refs[8:]
        places = places_of(out_refs, per)
        one_hot = slot_one_hot(place_ref, sor_ref[...], nz, per)
        own, other = own_ref[...], other_ref[...]
        lower = place_ref[2] == 0
        rows = jnp.concatenate(
            [jnp.where(lower, own, other), jnp.where(lower, other, own)], axis=0
        )
        hidden = jnp.dot(one_hot, rows, preferred_element_type=F32)
        gain = gain_ref[...].astype(F32)
        gain = jnp.concatenate([gain[j : j + 1] for j in range(gain.shape[0])], axis=1)
        slotted_ref[...] = (hidden * gain).astype(BF16)
        squares = jnp.sum(hidden * hidden, axis=1, keepdims=True)
        high = squares.astype(BF16).astype(F32)
        low = squares - high
        lane = lax.broadcasted_iota(jnp.int32, (per, HEAD_SIZE), 1)
        lane_high = place_ref[1] * 2
        for at, ref, z in places:
            packed = jnp.where(
                lane == lane_high,
                high[at : at + per],
                jnp.where(lane == lane_high + 1, low[at : at + per], 0.0),
            )
            packed = jnp.concatenate(
                [packed, jnp.zeros((SQUARE_ROWS - per, HEAD_SIZE), F32)], axis=0
            )
            ref[z, heads * TILES * per :, :] = packed.astype(BF16)
    else:
        slotted_ref, wq_ref, wk_ref, wv_ref = refs[1:5]
        *out_refs, acc = refs[5:]
        places = places_of(out_refs, per)

    columns = QUERIES_PER_KV * HEAD_SIZE
    slotted = slotted_ref[...]
    for g in range(heads):
        acc[:, :columns] = jnp.dot(
            slotted, wq_ref[:, g * columns : (g + 1) * columns], preferred_element_type=F32
        )
        narrow = slice(g * HEAD_SIZE, (g + 1) * HEAD_SIZE)
        acc[:, columns:] = jnp.dot(
            slotted,
            jnp.concatenate([wk_ref[:, narrow], wv_ref[:, narrow]], axis=1),
            preferred_element_type=F32,
        )
        for at, ref, z in places:
            block = jnp.concatenate(
                [
                    acc[at : at + per, c * HEAD_SIZE : (c + 1) * HEAD_SIZE]
                    for c in range(TILES)
                ],
                axis=0,
            )
            ref[z, g * TILES * per : (g + 1) * TILES * per, :] = block.astype(BF16)


def project(token, place, inputs, weights, loads, *, chunk, heads, nz, per):
    first = chunk == 0
    rows = 2 * nz * per
    depth = weights[0].shape[0]
    block_rows = heads * TILES * per + (SQUARE_ROWS if first else 0)
    counts = [nz, nz // 2, nz // 2] if Y_IN_HALVES[chunk] else [nz, nz]
    out_shapes = [((count, block_rows, HEAD_SIZE), BF16) for count in counts]
    return call(
        functools.partial(project_kernel, nz=nz, per=per, first=first, heads=heads),
        "project" + str(chunk),
        token,
        [place],
        [*inputs, *weights],
        out_shapes + ([((rows, depth), BF16)] if first else []),
        [pltpu.VMEM((rows, TILES * HEAD_SIZE), F32)],
        12,
        loads,
    )


def add_kernel(*refs, starts, count):
    terms = len(starts)
    outs = refs[terms:]
    each = outs[0].shape[0]
    for z in range(count):
        total = refs[0][starts[0] + z].astype(F32)
        for ref, start in zip(refs[1:terms], starts[1:]):
            total = total + ref[start + z].astype(F32)
        outs[z // each][z % each] = total.astype(BF16)


def add(name, token, arrays, starts, count, parts):
    shape = (count // parts,) + arrays[0].shape[1:]
    token, _, sums = call(
        functools.partial(add_kernel, starts=starts, count=count),
        name,
        token,
        [],
        arrays,
        [(shape, BF16)] * parts,
        [],
        2,
    )
    return token, sums


def join_kernel(a_ref, b_ref, out_ref):
    count = a_ref.shape[0]
    out_ref[:count] = a_ref[...]
    out_ref[count:] = b_ref[...]


def join(name, token, a, b):
    shape = (a.shape[0] + b.shape[0],) + a.shape[1:]
    token, _, (joined,) = call(join_kernel, name, token, [], [a, b], [(shape, BF16)], [], 2)
    return token, joined


def attend_kernel(*refs, first, heads, per, group, start_head):
    place_ref, lengths_ref, mine_ref, last_ref = refs[:4]
    rest = refs[4:]
    if first:
        qb_ref, kb_ref, vb_ref, cos_ref, sin_ref, k_ref, v_ref, out_ref, scale_ref = rest[:9]
    else:
        scale_in_ref, qb_ref, kb_ref, vb_ref, cos_ref, sin_ref, k_ref, v_ref, out_ref = rest[:9]
    fresh, result = rest[9:]
    body = heads * TILES * per
    head_rows = TILES * per

    if first:
        squares = mine_ref[0, body:, :].astype(F32) + last_ref[0, body:, :].astype(F32)
        total = jnp.sum(squares[:per], axis=1, keepdims=True)
        scale = jnp.broadcast_to(lax.rsqrt(total / MODEL_WIDTH + EPSILON), (per, HEAD_SIZE))
        scale_ref[...] = scale
    else:
        scale = scale_in_ref[...]
    cos, sin = cos_ref[...], sin_ref[...]
    query_bias = qb_ref[...].astype(F32)
    key_bias = kb_ref[...].astype(F32)
    value_bias = vb_ref[...].astype(F32)
    for g in range(heads):
        rows = pl.ds(g * head_rows, head_rows)
        summed = mine_ref[0, rows, :].astype(F32) + last_ref[0, rows, :].astype(F32)
        head = start_head + g
        for c in range(TILES):
            if c < QUERIES_PER_KV:
                at = head * QUERIES_PER_KV + c
                bias = query_bias[at : at + 1]
            else:
                bias = (key_bias if c == QUERIES_PER_KV else value_bias)[head : head + 1]
            tile = summed[c * per : (c + 1) * per] * scale + bias
            if c < TILES - 1:
                tile = tile * cos + pltpu.roll(tile, HEAD_SIZE // 2, 1) * sin
            fresh[pl.ds(g * head_rows + c * per, per), :] = tile.astype(BF16).astype(F32)

    positions = k_ref.shape[1]
    columns = slice(start_head * HEAD_SIZE, (start_head + heads) * HEAD_SIZE)
    qrows = heads * QUERIES_PER_KV
    lanes = group * qrows
    extra = 16
    tile = min(lanes, HEAD_SIZE)
    tile_pairs = tile // QUERIES_PER_KV
    tiles = lanes // tile if lanes % tile == 0 else -(-lanes // tile)
    widths = [min(tile, lanes - t * tile) for t in range(tiles)]
    lane_pairs = [
        lax.broadcasted_iota(jnp.int32, (HEAD_SIZE, width), 1) // QUERIES_PER_KV
        for width in widths
    ]
    top_row = lax.broadcasted_iota(jnp.int32, (extra, HEAD_SIZE), 0) == 0
    lane_slot = lax.broadcasted_iota(jnp.int32, (1, lanes), 1) // qrows
    row = lax.broadcasted_iota(jnp.int32, (positions + extra, lanes), 0)
    base = (place_ref[0] * 2 + place_ref[1]) * per
    for start in range(0, per, group):
        slots = range(start, start + group)
        queries = jnp.concatenate(
            [
                fresh[pl.ds(g * head_rows + s, QUERIES_PER_KV, stride=per), :]
                for s in slots
                for g in range(heads)
            ],
            axis=0,
        )
        turned = queries.T
        query, new_key = [], []
        for i, s in enumerate(slots):
            for g in range(heads):
                pair = i * heads + g
                at, own = divmod(pair, tile_pairs)
                pieces = [jnp.zeros((HEAD_SIZE, width), BF16) for width in widths]
                pieces[at] = jnp.where(
                    lane_pairs[at] == own, turned[:, at * tile : at * tile + widths[at]], 0.0
                ).astype(BF16)
                query.append(jnp.concatenate(pieces, axis=1))
                key = fresh[pl.ds(g * head_rows + QUERIES_PER_KV * per + s, 1), :]
                new_key.append(jnp.where(top_row, key, 0.0).astype(BF16))
        keys = jnp.concatenate(
            [
                jnp.concatenate([k_ref[s, :, columns] for s in slots], axis=1),
                jnp.concatenate(new_key, axis=1),
            ],
            axis=0,
        )
        scores = jnp.dot(keys, jnp.concatenate(query, axis=0), preferred_element_type=F32)

        lengths = jnp.zeros((1, lanes), jnp.int32)
        for i, s in enumerate(slots):
            lengths = jnp.where(lane_slot == i, lengths_ref[base + s], lengths)
        valid = (row < lengths) | (row == positions)
        scores = jnp.where(valid, scores * (1.0 / math.sqrt(HEAD_SIZE)), -1e30)
        top = jnp.max(scores, axis=0, keepdims=True)
        exps = jnp.where(valid, jnp.exp(scores - top), 0.0)
        weights = exps * (1.0 / jnp.sum(exps, axis=0, keepdims=True))
        cache_weights = weights[:positions].T
        own_weights = weights[positions : positions + 8].T[:, 0:1].astype(BF16).astype(F32)
        spread = []
        for i in range(group):
            lo, hi = i * qrows, (i + 1) * qrows
            low, high = lo // 16 * 16, -(-hi // 16) * 16
            rows = [
                jnp.zeros((lo - low, positions), F32),
                cache_weights[lo:hi],
                jnp.zeros((high - hi, positions), F32),
            ]
            rows = jnp.concatenate([r for r in rows if r.shape[0]], axis=0).astype(BF16)
            blocks = [
                jnp.zeros((low, positions), BF16), rows, jnp.zeros((lanes - high, positions), BF16),
            ]
            spread.append(jnp.concatenate([r for r in blocks if r.shape[0]], axis=0))
        spread = jnp.concatenate(spread, axis=1)
        values = v_ref[start : start + group, :, columns].reshape(group * positions, heads * HEAD_SIZE)
        mixed = jnp.dot(spread, values, preferred_element_type=F32)
        for i, s in enumerate(slots):
            for g in range(heads):
                lo = i * qrows + g * QUERIES_PER_KV
                hi = lo + QUERIES_PER_KV
                new_value = fresh[pl.ds(g * head_rows + (QUERIES_PER_KV + 1) * per + s, 1), :]
                result[pl.ds(g * QUERIES_PER_KV * per + s, QUERIES_PER_KV, stride=per), :] = (
                    mixed[lo:hi, g * HEAD_SIZE : (g + 1) * HEAD_SIZE]
                    + own_weights[lo:hi] * new_value
                )
    out_ref[0] = result[...].astype(BF16)


def attend(
    token, place, lengths, parts, scale, biases, cos, sin, keys, values, loads, *, chunk, heads
):
    first = chunk == 0
    per = keys.shape[0]
    out_rows = heads * QUERIES_PER_KV * per
    return call(
        functools.partial(
            attend_kernel,
            first=first,
            heads=heads,
            per=per,
            group=SLOTS_AT_ONCE[heads],
            start_head=sum(CHUNK_HEADS[:chunk]),
        ),
        "attend" + str(chunk),
        token,
        [place, lengths],
        list(parts) + ([] if first else [scale]) + list(biases) + [cos, sin],
        [((1, out_rows, HEAD_SIZE), BF16)] + ([((per, HEAD_SIZE), F32)] if first else []),
        [
            pltpu.VMEM((heads * TILES * per, HEAD_SIZE), F32),
            pltpu.VMEM((out_rows, HEAD_SIZE), F32),
        ],
        8,
        loads,
        [keys, values],
    )


def output_kernel(*refs, labels, nz, per, first, last, start_depth):
    count = len(labels)
    place_ref, block_refs, order_ref = refs[0], refs[1 : 1 + count], refs[1 + count]
    rest = refs[2 + count :]
    if not first:
        acc_in_ref, rest = rest[0], rest[1:]
    w_ref, rest = rest[0], rest[1:]
    if last:
        mine_ref, send_ref, stacked = rest
    else:
        acc_out_ref, *rest, stacked = rest
    tiles = block_refs[0].shape[1] // per
    depth = tiles * HEAD_SIZE

    if first:
        slot_of_row = order_ref[...]
        half = slot_of_row.shape[1] // 2
        swapped = jnp.concatenate([slot_of_row[:, half:], slot_of_row[:, :half]], axis=1)
        slot_of_row = jnp.where(place_ref[2] == 0, slot_of_row, swapped)
        one_hot = slot_one_hot(place_ref, slot_of_row, nz, per).astype(F32).T.astype(BF16)
        rest[0][...] = one_hot
    else:
        one_hot = order_ref[...]
    wide = {
        label: ref[z].astype(F32)
        for ref, own in zip(block_refs, labels)
        for z, label in enumerate(own)
    }
    wide = [wide[h, q] for h in range(2) for q in place_order(nz)]
    for c in range(tiles):
        stacked[:, c * HEAD_SIZE : (c + 1) * HEAD_SIZE] = jnp.concatenate(
            [block[c * per : (c + 1) * per] for block in wide], axis=0
        ).astype(BF16)
    stacked[...] = jnp.dot(one_hot, stacked[...], preferred_element_type=F32).astype(BF16)
    product = jnp.dot(
        stacked[...], w_ref[start_depth : start_depth + depth, :], preferred_element_type=F32
    )
    if not first:
        product = product + acc_in_ref[...]
    if last:
        half = product.shape[0] // 2
        mine_ref[...] = product[:half]
        send_ref[...] = product[half:].astype(BF16)
    else:
        acc_out_ref[...] = product


def output(token, place, blocks, labels, order, w_out, acc, loads, *, chunk, chunks, nz, per):
    first, last = chunk == 0, chunk == chunks - 1
    rows = 2 * nz * per
    width = w_out.shape[1]
    depth = CHUNK_HEADS[chunk] * QUERIES_PER_KV * HEAD_SIZE
    if last:
        out_shapes = [((rows // 2, width), F32), ((rows // 2, width), BF16)]
    else:
        out_shapes = [((rows, width), F32)] + ([((rows, rows), BF16)] if first else [])
    return call(
        functools.partial(
            output_kernel,
            labels=labels,
            nz=nz,
            per=per,
            first=first,
            last=last,
            start_depth=sum(CHUNK_HEADS[:chunk]) * QUERIES_PER_KV * HEAD_SIZE,
        ),
        "output" + str(chunk),
        token,
        [place],
        [*blocks, order] + ([] if first else [acc]),
        out_shapes,
        [pltpu.VMEM((rows, depth), BF16)],
        12,
        loads,
        [w_out],
    )


def on_device(
    hidden_rows,
    norm_gain,
    w_query,
    key_weight,
    value_weight,
    query_bias,
    key_bias_vector,
    value_bias_vector,
    rotated_key_cache,
    stored_value_cache,
    slot_valid_lengths,
    slot_of_row,
    w_out,
    *,
    size,
):
    nz = size // 2
    assert size % 2 == 0 and nz & (nz - 1) == 0 and nz > 2
    per = rotated_key_cache.shape[0]
    kv_heads = key_weight.shape[1] // HEAD_SIZE
    assert sum(CHUNK_HEADS) == kv_heads and per % SLOTS_AT_ONCE[1] == 0
    chunks = len(CHUNK_HEADS)
    gx = lax.axis_index("gx")
    gy = lax.axis_index("gy")
    place = jnp.stack([gx // 2, gx % 2, gy]).astype(jnp.int32)

    other = lax.ppermute(hidden_rows, "gy", [(0, 1), (1, 0)])
    sor = slot_of_row[None, :]
    gain = norm_gain.reshape(-1, HEAD_SIZE)

    lengths = lax.dynamic_slice_in_dim(slot_valid_lengths, gx * per, per, 0)
    lane = jnp.arange(HEAD_SIZE)
    half_width = HEAD_SIZE // 2
    frequency = ROPE_BASE ** (-((lane % half_width).astype(F32) * 2.0 / HEAD_SIZE))
    angles = lengths.astype(F32)[:, None] * frequency[None, :]
    cos = jnp.cos(angles)
    sin = jnp.sin(angles) * jnp.where(lane < half_width, -1.0, 1.0)[None, :]
    biases = [b.reshape(-1, HEAD_SIZE) for b in (query_bias, key_bias_vector, value_bias_vector)]

    def head_window(c, width):
        return pl.ds(sum(CHUNK_HEADS[:c]) * width, CHUNK_HEADS[c] * width)

    wide = QUERIES_PER_KV * HEAD_SIZE
    everything = pl.ds(0, w_query.shape[0])
    positions = rotated_key_cache.shape[1]
    all_columns = pl.ds(0, w_out.shape[1])
    same_z = neighbour_pairs(nz)
    scale = acc = None
    order = sor
    inputs = [hidden_rows, other, gain, sor]
    kept, swapped, reduced = {}, {}, {}
    loaded, gathered, waiting = {}, {}, {}

    def over_y(blocks, labels):
        return lax.ppermute(blocks, "gx", same_z), [(1 - h, q) for h, q in labels]

    def over_z(blocks, labels, stride):
        moved = lax.ppermute(blocks, "gx", stride_pairs(nz, stride))
        return moved, [(h, q ^ stride) for h, q in labels]

    def windows_of(kind, c):
        return [
            (array, (everything, head_window(c, n)))
            for array, n in ((w_query, wide), (key_weight, HEAD_SIZE), (value_weight, HEAD_SIZE))
        ]

    def file_loaded(wanted, arrays):
        arrays = list(arrays)
        for kind, c in wanted:
            loaded[kind, c] = [arrays.pop(0) for _ in windows_of(kind, c)]

    def loads_of(wanted):
        return [pair for kind, c in wanted for pair in windows_of(kind, c)]

    def do_load(token, wanted):
        name = "load" + "".join("_" + kind + str(c) for kind, c in wanted)
        token, arrays, _ = call(lambda: None, name, token, [], [], [], [], 1, loads_of(wanted))
        file_loaded(wanted, arrays)
        return token

    def do_project(token, c, wanted):
        nonlocal inputs
        token, arrays, outs = project(
            token, place, inputs, loaded["weights", c], loads_of(wanted),
            chunk=c, heads=CHUNK_HEADS[c], nz=nz, per=per,
        )
        file_loaded(wanted, arrays)
        kept[c] = outs[0]
        if c == 0:
            inputs = [outs[-1]]
        if Y_IN_HALVES[c]:
            far = lax.ppermute(outs[2], "gx", same_z)
            swapped[c] = (lax.ppermute(outs[1], "gx", same_z), 0), (far, 0)
        else:
            both = lax.ppermute(outs[1], "gx", same_z)
            swapped[c] = (both, 0), (both, nz // 2)
        return token

    def do_far(token, c, wanted):
        half = nz // 2
        token, (total,) = add(
            "add_far" + str(c), token, [kept[c], swapped[c][1][0]], [half, swapped[c][1][1]], half, 1
        )
        reduced[c] = lax.ppermute(total, "gx", stride_pairs(nz, 1))
        return token

    def do_near(token, c, wanted):
        terms, starts, count = [kept[c], swapped[c][0][0], reduced[c]], [0, 0, 0], nz // 2
        for stride in strides(nz)[1:]:
            token, (mine, sent) = add(
                "add_near" + str(c) + "_" + str(stride), token, terms, starts, count, 2
            )
            terms = [mine, lax.ppermute(sent, "gx", stride_pairs(nz, stride))]
            starts, count = [0, 0], count // 2
        reduced[c] = terms
        return token

    def do_attend(token, c, wanted):
        nonlocal scale
        token, arrays, outs = attend(
            token, place, slot_valid_lengths, reduced[c], scale, biases, cos, sin, rotated_key_cache, stored_value_cache,
            loads_of(wanted), chunk=c, heads=CHUNK_HEADS[c],
        )
        file_loaded(wanted, arrays)
        if c == 0:
            scale = outs[1]
        own = outs[0], [(0, 0)]
        first_move = over_y(*own) if GATHER[c] == "y first" else over_z(*own, strides(nz)[-1])
        waiting[c] = own, first_move
        return token

    def do_gather(token, c, wanted):
        held, moved = waiting[c]
        for stride in reversed(strides(nz) if GATHER[c] == "y first" else strides(nz)[:-1]):
            if GATHER[c] == "y first" and stride == 1:
                break
            token, joined = join("join" + str(c) + "_" + str(stride), token, held[0], moved[0])
            held = joined, held[1] + moved[1]
            moved = over_z(*held, stride)
        waiting[c] = held, moved
        gathered[c] = [held, moved]
        if GATHER[c] == "y halved":
            gathered[c].append(over_y(*held))
        return token

    def do_forward(token, c, wanted):
        held, moved = waiting[c]
        if GATHER[c] == "y halved":
            gathered[c].append(over_y(*moved))
            return token
        token, joined = join("join" + str(c), token, held[0], moved[0])
        held = joined, held[1] + moved[1]
        gathered[c] = [held, over_z(*held, 1) if GATHER[c] == "y first" else over_y(*held)]
        return token

    def do_output(token, c, wanted):
        nonlocal acc, order
        token, arrays, outs = output(
            token, place, [a for a, _ in gathered[c]], [own for _, own in gathered[c]], order,
            w_out, acc, loads_of(wanted),
            chunk=c, chunks=chunks, nz=nz, per=per,
        )
        file_loaded(wanted, arrays)
        acc = outs[0]
        if c == 0:
            order = outs[1]
        if c == chunks - 1:
            acc = outs
        return token

    token = jnp.zeros(TOKEN, F32)
    steps = {
        "project": do_project,
        "far": do_far,
        "near": do_near,
        "attend": do_attend,
        "gather": do_gather,
        "forward": do_forward,
        "output": do_output,
    }
    needs = {"project": "weights", "attend": "caches", "output": "out"}
    wanted = []
    for step, c in ORDER:
        if step not in steps:
            wanted.append((step, c))
            continue
        if step not in needs or (needs[step], c) in wanted:
            if wanted:
                token = do_load(token, wanted)
            wanted = []
        token = steps[step](token, c, wanted)
        wanted = []
    mine, send = acc
    received = lax.ppermute(send, "gy", [(0, 1), (1, 0)])
    return (hidden_rows.astype(F32) + mine + received.astype(F32)).astype(BF16)


def solution(mesh):
    in_specs = (
        P(("grp", "gy"), "gx"),
        P("gx"),
        P("gx", "gy"),
        P("gx", "gy"),
        P("gx", "gy"),
        P("gy"),
        P("gy"),
        P("gy"),
        P(("grp", "gx"), None, "gy"),
        P(("grp", "gx"), None, "gy"),
        P("grp"),
        P("grp"),
        P("gy", "gx"),
    )
    out_specs = P(("grp", "gy"), "gx")
    return jax.shard_map(
        functools.partial(on_device, size=mesh.shape["gx"]),
        mesh=mesh,
        in_specs=in_specs,
        out_specs=out_specs,
        check_vma=False,
    )
```

```python
import functools
import math

import jax
import jax.numpy as jnp
from jax import lax
from jax.experimental import pallas as pl
from jax.experimental.pallas import tpu as pltpu
from jax.sharding import PartitionSpec as P

MODEL_WIDTH = 8192
QUERY_HEADS = 64
KEY_VALUE_HEADS = 8
HEAD_SIZE = 128
QUERIES_PER_KV = QUERY_HEADS // KEY_VALUE_HEADS
TILES = QUERIES_PER_KV + 2
SQUARE_ROWS = 32

EPSILON = 1e-06
ROPE_BASE = 1000000.0
CHUNK_HEADS = (1, 2, 1)
F32 = jnp.float32
BF16 = jnp.bfloat16
MIB = 1024 * 1024
SLOTS_AT_ONCE = {1: 24, 2: 8, 3: 8, 4: 4}
PEAK_FLOP_PER_US = 1.1535e9
COSTS = {'attend0': 2, 'output0': 16, 'project1': 1, 'join1': 4, 'output1': 4, 'project2': 1, 'attend2': 4, 'join2': 8, 'join0_1': 4, 'add_near2_2': 1, 'join1_1': 0.3, 'project0': 16, 'output2': 16}
Y_IN_HALVES = (True, True, True)
GATHER = ('y halved', 'y halved', 'y halved')
ORDER = (
    ("weights", 0),
    ("weights", 1),
    ("project", 0),
    ("project", 1),
    ("weights", 2),
    ("far", 0),
    ("far", 1),
    ("project", 2),
    ("near", 0),
    ("near", 1),
    ("far", 2),
    ("attend", 0),
    ("attend", 1),
    ("near", 2),
    ("gather", 0),
    ("gather", 1),
    ("forward", 0),
    ("attend", 2),
    ("forward", 1),
    ("output", 0),
    ("gather", 2),
    ("forward", 2),
    ("output", 1),
    ("output", 2),
)
F32 = jnp.float32
BF16 = jnp.bfloat16


def neighbour_pairs(nz):
    return [(z * 2 + y, z * 2 + 1 - y) for z in range(nz) for y in range(2)]


def stride_pairs(nz, stride):
    return [(z * 2 + y, (z ^ stride) * 2 + y) for z in range(nz) for y in range(2)]


def strides(nz):
    return [1 << i for i in range(nz.bit_length() - 1)]


def place_order(nz):
    return sorted(range(nz), key=lambda q: [(q & b) != 0 for b in strides(nz)])


def slot_one_hot(place_ref, slot_of_row, nz, per):
    rows = slot_of_row.shape[1]
    base = lax.broadcasted_iota(jnp.int32, (per, rows), 0)
    blocks = []
    for h in range(2):
        for q in place_order(nz):
            owner = (place_ref[0] ^ q) * 2 + (place_ref[1] ^ h)
            blocks.append(jnp.where(base + owner * per == slot_of_row, 1.0, 0.0).astype(F32))
    return jnp.concatenate(blocks, axis=0).astype(BF16)


TOKEN = (8, HEAD_SIZE)


def estimate(name):
    flops = int(COSTS.get(name, 0) * PEAK_FLOP_PER_US)
    return pl.CostEstimate(flops=flops, bytes_accessed=0, transcendentals=0)


def copies_of(sources, windows, targets, sems):
    return [
        pltpu.make_async_copy(source.at[window], target, sems.at[i])
        for i, (source, window, target) in enumerate(zip(sources, windows, targets))
    ]


def call(
    kernel, name, token, scalars, arrays, out_shapes, scratch, vmem_mib, loads=(), resident=()
):
    arrays = list(arrays) + [
        pltpu.with_memory_space_constraint(array, pltpu.VMEM) for array in resident
    ]
    sources = [array for array, _ in loads]
    windows = [window for _, window in loads]
    loaded_shapes = [
        tuple(w.size if isinstance(w, pl.Slice) else n for w, n in zip(window, array.shape))
        for array, window in loads
    ]

    def body(*refs):
        refs = list(refs)
        del refs[0]
        source_refs = [refs.pop(0) for _ in loads]
        in_refs = [refs.pop(0) for _ in range(len(scalars) + len(arrays))]
        token_ref = refs.pop(0)
        target_refs = [refs.pop(0) for _ in loads]
        copies = copies_of(source_refs, windows, target_refs, refs.pop() if loads else None)
        for copy in copies:
            copy.start()
        token_ref[...] = jnp.zeros(TOKEN, F32)
        kernel(*in_refs, *refs)
        for copy in copies:
            copy.wait()

    vmem = pl.BlockSpec(memory_space=pltpu.VMEM)
    outs = pl.pallas_call(
        body,
        in_specs=[vmem]
        + [pl.BlockSpec(memory_space=pltpu.HBM)] * len(loads)
        + [pl.BlockSpec(memory_space=pltpu.SMEM)] * len(scalars)
        + [vmem] * len(arrays),
        out_specs=[vmem] * (1 + len(loads) + len(out_shapes)),
        out_shape=[pltpu.VMEM(TOKEN, F32)]
        + [pltpu.VMEM(shape, array.dtype) for shape, array in zip(loaded_shapes, sources)]
        + [pltpu.VMEM(shape, dtype) for shape, dtype in out_shapes],
        scratch_shapes=list(scratch) + ([pltpu.SemaphoreType.DMA((len(loads),))] if loads else []),
        compiler_params=pltpu.CompilerParams(vmem_limit_bytes=vmem_mib * MIB),
        cost_estimate=estimate(name),
        name=name,
    )(
        token,
        *[pltpu.with_memory_space_constraint(array, pltpu.HBM) for array in sources],
        *scalars,
        *arrays,
    )
    return outs[0], outs[1 : 1 + len(loads)], outs[1 + len(loads) :]


def places_of(refs, per):
    blocks = [(ref, z) for ref in refs for z in range(ref.shape[0])]
    return [(i * per, ref, z) for i, (ref, z) in enumerate(blocks)]


def project_kernel(*refs, nz, per, first, heads):
    place_ref = refs[0]
    if first:
        own_ref, other_ref, gain_ref, sor_ref, wq_ref, wk_ref, wv_ref = refs[1:8]
        *out_refs, slotted_ref, acc = refs[8:]
        places = places_of(out_refs, per)
        one_hot = slot_one_hot(place_ref, sor_ref[...], nz, per)
        own, other = own_ref[...], other_ref[...]
        lower = place_ref[2] == 0
        rows = jnp.concatenate(
            [jnp.where(lower, own, other), jnp.where(lower, other, own)], axis=0
        )
        hidden = jnp.dot(one_hot, rows, preferred_element_type=F32)
        gain = gain_ref[...].astype(F32)
        gain = jnp.concatenate([gain[j : j + 1] for j in range(gain.shape[0])], axis=1)
        slotted_ref[...] = (hidden * gain).astype(BF16)
        squares = jnp.sum(hidden * hidden, axis=1, keepdims=True)
        high = squares.astype(BF16).astype(F32)
        low = squares - high
        lane = lax.broadcasted_iota(jnp.int32, (per, HEAD_SIZE), 1)
        lane_high = (place_ref[0] * 2 + place_ref[1]) * 2
        for at, ref, z in places:
            packed = jnp.where(
                lane == lane_high,
                high[at : at + per],
                jnp.where(lane == lane_high + 1, low[at : at + per], 0.0),
            )
            packed = jnp.concatenate(
                [packed, jnp.zeros((SQUARE_ROWS - per, HEAD_SIZE), F32)], axis=0
            )
            ref[z, heads * TILES * per :, :] = packed.astype(BF16)
    else:
        slotted_ref, wq_ref, wk_ref, wv_ref = refs[1:5]
        *out_refs, acc = refs[5:]
        places = places_of(out_refs, per)

    columns = QUERIES_PER_KV * HEAD_SIZE
    slotted = slotted_ref[...]
    for g in range(heads):
        acc[:, :columns] = jnp.dot(
            slotted, wq_ref[:, g * columns : (g + 1) * columns], preferred_element_type=F32
        )
        narrow = slice(g * HEAD_SIZE, (g + 1) * HEAD_SIZE)
        acc[:, columns:] = jnp.dot(
            slotted,
            jnp.concatenate([wk_ref[:, narrow], wv_ref[:, narrow]], axis=1),
            preferred_element_type=F32,
        )
        for at, ref, z in places:
            block = jnp.concatenate(
                [
                    acc[at : at + per, c * HEAD_SIZE : (c + 1) * HEAD_SIZE]
                    for c in range(TILES)
                ],
                axis=0,
            )
            ref[z, g * TILES * per : (g + 1) * TILES * per, :] = block.astype(BF16)


def project(token, place, inputs, weights, loads, *, chunk, heads, nz, per):
    first = chunk == 0
    rows = 2 * nz * per
    depth = weights[0].shape[0]
    block_rows = heads * TILES * per + (SQUARE_ROWS if first else 0)
    counts = [nz, nz // 2, nz // 2] if Y_IN_HALVES[chunk] else [nz, nz]
    out_shapes = [((count, block_rows, HEAD_SIZE), BF16) for count in counts]
    return call(
        functools.partial(project_kernel, nz=nz, per=per, first=first, heads=heads),
        "project" + str(chunk),
        token,
        [place],
        [*inputs, *weights],
        out_shapes + ([((rows, depth), BF16)] if first else []),
        [pltpu.VMEM((rows, TILES * HEAD_SIZE), F32)],
        12,
        loads,
    )


def add_kernel(*refs, starts, count):
    terms = len(starts)
    outs = refs[terms:]
    each = outs[0].shape[0]
    for z in range(count):
        total = refs[0][starts[0] + z].astype(F32)
        for ref, start in zip(refs[1:terms], starts[1:]):
            total = total + ref[start + z].astype(F32)
        outs[z // each][z % each] = total.astype(BF16)


def add(name, token, arrays, starts, count, parts):
    shape = (count // parts,) + arrays[0].shape[1:]
    token, _, sums = call(
        functools.partial(add_kernel, starts=starts, count=count),
        name,
        token,
        [],
        arrays,
        [(shape, BF16)] * parts,
        [],
        2,
    )
    return token, sums


def join_kernel(a_ref, b_ref, out_ref):
    count = a_ref.shape[0]
    out_ref[:count] = a_ref[...]
    out_ref[count:] = b_ref[...]


def join(name, token, a, b):
    shape = (a.shape[0] + b.shape[0],) + a.shape[1:]
    token, _, (joined,) = call(join_kernel, name, token, [], [a, b], [(shape, BF16)], [], 2)
    return token, joined


def attend_kernel(*refs, first, heads, per, group, start_head):
    place_ref, lengths_ref, mine_ref, last_ref = refs[:4]
    rest = refs[4:]
    if first:
        qb_ref, kb_ref, vb_ref, cos_ref, sin_ref, k_ref, v_ref, out_ref, scale_ref = rest[:9]
    else:
        scale_in_ref, qb_ref, kb_ref, vb_ref, cos_ref, sin_ref, k_ref, v_ref, out_ref = rest[:9]
    fresh, result = rest[9:]
    body = heads * TILES * per
    head_rows = TILES * per

    if first:
        squares = mine_ref[0, body:, :].astype(F32) + last_ref[0, body:, :].astype(F32)
        total = jnp.sum(squares[:per], axis=1, keepdims=True)
        scale = jnp.broadcast_to(lax.rsqrt(total / MODEL_WIDTH + EPSILON), (per, HEAD_SIZE))
        scale_ref[...] = scale
    else:
        scale = scale_in_ref[...]
    cos, sin = cos_ref[...], sin_ref[...]
    query_bias = qb_ref[...].astype(F32)
    key_bias = kb_ref[...].astype(F32)
    value_bias = vb_ref[...].astype(F32)
    for g in range(heads):
        rows = pl.ds(g * head_rows, head_rows)
        summed = mine_ref[0, rows, :].astype(F32) + last_ref[0, rows, :].astype(F32)
        head = start_head + g
        for c in range(TILES):
            if c < QUERIES_PER_KV:
                at = head * QUERIES_PER_KV + c
                bias = query_bias[at : at + 1]
            else:
                bias = (key_bias if c == QUERIES_PER_KV else value_bias)[head : head + 1]
            tile = summed[c * per : (c + 1) * per] * scale + bias
            if c < TILES - 1:
                tile = tile * cos + pltpu.roll(tile, HEAD_SIZE // 2, 1) * sin
            fresh[pl.ds(g * head_rows + c * per, per), :] = tile.astype(BF16).astype(F32)

    positions = k_ref.shape[1]
    columns = slice(start_head * HEAD_SIZE, (start_head + heads) * HEAD_SIZE)
    qrows = heads * QUERIES_PER_KV
    lanes = group * qrows
    extra = 16
    tile = min(lanes, HEAD_SIZE)
    tile_pairs = tile // QUERIES_PER_KV
    tiles = lanes // tile if lanes % tile == 0 else -(-lanes // tile)
    widths = [min(tile, lanes - t * tile) for t in range(tiles)]
    lane_pairs = [
        lax.broadcasted_iota(jnp.int32, (HEAD_SIZE, width), 1) // QUERIES_PER_KV
        for width in widths
    ]
    top_row = lax.broadcasted_iota(jnp.int32, (extra, HEAD_SIZE), 0) == 0
    lane_slot = lax.broadcasted_iota(jnp.int32, (1, lanes), 1) // qrows
    row = lax.broadcasted_iota(jnp.int32, (positions + extra, lanes), 0)
    base = (place_ref[0] * 2 + place_ref[1]) * per
    for start in range(0, per, group):
        slots = range(start, start + group)
        queries = jnp.concatenate(
            [
                fresh[pl.ds(g * head_rows + s, QUERIES_PER_KV, stride=per), :]
                for s in slots
                for g in range(heads)
            ],
            axis=0,
        )
        turned = queries.T
        query, new_key = [], []
        for i, s in enumerate(slots):
            for g in range(heads):
                pair = i * heads + g
                at, own = divmod(pair, tile_pairs)
                pieces = [jnp.zeros((HEAD_SIZE, width), BF16) for width in widths]
                pieces[at] = jnp.where(
                    lane_pairs[at] == own, turned[:, at * tile : at * tile + widths[at]], 0.0
                ).astype(BF16)
                query.append(jnp.concatenate(pieces, axis=1))
                key = fresh[pl.ds(g * head_rows + QUERIES_PER_KV * per + s, 1), :]
                new_key.append(jnp.where(top_row, key, 0.0).astype(BF16))
        keys = jnp.concatenate(
            [
                jnp.concatenate([k_ref[s, :, columns] for s in slots], axis=1),
                jnp.concatenate(new_key, axis=1),
            ],
            axis=0,
        )
        scores = jnp.dot(keys, jnp.concatenate(query, axis=0), preferred_element_type=F32)

        lengths = jnp.zeros((1, lanes), jnp.int32)
        for i, s in enumerate(slots):
            lengths = jnp.where(lane_slot == i, lengths_ref[base + s], lengths)
        valid = (row < lengths) | (row == positions)
        scores = jnp.where(valid, scores * (1.0 / math.sqrt(HEAD_SIZE)), -1e30)
        top = jnp.max(scores, axis=0, keepdims=True)
        exps = jnp.where(valid, jnp.exp(scores - top), 0.0)
        weights = exps * (1.0 / jnp.sum(exps, axis=0, keepdims=True))
        cache_weights = weights[:positions].T
        own_weights = weights[positions : positions + 8].T[:, 0:1].astype(BF16).astype(F32)
        spread = []
        for i in range(group):
            lo, hi = i * qrows, (i + 1) * qrows
            low, high = lo // 16 * 16, -(-hi // 16) * 16
            rows = [
                jnp.zeros((lo - low, positions), F32),
                cache_weights[lo:hi],
                jnp.zeros((high - hi, positions), F32),
            ]
            rows = jnp.concatenate([r for r in rows if r.shape[0]], axis=0).astype(BF16)
            blocks = [
                jnp.zeros((low, positions), BF16), rows, jnp.zeros((lanes - high, positions), BF16),
            ]
            spread.append(jnp.concatenate([r for r in blocks if r.shape[0]], axis=0))
        spread = jnp.concatenate(spread, axis=1)
        values = v_ref[start : start + group, :, columns].reshape(group * positions, heads * HEAD_SIZE)
        mixed = jnp.dot(spread, values, preferred_element_type=F32)
        for i, s in enumerate(slots):
            for g in range(heads):
                lo = i * qrows + g * QUERIES_PER_KV
                hi = lo + QUERIES_PER_KV
                new_value = fresh[pl.ds(g * head_rows + (QUERIES_PER_KV + 1) * per + s, 1), :]
                result[pl.ds(g * QUERIES_PER_KV * per + s, QUERIES_PER_KV, stride=per), :] = (
                    mixed[lo:hi, g * HEAD_SIZE : (g + 1) * HEAD_SIZE]
                    + own_weights[lo:hi] * new_value
                )
    out_ref[0] = result[...].astype(BF16)


def attend(
    token, place, lengths, parts, scale, biases, cos, sin, keys, values, loads, *, chunk, heads
):
    first = chunk == 0
    per = keys.shape[0]
    out_rows = heads * QUERIES_PER_KV * per
    return call(
        functools.partial(
            attend_kernel,
            first=first,
            heads=heads,
            per=per,
            group=SLOTS_AT_ONCE[heads],
            start_head=sum(CHUNK_HEADS[:chunk]),
        ),
        "attend" + str(chunk),
        token,
        [place, lengths],
        list(parts) + ([] if first else [scale]) + list(biases) + [cos, sin],
        [((1, out_rows, HEAD_SIZE), BF16)] + ([((per, HEAD_SIZE), F32)] if first else []),
        [
            pltpu.VMEM((heads * TILES * per, HEAD_SIZE), F32),
            pltpu.VMEM((out_rows, HEAD_SIZE), F32),
        ],
        8,
        loads,
        [keys, values],
    )


def output_kernel(*refs, labels, nz, per, first, last, start_depth):
    count = len(labels)
    place_ref, block_refs, order_ref = refs[0], refs[1 : 1 + count], refs[1 + count]
    rest = refs[2 + count :]
    if not first:
        acc_in_ref, rest = rest[0], rest[1:]
    w_ref, rest = rest[0], rest[1:]
    if last:
        send_ref, stacked = rest
    else:
        acc_out_ref, *rest, stacked = rest
    tiles = block_refs[0].shape[1] // per
    depth = tiles * HEAD_SIZE

    if first:
        slot_of_row = order_ref[...]
        half = slot_of_row.shape[1] // 2
        swapped = jnp.concatenate([slot_of_row[:, half:], slot_of_row[:, :half]], axis=1)
        slot_of_row = jnp.where(place_ref[2] == 0, slot_of_row, swapped)
        one_hot = slot_one_hot(place_ref, slot_of_row, nz, per).astype(F32).T.astype(BF16)
        rest[0][...] = one_hot
    else:
        one_hot = order_ref[...]
    wide = {
        label: ref[z].astype(F32)
        for ref, own in zip(block_refs, labels)
        for z, label in enumerate(own)
    }
    wide = [wide[h, q] for h in range(2) for q in place_order(nz)]
    for c in range(tiles):
        stacked[:, c * HEAD_SIZE : (c + 1) * HEAD_SIZE] = jnp.concatenate(
            [block[c * per : (c + 1) * per] for block in wide], axis=0
        ).astype(BF16)
    if last:
        half = one_hot.shape[0] // 2
        one_hot, acc = one_hot[half:], acc_in_ref[half:]
    permuted = jnp.dot(one_hot, stacked[...], preferred_element_type=F32).astype(BF16)
    product = jnp.dot(
        permuted, w_ref[start_depth : start_depth + depth, :], preferred_element_type=F32
    )
    if last:
        send_ref[...] = (product + acc).astype(BF16)
    elif first:
        acc_out_ref[...] = product
    else:
        acc_out_ref[...] = product + acc_in_ref[...]


def own_output_kernel(
    stacked_ref, order_ref, acc_ref, hidden_ref, w_ref, mine_ref, *, start_depth
):
    half = mine_ref.shape[0]
    depth = stacked_ref.shape[1]
    permuted = jnp.dot(order_ref[:half], stacked_ref[...], preferred_element_type=F32)
    product = jnp.dot(
        permuted.astype(BF16),
        w_ref[start_depth : start_depth + depth, :],
        preferred_element_type=F32,
    )
    mine_ref[...] = hidden_ref[...].astype(F32) + (product + acc_ref[:half])


def output(token, place, blocks, labels, order, w_out, acc, loads, *, chunk, chunks, nz, per):
    first, last = chunk == 0, chunk == chunks - 1
    rows = 2 * nz * per
    width = w_out.shape[1]
    depth = CHUNK_HEADS[chunk] * QUERIES_PER_KV * HEAD_SIZE
    if last:
        out_shapes = [((rows // 2, width), BF16), ((rows, depth), BF16)]
    else:
        out_shapes = [((rows, width), F32)] + ([((rows, rows), BF16)] if first else [])
    return call(
        functools.partial(
            output_kernel,
            labels=labels,
            nz=nz,
            per=per,
            first=first,
            last=last,
            start_depth=sum(CHUNK_HEADS[:chunk]) * QUERIES_PER_KV * HEAD_SIZE,
        ),
        "output" + str(chunk),
        token,
        [place],
        [*blocks, order] + ([] if first else [acc]),
        out_shapes,
        [] if last else [pltpu.VMEM((rows, depth), BF16)],
        12,
        loads,
        [w_out],
    )


def own_output(token, stacked, order, acc, hidden, w_out, *, chunk):
    start = sum(CHUNK_HEADS[:chunk]) * QUERIES_PER_KV * HEAD_SIZE
    token, _, (mine,) = call(
        functools.partial(own_output_kernel, start_depth=start),
        "own_output",
        token,
        [],
        [stacked, order, acc, hidden],
        [(hidden.shape, F32)],
        [],
        12,
        (),
        [w_out],
    )
    return token, mine


def on_device(
    hidden_rows,
    norm_gain,
    w_query,
    key_weight,
    value_weight,
    query_bias,
    key_bias_vector,
    value_bias_vector,
    rotated_key_cache,
    stored_value_cache,
    slot_valid_lengths,
    slot_of_row,
    w_out,
    *,
    size,
):
    nz = size // 2
    assert size % 2 == 0 and nz & (nz - 1) == 0 and nz > 2
    per = rotated_key_cache.shape[0]
    kv_heads = key_weight.shape[1] // HEAD_SIZE
    assert sum(CHUNK_HEADS) == kv_heads and per % SLOTS_AT_ONCE[1] == 0
    chunks = len(CHUNK_HEADS)
    gx = lax.axis_index("gx")
    gy = lax.axis_index("gy")
    place = jnp.stack([gx // 2, gx % 2, gy]).astype(jnp.int32)

    other = lax.ppermute(hidden_rows, "gy", [(0, 1), (1, 0)])
    sor = slot_of_row[None, :]
    gain = norm_gain.reshape(-1, HEAD_SIZE)

    lengths = lax.dynamic_slice_in_dim(slot_valid_lengths, gx * per, per, 0)
    lane = jnp.arange(HEAD_SIZE)
    half_width = HEAD_SIZE // 2
    frequency = ROPE_BASE ** (-((lane % half_width).astype(F32) * 2.0 / HEAD_SIZE))
    angles = lengths.astype(F32)[:, None] * frequency[None, :]
    cos = jnp.cos(angles)
    sin = jnp.sin(angles) * jnp.where(lane < half_width, -1.0, 1.0)[None, :]
    biases = [b.reshape(-1, HEAD_SIZE) for b in (query_bias, key_bias_vector, value_bias_vector)]

    def head_window(c, width):
        return pl.ds(sum(CHUNK_HEADS[:c]) * width, CHUNK_HEADS[c] * width)

    wide = QUERIES_PER_KV * HEAD_SIZE
    everything = pl.ds(0, w_query.shape[0])
    positions = rotated_key_cache.shape[1]
    all_columns = pl.ds(0, w_out.shape[1])
    same_z = neighbour_pairs(nz)
    scale = acc = None
    order = sor
    inputs = [hidden_rows, other, gain, sor]
    kept, swapped, reduced = {}, {}, {}
    loaded, gathered, waiting = {}, {}, {}

    def over_y(blocks, labels):
        return lax.ppermute(blocks, "gx", same_z), [(1 - h, q) for h, q in labels]

    def over_z(blocks, labels, stride):
        moved = lax.ppermute(blocks, "gx", stride_pairs(nz, stride))
        return moved, [(h, q ^ stride) for h, q in labels]

    def windows_of(kind, c):
        return [
            (array, (everything, head_window(c, n)))
            for array, n in ((w_query, wide), (key_weight, HEAD_SIZE), (value_weight, HEAD_SIZE))
        ]

    def file_loaded(wanted, arrays):
        arrays = list(arrays)
        for kind, c in wanted:
            loaded[kind, c] = [arrays.pop(0) for _ in windows_of(kind, c)]

    def loads_of(wanted):
        return [pair for kind, c in wanted for pair in windows_of(kind, c)]

    def do_load(token, wanted):
        name = "load" + "".join("_" + kind + str(c) for kind, c in wanted)
        token, arrays, _ = call(lambda: None, name, token, [], [], [], [], 1, loads_of(wanted))
        file_loaded(wanted, arrays)
        return token

    def do_project(token, c, wanted):
        nonlocal inputs
        token, arrays, outs = project(
            token, place, inputs, loaded["weights", c], loads_of(wanted),
            chunk=c, heads=CHUNK_HEADS[c], nz=nz, per=per,
        )
        file_loaded(wanted, arrays)
        kept[c] = outs[0]
        if c == 0:
            inputs = [outs[-1]]
        if Y_IN_HALVES[c]:
            far = lax.ppermute(outs[2], "gx", same_z)
            swapped[c] = (lax.ppermute(outs[1], "gx", same_z), 0), (far, 0)
        else:
            both = lax.ppermute(outs[1], "gx", same_z)
            swapped[c] = (both, 0), (both, nz // 2)
        return token

    def do_far(token, c, wanted):
        half = nz // 2
        token, (total,) = add(
            "add_far" + str(c), token, [kept[c], swapped[c][1][0]], [half, swapped[c][1][1]], half, 1
        )
        reduced[c] = lax.ppermute(total, "gx", stride_pairs(nz, 1))
        return token

    def do_near(token, c, wanted):
        terms, starts, count = [kept[c], swapped[c][0][0], reduced[c]], [0, 0, 0], nz // 2
        for stride in strides(nz)[1:]:
            token, (mine, sent) = add(
                "add_near" + str(c) + "_" + str(stride), token, terms, starts, count, 2
            )
            terms = [mine, lax.ppermute(sent, "gx", stride_pairs(nz, stride))]
            starts, count = [0, 0], count // 2
        reduced[c] = terms
        return token

    def do_attend(token, c, wanted):
        nonlocal scale
        token, arrays, outs = attend(
            token, place, slot_valid_lengths, reduced[c], scale, biases, cos, sin, rotated_key_cache, stored_value_cache,
            loads_of(wanted), chunk=c, heads=CHUNK_HEADS[c],
        )
        file_loaded(wanted, arrays)
        if c == 0:
            scale = outs[1]
        own = outs[0], [(0, 0)]
        first_move = over_y(*own) if GATHER[c] == "y first" else over_z(*own, strides(nz)[-1])
        waiting[c] = own, first_move
        return token

    def do_gather(token, c, wanted):
        held, moved = waiting[c]
        for stride in reversed(strides(nz) if GATHER[c] == "y first" else strides(nz)[:-1]):
            if GATHER[c] == "y first" and stride == 1:
                break
            token, joined = join("join" + str(c) + "_" + str(stride), token, held[0], moved[0])
            held = joined, held[1] + moved[1]
            moved = over_z(*held, stride)
        waiting[c] = held, moved
        gathered[c] = [held, moved]
        if GATHER[c] == "y halved":
            gathered[c].append(over_y(*held))
        return token

    def do_forward(token, c, wanted):
        held, moved = waiting[c]
        if GATHER[c] == "y halved":
            gathered[c].append(over_y(*moved))
            return token
        token, joined = join("join" + str(c), token, held[0], moved[0])
        held = joined, held[1] + moved[1]
        gathered[c] = [held, over_z(*held, 1) if GATHER[c] == "y first" else over_y(*held)]
        return token

    def do_output(token, c, wanted):
        nonlocal acc, order
        token, arrays, outs = output(
            token, place, [a for a, _ in gathered[c]], [own for _, own in gathered[c]], order,
            w_out, acc, loads_of(wanted),
            chunk=c, chunks=chunks, nz=nz, per=per,
        )
        file_loaded(wanted, arrays)
        if c == chunks - 1:
            send, stacked = outs
            token, mine = own_output(token, stacked, order, acc, hidden_rows, w_out, chunk=c)
            acc = mine, send
            return token
        acc = outs[0]
        if c == 0:
            order = outs[1]
        return token

    token = jnp.zeros(TOKEN, F32)
    steps = {
        "project": do_project,
        "far": do_far,
        "near": do_near,
        "attend": do_attend,
        "gather": do_gather,
        "forward": do_forward,
        "output": do_output,
    }
    needs = {"project": "weights", "attend": "caches", "output": "out"}
    wanted = []
    for step, c in ORDER:
        if step not in steps:
            wanted.append((step, c))
            continue
        if step not in needs or (needs[step], c) in wanted:
            if wanted:
                token = do_load(token, wanted)
            wanted = []
        token = steps[step](token, c, wanted)
        wanted = []
    mine, send = acc
    received = lax.ppermute(send, "gy", [(0, 1), (1, 0)])
    return (mine + received.astype(F32)).astype(BF16)


def solution(mesh):
    in_specs = (
        P(("grp", "gy"), "gx"),
        P("gx"),
        P("gx", "gy"),
        P("gx", "gy"),
        P("gx", "gy"),
        P("gy"),
        P("gy"),
        P("gy"),
        P(("grp", "gx"), None, "gy"),
        P(("grp", "gx"), None, "gy"),
        P("grp"),
        P("grp"),
        P("gy", "gx"),
    )
    out_specs = P(("grp", "gy"), "gx")
    return jax.shard_map(
        functools.partial(on_device, size=mesh.shape["gx"]),
        mesh=mesh,
        in_specs=in_specs,
        out_specs=out_specs,
        check_vma=False,
    )
```
